32 devices in a mesh: dp: 16 (over z, y, x), mp: 2 (over core).
Axes of the slice: x: 2, y: 2, z: 4, core: 2. Of those that a mesh axis runs over, the one named last changes fastest.
Arguments:
- tokens: bfloat16 [32768, 1024], P(('dp', 'mp')), may hold values from -6 to 6
- memory: bfloat16 [32768, 1024], P(('dp', 'mp')), may hold values from -6 to 6
- cotangent: bfloat16 [32768, 1024], P(('dp', 'mp')), may hold values from -6 to 6
- bucket: int32 [32], P('dp'), may hold values from 0 to 2, as said below
- target_lengths: int32 [32, 4], P('dp'), may hold values from 1 to 1024, as said below
- memory_lengths: int32 [32, 4], P('dp'), may hold values from 1 to 1024, as said below
- block_slot: int32 [128], replicated, may hold values from 0 to 127, each once
- col_weights: bfloat16 [10, 1024, 1024], P(None, None, 'mp')
- row_weights: bfloat16 [6, 1024, 1024], P(None, 'mp')
- shared_vectors: float32 [9, 1024], replicated
- split_vectors: float32 [8, 1024], P(None, 'mp'), may hold values from -0.6 to 0.6
- shared_first: float32 [9, 1024], replicated
- shared_second: float32 [9, 1024], replicated, as said below
- split_first: float32 [8, 1024], P(None, 'mp')
- split_second: float32 [8, 1024], P(None, 'mp'), as said below
- slot_first: float32 [128, 2, 256, 256], P('dp', 'mp')
- slot_second: float32 [128, 2, 256, 256], P('dp', 'mp'), as said below
- slot_master: float32 [128, 2, 256, 256], P('dp', 'mp'), may hold values from -0.1875 to 0.1875
- slot_left: float32 [128, 2, 256, 256], P('dp', 'mp'), as said below
- slot_right: float32 [128, 2, 256, 256], P('dp', 'mp'), as said below
- left_basis: float32 [128, 2, 256, 256], P('dp', 'mp'), may hold values from -1 to 1, as said below
- right_basis: float32 [128, 2, 256, 256], P('dp', 'mp'), may hold values from -1 to 1, as said below
Outputs:
- output: bfloat16 [32768, 1024], P(('dp', 'mp'))
- input_grad: float32 [32768, 1024], P(('dp', 'mp'))
- memory_grad: float32 [32768, 1024], P(('dp', 'mp'))
- first_moment: float32 [128, 2, 256, 256], P('dp', 'mp')
- second_moment: float32 [128, 2, 256, 256], P('dp', 'mp')
- master_weight: float32 [128, 2, 256, 256], P('dp', 'mp')
- master_copy: bfloat16 [128, 2, 256, 256], P('dp', 'mp')
- left_stat: float32 [128, 2, 256, 256], P('dp', 'mp')
- right_stat: float32 [128, 2, 256, 256], P('dp', 'mp')
- left_rotation: float32 [128, 2, 256, 256], P('dp', 'mp')
- right_rotation: float32 [128, 2, 256, 256], P('dp', 'mp')
- shared_mean: float32 [9, 1024], replicated
- shared_square: float32 [9, 1024], replicated
- shared_values: float32 [9, 1024], replicated
- split_mean: float32 [8, 1024], P(None, 'mp')
- split_square: float32 [8, 1024], P(None, 'mp')
- split_values: float32 [8, 1024], P(None, 'mp')
- grad_norm: float32 [], replicated
The draws below stay inside these ranges and needn't reach their ends.
Inputs may be any that keep to these rules, and one draw needn't show every extreme that they name: Row r holds 2**bucket[r] sequences in aligned segments of 1024 / 2**bucket[r] target and 1024 / 2**bucket[r] memory positions; the last row has bucket 0. target_lengths[r, s] is at least 1 and at most the segment's size; entries for s beyond the row's sequences are not used; the last row's first sequence has 1024 positions. memory_lengths[r, s] is at least 1 and at most the segment's size; the last row's first sequence has 1024 memory positions. `block_slot`: each slot holds exactly one block. `left_basis`: each block's basis is orthogonal. `right_basis`: each block's basis is orthogonal. `slot_left`: each block is symmetric positive definite. `slot_right`: each block is symmetric positive definite. `slot_second`: positive. `shared_second`: positive. `split_second`: positive.
All inputs are finite; a program needn't handle non-finite values.
Results may differ from the reference program's by a relative error of at most 0.04.
Values may be sent and summed in bfloat16 or wider, within the bound.
A program may use at most 384 MiB of HBM per device.

```python
import math
from functools import partial
import jax
import jax.numpy as jnp
from jax import lax

D = 1024
HEADS = 16
HEAD_DIM = 64
LEN = 1024
MEMLEN = 1024
BS = 256
STEP = 10
ROWS = 32
TOKENS = 32768
MEMTOK = 32768
NBLOCKS = 128


def grad_scale():
    return (16.0 * D * D) ** (-0.5)


def bell_noise(key, shape):
    return jax.random.normal(key, shape, jnp.float32)


def spread_lengths(key, bucket, extent, places):
    segment_size = extent // jnp.left_shift(1, bucket)
    target_size = jnp.maximum(segment_size * (ROWS + 2 * places) // (3 * ROWS), 1)
    jitter = jax.random.randint(key, (ROWS, 4), 0, 1 << 20) % (target_size[:, None] // 2 + 1)
    lengths = jnp.clip(target_size[:, None] - jitter, 1, segment_size[:, None])
    numbers = jnp.arange(4, dtype=jnp.int32)
    whole_row = (places[:, None] == ROWS - 1) & (numbers[None, :] == 0)
    return jnp.where(whole_row, extent, lengths).astype(jnp.int32)


def plan_rows(key):
    subkeys = jax.random.split(key, 3)
    places = jnp.arange(ROWS, dtype=jnp.int32)
    bucket = jax.random.randint(subkeys[0], (ROWS,), 0, 3)
    bucket = jnp.where(places == ROWS - 1, 0, bucket).astype(jnp.int32)
    return (bucket, spread_lengths(subkeys[1], bucket, LEN, places), spread_lengths(subkeys[2], bucket, MEMLEN, places))


def second_level(key, shape, magnitude):
    return 0.0101 * magnitude * magnitude * jnp.exp(jax.random.uniform(key, shape, jnp.float32, 0.0, math.log(4.0)))


def statistic(key):
    subkeys = jax.random.split(key, 2)
    level = 0.0526 * BS * grad_scale() ** 2
    diagonal = level * jnp.exp(jax.random.uniform(subkeys[0], (NBLOCKS, 2, BS), jnp.float32, 0.0, math.log(4.0)))
    raw = jax.random.uniform(subkeys[1], (NBLOCKS, 2, BS, BS), jnp.float32, -1.0, 1.0)
    symmetric = 0.25 * level / BS * (raw + jnp.swapaxes(raw, -1, -2))
    identity = jnp.eye(BS, dtype=bool)
    return jnp.where(identity, diagonal[..., None, :], symmetric)


def rotation(key):
    angle = jax.random.uniform(key, (NBLOCKS, 2, BS // 2), jnp.float32, -math.pi, math.pi)
    row_place = jnp.arange(BS)[:, None]
    col_place = jnp.arange(BS)[None, :]
    paired = row_place // 2 == col_place // 2
    angles = jnp.repeat(angle, 2, axis=-1)[..., :, None]
    cosine = jnp.cos(angles)
    sine = jnp.sin(angles)
    entry = jnp.where(row_place % 2 == col_place % 2, cosine, jnp.where(row_place % 2 == 0, -sine, sine))
    return jnp.where(paired, entry, 0.0)


def draw_bucket(key, part):
    plan = plan_rows(key)
    return plan[0]


def draw_target_lengths(key, part):
    plan = plan_rows(key)
    return plan[1]


def draw_memory_lengths(key, part):
    plan = plan_rows(key)
    return plan[2]


def draw_col_weights(key, part):
    key = jax.random.fold_in(key, 11)
    noise = bell_noise(key, (10, D, D))
    factor = jnp.array([2.0, 1.0, 1.0, 2.0, 1.0, 1.0, 1.0, 1.0, 1.0, 1.0], jnp.float32) * D ** (-0.5)
    return (noise * factor[:, None, None]).astype(jnp.bfloat16)


def draw_row_weights(key, part):
    key = jax.random.fold_in(key, 12)
    noise = bell_noise(key, (6, D, D))
    factor = jnp.array([4.0, 4.0, 0.5, 0.5, 0.5, 0.5], jnp.float32) * D ** (-0.5)
    return (noise * factor[:, None, None]).astype(jnp.bfloat16)


def draw_shared_vectors(key, part):
    key = jax.random.fold_in(key, 13)
    noise = bell_noise(key, (9, D))
    ramp = 0.6 + 0.8 * jnp.arange(D, dtype=jnp.float32) / D
    numbers = jnp.arange(9)[:, None]
    is_gain = (numbers < 6) & (numbers % 2 == 0)
    return jnp.where(is_gain, ramp * (1.0 + 0.1 * noise), 0.1 * noise)


def draw_shared_first(key, part):
    key = jax.random.fold_in(key, 21)
    noise = bell_noise(key, (9, D))
    return 0.33 * grad_scale() * noise


def draw_shared_second(key, part):
    key = jax.random.fold_in(key, 22)
    return second_level(key, (9, D), 3.0 * grad_scale())


def draw_split_first(key, part):
    key = jax.random.fold_in(key, 23)
    noise = bell_noise(key, (8, D))
    return 0.33 * grad_scale() * noise


def draw_split_second(key, part):
    key = jax.random.fold_in(key, 24)
    return second_level(key, (8, D), 3.0 * grad_scale())


def draw_slot_first(key, part):
    key = jax.random.fold_in(key, 25)
    noise = bell_noise(key, (NBLOCKS, 2, BS, BS))
    return 0.11 * grad_scale() * noise


def draw_slot_second(key, part):
    key = jax.random.fold_in(key, 26)
    return second_level(key, (NBLOCKS, 2, BS, BS), grad_scale())


def draw_slot_left(key, part):
    key = jax.random.fold_in(key, 31)
    return statistic(key)


def draw_slot_right(key, part):
    key = jax.random.fold_in(key, 32)
    return statistic(key)


def draw_left_basis(key, part):
    key = jax.random.fold_in(key, 41)
    return rotation(key)


def draw_right_basis(key, part):
    key = jax.random.fold_in(key, 42)
    return rotation(key)


def levels(own_key, shape, cuts, smallest, high):
    def one(axis_at, shards_of):
        heights = jax.random.uniform(jax.random.fold_in(jax.random.fold_in(own_key, 6), axis_at), (shards_of,), jnp.float32, smallest / len(cuts), high / len(cuts))
        return jnp.repeat(jnp.exp(heights), shape[axis_at] // shards_of).reshape((-1,) + (1,) * (len(shape) - axis_at - 1))

    level = one(*cuts[0])
    for cut in cuts[1:]:
        level = level * one(*cut)
    return level


def scatter_about(own_key, shape, deviation, most, cuts=(), kind=jnp.bfloat16):
    level = levels(own_key, shape, cuts, -0.22, 0.18) if cuts else 1.0
    values = jax.random.normal(own_key, shape, jnp.float32) * deviation * level
    return jnp.minimum(jnp.maximum(values, -most), most).astype(kind)


def setup_inputs(seed: int = 0) -> dict:
    key_list = jax.random.split(jax.random.key(seed), 23)
    tokens = scatter_about(key_list[0], (TOKENS, D), 1.0, 6.0, ((0, 32),))
    memory = scatter_about(key_list[1], (MEMTOK, D), 1.0, 6.0, ((0, 32),))
    cotangent = scatter_about(key_list[2], (TOKENS, D), 1.0, 6.0, ((0, 32),))
    bucket = draw_bucket(jax.random.fold_in(key_list[22], 71), 0)
    target_lengths = draw_target_lengths(jax.random.fold_in(key_list[22], 71), 0)
    memory_lengths = draw_memory_lengths(jax.random.fold_in(key_list[22], 71), 0)
    block_slot = jax.random.permutation(key_list[6], NBLOCKS).astype(jnp.int32)
    col_weights = draw_col_weights(jax.random.fold_in(key_list[22], 71), 0)
    row_weights = draw_row_weights(jax.random.fold_in(key_list[22], 71), 0)
    shared_vectors = draw_shared_vectors(jax.random.fold_in(key_list[22], 71), 0)
    split_vectors = scatter_about(key_list[10], (8, D), 0.1, 0.6, ((1, 2),), jnp.float32)
    shared_first = draw_shared_first(jax.random.fold_in(key_list[22], 71), 0)
    shared_second = draw_shared_second(jax.random.fold_in(key_list[22], 71), 0)
    split_first = draw_split_first(jax.random.fold_in(key_list[22], 71), 0)
    split_second = draw_split_second(jax.random.fold_in(key_list[22], 71), 0)
    slot_first = draw_slot_first(jax.random.fold_in(key_list[22], 71), 0)
    slot_second = draw_slot_second(jax.random.fold_in(key_list[22], 71), 0)
    slot_master = scatter_about(key_list[17], (NBLOCKS, 2, BS, BS), D ** -0.5, 0.1875, ((0, 16), (1, 2)), jnp.float32)
    slot_left = draw_slot_left(jax.random.fold_in(key_list[22], 71), 0)
    slot_right = draw_slot_right(jax.random.fold_in(key_list[22], 71), 0)
    left_basis = draw_left_basis(jax.random.fold_in(key_list[22], 71), 0)
    right_basis = draw_right_basis(jax.random.fold_in(key_list[22], 71), 0)
    return {"tokens": tokens, "memory": memory, "cotangent": cotangent, "bucket": bucket, "target_lengths": target_lengths, "memory_lengths": memory_lengths, "block_slot": block_slot, "col_weights": col_weights, "row_weights": row_weights, "shared_vectors": shared_vectors, "split_vectors": split_vectors, "shared_first": shared_first, "shared_second": shared_second, "split_first": split_first, "split_second": split_second, "slot_first": slot_first, "slot_second": slot_second, "slot_master": slot_master, "slot_left": slot_left, "slot_right": slot_right, "left_basis": left_basis, "right_basis": right_basis}


highest = lax.Precision.HIGHEST
clip_limit = 1.0
weight_rate = 0.03
shared_rate = 0.6
split_rate = 0.2
weight_decay = 0.01

@jax.custom_vjp
def low(v):
    return lax.optimization_barrier(v.astype(jnp.bfloat16)).astype(jnp.float32)

@jax.custom_vjp
def low_back(v):
    return v

def low_keep(v):
    return (low(v), None)

def low_pass(kept, grad):
    return (grad,)

def back_keep(v):
    return (v, None)

def back_low(kept, grad):
    return (low(grad),)
low.defvjp(low_keep, low_pass)
low_back.defvjp(back_keep, back_low)

def rounded_both(values):
    return low_back(low(values))

def layer_norm(values, scale_row, shift_row):
    middle = lax.optimization_barrier(jnp.mean(values, axis=-1, keepdims=True))
    centered = values - middle
    spread = lax.optimization_barrier(jnp.mean(centered * centered, axis=-1, keepdims=True))
    return centered * lax.rsqrt(spread + 1e-05) * scale_row + shift_row

def exact_gelu(values):
    return jax.nn.gelu(values, approximate=False)

def layout(bucket_row, length_row, extent):
    segment_size = extent // jnp.left_shift(jnp.int32(1), bucket_row)
    places = jnp.arange(extent, dtype=jnp.int32)
    segment = places // segment_size
    offset = places - segment * segment_size
    numbers = jnp.arange(4, dtype=jnp.int32)
    live = jnp.any((segment[:, None] == numbers[None, :]) & (offset[:, None] < length_row[None, :]), axis=1)
    return (segment, live)

def causal_mask(segment):
    places = jnp.arange(segment.shape[0], dtype=jnp.int32)
    return (segment[:, None] == segment[None, :]) & (places[None, :] <= places[:, None])

def cross_mask(segment, memory_segment, memory_live):
    return (segment[:, None] == memory_segment[None, :]) & memory_live[None, :]

def project(values, weight):
    return jnp.dot(values, weight, precision=highest)

def split_heads(values, extent):
    return values.reshape(-1, extent, HEADS, HEAD_DIM)

def attention(queries, key_rows, value_rows, allowed, score_scale):
    scores = low_back(jnp.einsum('qhd,khd->hqk', queries, key_rows, precision=highest) * score_scale)
    scores = jnp.where(allowed[None], scores, -1e+30)
    largest = lax.optimization_barrier(jnp.max(scores, axis=-1, keepdims=True))
    weights = jnp.exp(scores - largest)
    shares = weights / lax.optimization_barrier(jnp.sum(weights, axis=-1, keepdims=True))
    return jnp.einsum('hqk,khd->qhd', low(shares), value_rows, precision=highest)

def forward(tokens_wide, memory_wide, col_wide, row_wide, shared_wide, split_wide, bucket, target_lengths, memory_lengths):
    all_tokens = tokens_wide.shape[0]
    score_scale = HEAD_DIM ** (-0.5)
    normed_first = low(layer_norm(tokens_wide, shared_wide[0], shared_wide[1]))
    queries = rounded_both(project(normed_first, col_wide[0]) + split_wide[0])
    self_keys = rounded_both(project(normed_first, col_wide[1]))
    self_values = rounded_both(project(normed_first, col_wide[2]) + split_wide[1])

    def self_row(inputs):
        query_row, key_row, value_row, bucket_row, length_row = inputs
        segment, live = layout(bucket_row, length_row, LEN)
        return attention(query_row, key_row, value_row, causal_mask(segment), score_scale)
    self_out = lax.map(jax.checkpoint(self_row), (split_heads(queries, LEN), split_heads(self_keys, LEN), split_heads(self_values, LEN), bucket, target_lengths))
    self_out = rounded_both(self_out.reshape(all_tokens, D))
    residual_first = tokens_wide + low_back(project(self_out, row_wide[0])) + shared_wide[6]
    normed_second = low(layer_norm(residual_first, shared_wide[2], shared_wide[3]))
    cross_queries = rounded_both(project(normed_second, col_wide[3]) + split_wide[2])
    memory_keys = rounded_both(project(memory_wide, col_wide[4]))
    memory_values = rounded_both(project(memory_wide, col_wide[5]) + split_wide[3])

    def cross_row(inputs):
        query_row, key_row, value_row, bucket_row, length_row, memory_row = inputs
        segment, live = layout(bucket_row, length_row, LEN)
        memory_segment, memory_live = layout(bucket_row, memory_row, MEMLEN)
        return attention(query_row, key_row, value_row, cross_mask(segment, memory_segment, memory_live), score_scale)
    cross_out = lax.map(jax.checkpoint(cross_row), (split_heads(cross_queries, LEN), split_heads(memory_keys, MEMLEN), split_heads(memory_values, MEMLEN), bucket, target_lengths, memory_lengths))
    cross_out = rounded_both(cross_out.reshape(all_tokens, D))
    residual_second = residual_first + low_back(project(cross_out, row_wide[1])) + shared_wide[7]
    normed_third = low(layer_norm(residual_second, shared_wide[4], shared_wide[5]))
    pre_act = low_back(jnp.einsum('td,sde->tse', normed_third, col_wide[6:10], precision=highest) + split_wide[4:8])
    hidden = rounded_both(exact_gelu(pre_act))
    down = low_back(jnp.einsum('tse,sed->td', hidden, row_wide[2:6], precision=highest))
    return residual_second + down + shared_wide[8]

def to_blocks(col_part, row_part):
    stacked, height, breadth = col_part.shape
    tiles_cols = col_part.reshape(stacked, height // BS, BS, breadth // BS, BS).transpose(0, 1, 3, 2, 4).reshape(-1, BS, BS)
    stacked, height, breadth = row_part.shape
    tiles_rows = row_part.reshape(stacked, height // BS, BS, breadth // BS, BS).transpose(0, 1, 3, 2, 4).reshape(-1, BS, BS)
    return jnp.concatenate([tiles_cols, tiles_rows], axis=0)

def slot_order(block_slot):
    numbers = jnp.arange(block_slot.shape[0], dtype=jnp.int32)
    return lax.optimization_barrier(jnp.sum(jnp.where(block_slot[None, :] == numbers[:, None], numbers[None, :], 0), axis=1)).astype(jnp.int32)

def chol_orthonormal(matrix):
    gram_matrix = jnp.einsum('...ki,...kj->...ij', matrix, matrix, precision=highest)
    factor = jnp.linalg.cholesky(gram_matrix)
    solved = jax.scipy.linalg.solve_triangular(factor, jnp.swapaxes(matrix, -1, -2), lower=True)
    return jnp.swapaxes(solved, -1, -2)

def soap_step(gradient, first_state, second_state, master, left_state, right_state, left_basis, right_basis):
    left_new = 0.95 * left_state + 0.05 * jnp.einsum('...ik,...jk->...ij', gradient, gradient, precision=highest)
    right_new = 0.95 * right_state + 0.05 * jnp.einsum('...ki,...kj->...ij', gradient, gradient, precision=highest)
    partial_rot = jnp.einsum('...ki,...kj->...ij', left_basis, gradient, precision=highest)
    rotated = jnp.einsum('...ik,...kj->...ij', partial_rot, right_basis, precision=highest)
    first_new = 0.9 * first_state + 0.1 * rotated
    second_new = 0.99 * second_state + 0.01 * rotated * rotated
    ratio = first_new / (1.0 - 0.9 ** STEP) / (jnp.sqrt(second_new / (1.0 - 0.99 ** STEP)) + 1e-08)
    turned = jnp.einsum('...ik,...kj->...ij', left_basis, ratio, precision=highest)
    stepped = jnp.einsum('...ik,...jk->...ij', turned, right_basis, precision=highest)
    master_new = master - weight_rate * (stepped + weight_decay * master)
    left_rot = chol_orthonormal(jnp.einsum('...ik,...kj->...ij', left_new, left_basis, precision=highest))
    right_rot = chol_orthonormal(jnp.einsum('...ik,...kj->...ij', right_new, right_basis, precision=highest))
    return (first_new, second_new, master_new, left_new, right_new, left_rot, right_rot)

def adam_step(gradient, first_state, second_state, values, step_rate):
    first_new = 0.9 * first_state + 0.1 * gradient
    second_new = 0.99 * second_state + 0.01 * gradient * gradient
    ratio = first_new / (1.0 - 0.9 ** STEP) / (jnp.sqrt(second_new / (1.0 - 0.99 ** STEP)) + 1e-08)
    return (first_new, second_new, values - step_rate * ratio)

def reference(tokens, memory, cotangent, bucket, target_lengths, memory_lengths, block_slot, col_weights, row_weights, shared_vectors, split_vectors, shared_first, shared_second, split_first, split_second, slot_first, slot_second, slot_master, slot_left, slot_right, left_basis, right_basis):

    def run(tokens_wide, memory_wide, col_wide, row_wide, shared_wide, split_wide):
        return forward(tokens_wide, memory_wide, col_wide, row_wide, shared_wide, split_wide, bucket, target_lengths, memory_lengths)
    result, pullback = jax.vjp(run, tokens.astype(jnp.float32), memory.astype(jnp.float32), col_weights.astype(jnp.float32), row_weights.astype(jnp.float32), shared_vectors, split_vectors)
    segments, live = jax.vmap(partial(layout, extent=LEN))(bucket, target_lengths)
    weighting = cotangent.astype(jnp.float32) * live.reshape(-1, 1).astype(jnp.float32)
    input_grad, memory_grad, grad_cols, grad_rows, shared_grad, split_grad = pullback(weighting)
    width = D // 2
    halves = [to_blocks(grad_cols[:, :, section * width:(section + 1) * width], grad_rows[:, section * width:(section + 1) * width, :]) for section in range(2)]
    blocks = jnp.stack(halves, axis=1)
    slot_grad = jnp.take(blocks, slot_order(block_slot), axis=0)
    grad_norm = jnp.sqrt(jnp.sum(slot_grad * slot_grad) + jnp.sum(shared_grad * shared_grad) + jnp.sum(split_grad * split_grad))
    clip = clip_limit / jnp.maximum(grad_norm, clip_limit)
    first_moment, second_moment, master_weight, left_stat, right_stat, left_rotation, right_rotation = soap_step(slot_grad * clip, slot_first, slot_second, slot_master, slot_left, slot_right, left_basis, right_basis)
    shared_mean, shared_square, shared_values = adam_step(shared_grad * clip, shared_first, shared_second, shared_vectors, shared_rate)
    split_mean, split_square, split_values = adam_step(split_grad * clip, split_first, split_second, split_vectors, split_rate)
    return (result.astype(jnp.bfloat16), input_grad, memory_grad, first_moment, second_moment, master_weight, master_weight.astype(jnp.bfloat16), left_stat, right_stat, left_rotation, right_rotation, shared_mean, shared_square, shared_values, split_mean, split_square, split_values, grad_norm)
```

```python
from functools import partial

import jax
import jax.numpy as jnp
from jax import lax
from jax.experimental import pallas as pl
from jax.experimental.pallas import tpu as pltpu
from jax.sharding import PartitionSpec as P

HEAD_DIM=64; TQ=256
SCALE=HEAD_DIM**-0.5
EXPC=SCALE*1.4426950408889634
NEG=-1e30
NT=(((1,),(1,)),((),()))
NN=(((1,),(0,)),((),()))

def tail_mask(causal, limit):
    r=lax.broadcasted_iota(jnp.int32,(TQ,TQ),0)
    if causal:
        return r<=lax.broadcasted_iota(jnp.int32,(TQ,TQ),1)
    return r<limit

def fwd_kernel(causal, tiles, plan, q_ref, k_ref, v_ref, o_ref, l_ref, vt_ref):
    i=pl.program_id(1)
    start=plan[0,i]; count=plan[1,i]; limit=plan[2,i]
    @pl.when(i==0)
    def _():
        vt_ref[...]=v_ref[...].astype(jnp.float32).T.astype(jnp.bfloat16)
    for n in range(1,tiles+1):
        @pl.when(count==n)
        def _(n=n):
            outs=[]; logs=[]
            for h in range(2):
                cols=slice(h*HEAD_DIM,(h+1)*HEAD_DIM)
                q=q_ref[:,cols]
                parts=[]
                for j in range(n):
                    k=k_ref[pl.ds(pl.multiple_of((start+j)*TQ,TQ),TQ),cols]
                    s=lax.dot_general(k,q,NT,preferred_element_type=jnp.float32)
                    if j==n-1:
                        s=jnp.where(tail_mask(causal,limit),s,NEG)
                    parts.append(s)
                top=parts[0].max(axis=0,keepdims=True)
                for s in parts[1:]: top=jnp.maximum(top,s.max(axis=0,keepdims=True))
                total=None; acc=None
                for j,s in enumerate(parts):
                    p=jnp.exp2((s-top)*EXPC)
                    t=p.sum(axis=0,keepdims=True)
                    total=t if total is None else total+t
                    vt=vt_ref[cols,pl.ds(pl.multiple_of((start+j)*TQ,TQ),TQ)]
                    a=lax.dot_general(vt,p.astype(jnp.bfloat16),NN,preferred_element_type=jnp.float32)
                    acc=a if acc is None else acc+a
                outs.append(acc*(1.0/total))
                logs.append(top+jnp.log2(total)*(1.0/EXPC))
            o_ref[...]=jnp.concatenate(outs,axis=0).T.astype(o_ref.dtype)
            l_ref[0]=jnp.concatenate(logs,axis=0)

def attention(q,k,v,plan,causal):
    T,W=q.shape; M=k.shape[0]; pairs=W//128; tiles=M//TQ
    return pl.pallas_call(
        partial(fwd_kernel,causal,tiles),
        out_shape=(jax.ShapeDtypeStruct((T,W),jnp.bfloat16),jax.ShapeDtypeStruct((pairs,2,T),jnp.float32)),
        grid_spec=pltpu.PrefetchScalarGridSpec(num_scalar_prefetch=1,grid=(pairs,T//TQ),
            in_specs=[pl.BlockSpec((TQ,128),lambda h,i,_:(i,h)),
                      pl.BlockSpec((M,128),lambda h,i,_:(0,h)),
                      pl.BlockSpec((M,128),lambda h,i,_:(0,h))],
            out_specs=[pl.BlockSpec((TQ,128),lambda h,i,_:(i,h)),
                       pl.BlockSpec((1,2,TQ),lambda h,i,_:(h,0,i))],
            scratch_shapes=[pltpu.VMEM((128,M),jnp.bfloat16)]),
        compiler_params=pltpu.CompilerParams(vmem_limit_bytes=48*1024*1024),
        cost_estimate=pl.CostEstimate(flops=4*T*M*W//2,bytes_accessed=8*T*W,transcendentals=T*M*W//128),
    )(plan,q,k,v)

def bwd_kernel(causal, tiles, plan, q_ref, k_ref, v_ref, g_ref, l_ref, dq_ref, dk_ref, dv_ref, kt_ref, dk_acc, dv_acc):
    i=pl.program_id(1)
    start=plan[0,i]; count=plan[1,i]; limit=plan[2,i]
    @pl.when(i==0)
    def _():
        kt_ref[...]=k_ref[...].astype(jnp.float32).T.astype(jnp.bfloat16)
        dk_acc[...]=jnp.zeros_like(dk_acc)
        dv_acc[...]=jnp.zeros_like(dv_acc)
    for n in range(1,tiles+1):
        @pl.when(count==n)
        def _(n=n):
            outs=[]
            for h in range(2):
                cols=slice(h*HEAD_DIM,(h+1)*HEAD_DIM)
                q=q_ref[:,cols]; g=g_ref[:,cols]
                log=l_ref[0,h:h+1,:]
                ps=[]; ts=[]; delta=None
                for j in range(n):
                    rows=pl.ds(pl.multiple_of((start+j)*TQ,TQ),TQ)
                    s=lax.dot_general(k_ref[rows,cols],q,NT,preferred_element_type=jnp.float32)
                    p=jnp.exp2((s-log)*EXPC)
                    if j==n-1:
                        p=jnp.where(tail_mask(causal,limit),p,0.0)
                    dp=lax.dot_general(v_ref[rows,cols],g,NT,preferred_element_type=jnp.float32)
                    t=p*dp
                    d=t.sum(axis=0,keepdims=True)
                    delta=d if delta is None else delta+d
                    ps.append(p); ts.append(t)
                    dv_acc[rows,cols]+=lax.dot_general(p.astype(jnp.bfloat16),g,NN,preferred_element_type=jnp.float32)
                acc=None
                for j in range(n):
                    rows=pl.ds(pl.multiple_of((start+j)*TQ,TQ),TQ)
                    ds=(ts[j]-ps[j]*delta).astype(jnp.bfloat16)
                    dk_acc[rows,cols]+=lax.dot_general(ds,q,NN,preferred_element_type=jnp.float32)
                    a=lax.dot_general(kt_ref[cols,rows],ds,NN,preferred_element_type=jnp.float32)
                    acc=a if acc is None else acc+a
                outs.append(acc*SCALE)
            dq_ref[...]=jnp.concatenate(outs,axis=0).T.astype(dq_ref.dtype)
    @pl.when(i==pl.num_programs(1)-1)
    def _():
        dk_ref[...]=(dk_acc[...]*SCALE).astype(dk_ref.dtype)
        dv_ref[...]=dv_acc[...].astype(dv_ref.dtype)

def attention_back(q,k,v,g,logs,plan,causal):
    T,W=q.shape; M=k.shape[0]; pairs=W//128; tiles=M//TQ
    return pl.pallas_call(
        partial(bwd_kernel,causal,tiles),
        out_shape=(jax.ShapeDtypeStruct((T,W),jnp.bfloat16),jax.ShapeDtypeStruct((M,W),jnp.bfloat16),jax.ShapeDtypeStruct((M,W),jnp.bfloat16)),
        grid_spec=pltpu.PrefetchScalarGridSpec(num_scalar_prefetch=1,grid=(pairs,T//TQ),
            in_specs=[pl.BlockSpec((TQ,128),lambda h,i,_:(i,h)),
                      pl.BlockSpec((M,128),lambda h,i,_:(0,h)),
                      pl.BlockSpec((M,128),lambda h,i,_:(0,h)),
                      pl.BlockSpec((TQ,128),lambda h,i,_:(i,h)),
                      pl.BlockSpec((1,2,TQ),lambda h,i,_:(h,0,i))],
            out_specs=[pl.BlockSpec((TQ,128),lambda h,i,_:(i,h)),
                       pl.BlockSpec((M,128),lambda h,i,_:(0,h)),
                       pl.BlockSpec((M,128),lambda h,i,_:(0,h))],
            scratch_shapes=[pltpu.VMEM((128,M),jnp.bfloat16),pltpu.VMEM((M,128),jnp.float32),pltpu.VMEM((M,128),jnp.float32)]),
        compiler_params=pltpu.CompilerParams(vmem_limit_bytes=48*1024*1024),
        cost_estimate=pl.CostEstimate(flops=10*T*M*W//2,bytes_accessed=14*T*W,transcendentals=T*M*W//128),
    )(plan,q,k,v,g,logs)

def self_plan(bucket,T):
    i=jnp.arange(T//TQ,dtype=jnp.int32)
    seg=(T//TQ)//jnp.left_shift(jnp.int32(1),bucket)
    start=i//seg*seg
    return jnp.stack([start,i-start+1,jnp.full_like(i,TQ)])

def cross_plan(bucket,lengths,T,M):
    i=jnp.arange(T//TQ,dtype=jnp.int32)
    qseg=(T//TQ)//jnp.left_shift(jnp.int32(1),bucket)
    mseg=(M//TQ)//jnp.left_shift(jnp.int32(1),bucket)
    seq=i//qseg
    length=jnp.sum(jnp.where(seq[:,None]==jnp.arange(lengths.shape[0],dtype=jnp.int32)[None,:],lengths[None,:],0),axis=1)
    count=(length+TQ-1)//TQ
    return jnp.stack([seq*mseg,count,length-(count-1)*TQ])

BS=256; STEP=10
weight_rate=0.03; weight_decay=0.01
HI=lax.Precision.HIGHEST
def hdot(a,b,dims,precision=HI):
    return lax.dot_general(a,b,(dims,((),())),precision=precision,preferred_element_type=jnp.float32)
DIM_NN=((1,),(0,)); DIM_NT=((1,),(1,)); DIM_TN=((0,),(0,))

def soap_kernel(clip_ref,g_ref,first,second,master,left,right,ql_ref,qr_ref,
                first_o,second_o,master_o,copy_o,left_o,right_o,al_o,ar_o,ml_o,mr_o):
    clip=clip_ref[0,0]
    g=g_ref[0]*clip
    ql=ql_ref[0]; qr=qr_ref[0]
    left_new=0.95*left[0]+0.05*hdot(g,g,DIM_NT)
    left_o[0]=left_new
    al=hdot(left_new,ql,DIM_NN); al_o[0]=al
    ml_o[0]=hdot(al,al,DIM_TN)
    right_new=0.95*right[0]+0.05*hdot(g,g,DIM_TN)
    right_o[0]=right_new
    ar=hdot(right_new,qr,DIM_NN); ar_o[0]=ar
    mr_o[0]=hdot(ar,ar,DIM_TN)
    rot=hdot(hdot(ql,g,DIM_TN),qr,DIM_NN)
    f=0.9*first[0]+0.1*rot; first_o[0]=f
    s=0.99*second[0]+0.01*rot*rot; second_o[0]=s
    ratio=f/(1.0-0.9**STEP)/(jnp.sqrt(s/(1.0-0.99**STEP))+1e-8)
    stepped=hdot(hdot(ql,ratio,DIM_NN),qr,DIM_NT)
    m=master[0]-weight_rate*(stepped+weight_decay*master[0])
    master_o[0]=m; copy_o[0]=m.astype(jnp.bfloat16)

def soap_stage(clip,g,first,second,master,left,right,ql,qr):
    n=g.shape[0]
    spec=pl.BlockSpec((1,BS,BS),lambda i:(i,0,0))
    f32=jax.ShapeDtypeStruct((n,BS,BS),jnp.float32)
    return pl.pallas_call(soap_kernel,grid=(n,),
        out_shape=(f32,f32,f32,jax.ShapeDtypeStruct((n,BS,BS),jnp.bfloat16),f32,f32,f32,f32,f32,f32),
        in_specs=[pl.BlockSpec(memory_space=pltpu.SMEM)]+[spec]*8,
        out_specs=[spec]*10,
        compiler_params=pltpu.CompilerParams(vmem_limit_bytes=48*1024*1024),
    )(clip.reshape(1,1),g,first,second,master,left,right,ql,qr)

PW=64
def chol_kernel(al_ref,ar_ref,ml_ref,mr_ref,ql_o,qr_o,work,tile,lane_sel):
    n=al_ref.shape[0]
    row=lax.broadcasted_iota(jnp.int32,(BS,BS),0); col=lax.broadcasted_iota(jnp.int32,(BS,BS),1)
    eye=(row==col).astype(jnp.float32)
    def load(m,_):
        work[m,:,0:BS]=ml_ref[m]; work[n+m,:,0:BS]=mr_ref[m]
        work[m,:,BS:]=eye; work[n+m,:,BS:]=eye
        return 0
    lax.fori_loop(0,n,load,0)
    prow=lax.broadcasted_iota(jnp.int32,(PW,2*PW),0); pcol=lax.broadcasted_iota(jnp.int32,(PW,2*PW),1)
    ident=(pcol==prow+PW).astype(jnp.float32)
    for p in range(BS//PW):
        lo=p*PW
        def fill(m,_):
            d=work[m,lo:lo+PW,(lo//128)*128:(lo//128)*128+128]
            if lo%128: d=pltpu.roll(d,64,1)
            tile[m]=jnp.where(pcol<PW,d,ident)
            return 0
        lax.fori_loop(0,2*n,fill,0)
        def step(k,_):
            t=tile[...]
            idx=jnp.full((2*n*PW,2*PW),k,jnp.int32)
            c=jnp.take_along_axis(t.reshape(2*n*PW,2*PW),idx,axis=1).reshape(2*n,PW,2*PW)
            r=tile[:,pl.ds(k,1),:]
            d=jnp.take_along_axis(r.reshape(2*n,2*PW),jnp.full((2*n,2*PW),k,jnp.int32),axis=1).reshape(2*n,1,2*PW)
            r=r*(1.0/d)
            below=lax.broadcasted_iota(jnp.int32,(2*n,PW,2*PW),1)>k
            tile[...]=t-jnp.where(below,c,0.0)*r
            return 0
        lax.fori_loop(0,PW,step,0)
        def apply(m,_):
            t=tile[m]
            d=jnp.sum(jnp.where(pcol==prow,t,0.0),axis=1,keepdims=True)
            ci=(t*lax.rsqrt(d))[:,PW:]
            r=hdot(ci,work[m,lo:lo+PW,:],DIM_NN)
            work[m,lo:lo+PW,BS:]=r[:,BS:]
            if p<BS//PW-1:
                work[m,lo+PW:,:]-=hdot(r[:,lo+PW:BS],r,DIM_TN)
            return 0
        lax.fori_loop(0,2*n,apply,0)
    def final(m,_):
        ql_o[m]=hdot(al_ref[m],work[m,:,BS:],DIM_NT)
        qr_o[m]=hdot(ar_ref[m],work[n+m,:,BS:],DIM_NT)
        return 0
    lax.fori_loop(0,n,final,0)

def chol_stage(al,ar,ml,mr):
    n=al.shape[0]
    f32=jax.ShapeDtypeStruct((n,BS,BS),jnp.float32)
    vm=pl.BlockSpec(memory_space=pltpu.VMEM)
    return pl.pallas_call(chol_kernel,out_shape=(f32,f32),in_specs=[vm]*4,out_specs=[vm]*2,
        scratch_shapes=[pltpu.VMEM((2*n,BS,2*BS),jnp.float32),pltpu.VMEM((2*n,PW,2*PW),jnp.float32),pltpu.SMEM((1,),jnp.int32)],
        compiler_params=pltpu.CompilerParams(vmem_limit_bytes=56*1024*1024))(al,ar,ml,mr)

def soap(clip,g,first,second,master,left,right,ql,qr):
    f,s,m,c,l,r,al,ar,ml,mr=soap_stage(clip,g,first,second,master,left,right,ql,qr)
    lr,rr=chol_stage(al,ar,ml,mr)
    return f,s,m,c,l,r,lr,rr


LEN = 1024
shared_rate = 0.6
split_rate = 0.2
clip_limit = 1.0
SWAP = [(0, 1), (1, 0)]


def adam_step(gradient, first_state, second_state, values, step_rate):
    first_new = 0.9 * first_state + 0.1 * gradient
    second_new = 0.99 * second_state + 0.01 * gradient * gradient
    ratio = first_new / (1.0 - 0.9**STEP) / (jnp.sqrt(second_new / (1.0 - 0.99**STEP)) + 1e-08)
    return (first_new, second_new, values - step_rate * ratio)


def norm_forward(values, gain, shift):
    centered = values - jnp.mean(values, axis=-1, keepdims=True)
    inverse = lax.rsqrt(jnp.mean(centered * centered, axis=-1, keepdims=True) + 1e-05)
    hat = centered * inverse
    return (hat * gain + shift).astype(jnp.bfloat16), (values, inverse)


def norm_back(saved, gain, grad):
    values, inverse = saved
    hat = (values - jnp.mean(values, axis=-1, keepdims=True)) * inverse
    inner = grad * gain
    back = inverse * (
        inner
        - jnp.mean(inner, axis=-1, keepdims=True)
        - hat * jnp.mean(inner * hat, axis=-1, keepdims=True)
    )
    return back, jnp.sum(grad * hat, axis=0), jnp.sum(grad, axis=0)


def dot32(a, b):
    return jnp.dot(a, b, preferred_element_type=jnp.float32)


def low(a):
    return a.astype(jnp.bfloat16)


def wide(a):
    return a.astype(jnp.float32)


def up_kernel(x_ref, w_ref, b_ref, h_ref, d_ref):
    rows = 256
    for r in range(x_ref.shape[0] // rows):
        at = slice(r * rows, (r + 1) * rows)
        v = jnp.dot(x_ref[at, :], w_ref[0], preferred_element_type=jnp.float32) + b_ref[0]
        z = jnp.abs(v)
        t = 1.0 / (1.0 + (0.3275911 * 0.7071067811865476) * z)
        e = jnp.exp2(v * v * (-0.5 * 1.4426950408889634))
        poly = t * (
            0.5 * 0.254829592
            + t * (0.5 * -0.284496736 + t * (0.5 * 1.421413741 + t * (0.5 * -1.453152027 + t * (0.5 * 1.061405429))))
        )
        tail = poly * e
        phi = jnp.where(v >= 0.0, 1.0 - tail, tail)
        h_ref[0, at, :] = (v * phi).astype(h_ref.dtype)
        d_ref[0, at, :] = (phi + v * e * 0.3989422804014327).astype(d_ref.dtype)


def up_project(x, col, bias):
    rows, depth = x.shape
    width = col.shape[2]
    shape = jax.ShapeDtypeStruct((4, rows, width), jnp.bfloat16)
    return pl.pallas_call(
        up_kernel,
        grid=(4,),
        out_shape=(shape, shape),
        in_specs=[
            pl.BlockSpec((rows, depth), lambda s: (0, 0)),
            pl.BlockSpec((1, depth, width), lambda s: (s + 6, 0, 0)),
            pl.BlockSpec((1, 1, width), lambda s: (s, 0, 0)),
        ],
        out_specs=[pl.BlockSpec((1, rows, width), lambda s: (s, 0, 0))] * 2,
        compiler_params=pltpu.CompilerParams(vmem_limit_bytes=48 * 1024 * 1024),
        cost_estimate=pl.CostEstimate(
            flops=8 * rows * depth * width, bytes_accessed=24 * rows * width, transcendentals=8 * rows * width
        ),
    )(x, col, bias[4:8, None, :])


def exchange(array):
    return lax.ppermute(array, "mp", SWAP)


def to_parts(array, parts):
    stacked, height, width = array.shape
    return array.reshape(stacked * height // BS, parts, BS // parts, width)


def scatter_sum(array, first_bits):
    parts = array.shape[1]
    bits = parts.bit_length() - 1
    index = lax.axis_index("dp")
    array = array.reshape((array.shape[0],) + (2,) * bits + array.shape[2:])
    left = list(range(bits - 1, -1, -1))
    order = [b for b in first_bits if b < bits] + [b for b in range(bits) if b not in first_bits]
    for b in order:
        axis = 1 + left.index(b)
        left.remove(b)
        mine = (index >> b) & 1
        keep = lax.dynamic_index_in_dim(array, mine, axis, keepdims=False)
        send = lax.dynamic_index_in_dim(array, 1 - mine, axis, keepdims=False)
        got = lax.ppermute(send, "dp", [(i, i ^ (1 << b)) for i in range(parts)])
        array = low(wide(keep) + wide(got))
    return array


def all_sum(array, parts):
    array = array + lax.ppermute(array, "mp", SWAP)
    for b in range(parts.bit_length() - 1):
        array = array + lax.ppermute(array, "dp", [(i, i ^ (1 << b)) for i in range(parts)])
    return array


def slot_order(block_slot):
    numbers = jnp.arange(block_slot.shape[0], dtype=jnp.int32)
    return jnp.sum(jnp.where(block_slot[None, :] == numbers[:, None], numbers[None, :], 0), axis=1)


def on_device(
    parts,
    tokens,
    memory,
    cotangent,
    bucket,
    target_lengths,
    memory_lengths,
    block_slot,
    col_weights,
    row_weights,
    shared_vectors,
    split_vectors,
    shared_first,
    shared_second,
    split_first,
    split_second,
    slot_first,
    slot_second,
    slot_master,
    slot_left,
    slot_right,
    left_basis,
    right_basis,
):
    core = lax.axis_index("mp")
    half = col_weights.shape[2]
    shared = shared_vectors
    own_bucket = lax.dynamic_index_in_dim(bucket, core, 0, keepdims=False)
    own_target = lax.dynamic_index_in_dim(target_lengths, core, 0, keepdims=False)
    own_memory = lax.dynamic_index_in_dim(memory_lengths, core, 0, keepdims=False)
    rows = tokens.shape[0]
    self_at = self_plan(own_bucket, rows)
    cross_at = cross_plan(own_bucket, own_memory, rows, memory.shape[0])
    places = jnp.arange(rows, dtype=jnp.int32)
    size = rows // jnp.left_shift(jnp.int32(1), own_bucket)
    segment = places // size
    live = jnp.any(
        (segment[:, None] == jnp.arange(4, dtype=jnp.int32)[None, :])
        & ((places - segment * size)[:, None] < own_target[None, :]),
        axis=1,
    )
    cols = (col_weights, exchange(col_weights))
    rws = (row_weights, exchange(row_weights))
    splits = (split_vectors, exchange(split_vectors))
    both = (0, 1)

    tokens_wide = wide(tokens)
    normed1, saved1 = norm_forward(tokens_wide, shared[0], shared[1])
    query, key, value, mem_key, mem_value, self_out, self_log = ([], [], [], [], [], [], [])
    for h in both:
        query.append(low(dot32(normed1, cols[h][0]) + splits[h][0]))
        key.append(low(dot32(normed1, cols[h][1])))
        value.append(low(dot32(normed1, cols[h][2]) + splits[h][1]))
        mem_key.append(low(dot32(memory, cols[h][4])))
        mem_value.append(low(dot32(memory, cols[h][5]) + splits[h][3]))
        out, log = attention(query[h], key[h], value[h], self_at, True)
        self_out.append(out)
        self_log.append(log)
    resid1 = tokens_wide + (dot32(self_out[0], rws[0][0]) + dot32(self_out[1], rws[1][0])) + shared[6]
    normed2, saved2 = norm_forward(resid1, shared[2], shared[3])
    cross_query, cross_out, cross_log = ([], [], [])
    for h in both:
        cross_query.append(low(dot32(normed2, cols[h][3]) + splits[h][2]))
        out, log = attention(cross_query[h], mem_key[h], mem_value[h], cross_at, False)
        cross_out.append(out)
        cross_log.append(log)
    resid2 = resid1 + (dot32(cross_out[0], rws[0][1]) + dot32(cross_out[1], rws[1][1])) + shared[7]
    normed3, saved3 = norm_forward(resid2, shared[4], shared[5])
    hidden, slope = ([], [])
    for h in both:
        a, b = up_project(normed3, cols[h], splits[h])
        hidden.append(a)
        slope.append(b)
    down = sum(
        jnp.einsum("ste,sed->td", hidden[h], rws[h][2:6], preferred_element_type=jnp.float32) for h in both
    )
    output = low(resid2 + down + shared[8])

    grad_out = jnp.where(live[:, None], cotangent, jnp.zeros_like(cotangent))
    grad_pre, grad_down, grad_up = ([], [], [])
    for h in both:
        grad_down.append(jnp.einsum("ste,td->sed", hidden[h], grad_out, preferred_element_type=jnp.float32))
        back = jnp.einsum("td,sed->ste", grad_out, rws[h][2:6], preferred_element_type=jnp.float32)
        grad_pre.append(low(wide(low(back)) * wide(slope[h])))
        grad_up.append(jnp.einsum("td,ste->sde", normed3, grad_pre[h], preferred_element_type=jnp.float32))
    up_bias = [jnp.sum(wide(grad_pre[h]), axis=1) for h in both]

    def reduce_parts(own, peer, first_bits):
        got = exchange(low(peer))
        return scatter_sum(to_parts(low(own + wide(got)), parts), first_bits)

    up_piece = reduce_parts(*grad_up, (0, 1))
    down_piece = reduce_parts(*grad_down, (1, 0))
    grad_normed3 = sum(
        jnp.einsum("ste,sde->td", grad_pre[h], cols[h][6:10], preferred_element_type=jnp.float32) for h in both
    )
    back3, gain3, shift3 = norm_back(saved3, shared[4], grad_normed3)
    grad_resid2 = wide(grad_out) + back3
    grad2 = low(grad_resid2)
    cross_row = [jnp.einsum("tf,td->fd", cross_out[h], grad2, preferred_element_type=jnp.float32) for h in both]
    grad_cq, grad_mk, grad_mv = ([], [], [])
    for h in both:
        grad = low(jnp.einsum("td,fd->tf", grad2, rws[h][1], preferred_element_type=jnp.float32))
        a, b, c = attention_back(
            cross_query[h], mem_key[h], mem_value[h], grad, cross_log[h], cross_at, False
        )
        grad_cq.append(a)
        grad_mk.append(b)
        grad_mv.append(c)

    def outer(x, g):
        return jnp.einsum("td,te->de", x, g, preferred_element_type=jnp.float32)

    def inner(g, w):
        return jnp.einsum("te,de->td", g, w, preferred_element_type=jnp.float32)

    cross_cols = [
        jnp.stack([outer(normed2, grad_cq[h]), outer(memory, grad_mk[h]), outer(memory, grad_mv[h])])
        for h in both
    ]
    cross_piece = reduce_parts(*cross_cols, (0, 1))
    memory_grad = sum(inner(grad_mk[h], cols[h][4]) + inner(grad_mv[h], cols[h][5]) for h in both)
    grad_normed2 = sum(inner(grad_cq[h], cols[h][3]) for h in both)
    back2, gain2, shift2 = norm_back(saved2, shared[2], grad_normed2)
    grad_resid1 = grad_resid2 + back2
    grad1 = low(grad_resid1)
    self_row = [jnp.einsum("tf,td->fd", self_out[h], grad1, preferred_element_type=jnp.float32) for h in both]
    row_piece = reduce_parts(*[jnp.stack([self_row[h], cross_row[h]]) for h in both], (1, 0))
    grad_q, grad_k, grad_v = ([], [], [])
    for h in both:
        grad = low(jnp.einsum("td,fd->tf", grad1, rws[h][0], preferred_element_type=jnp.float32))
        a, b, c = attention_back(query[h], key[h], value[h], grad, self_log[h], self_at, True)
        grad_q.append(a)
        grad_k.append(b)
        grad_v.append(c)
    self_cols = [
        jnp.stack([outer(normed1, grad_q[h]), outer(normed1, grad_k[h]), outer(normed1, grad_v[h])])
        for h in both
    ]
    got = exchange(low(self_cols[1]))
    self_sum = to_parts(low(self_cols[0] + wide(got)), parts)
    middle = self_sum.shape[0] // 2
    self_piece = jnp.concatenate(
        [scatter_sum(self_sum[:middle], (0, 1)), scatter_sum(self_sum[middle:], (1, 0))], axis=0
    )
    grad_normed1 = sum(
        inner(grad_q[h], cols[h][0]) + inner(grad_k[h], cols[h][1]) + inner(grad_v[h], cols[h][2]) for h in both
    )
    back1, gain1, shift1 = norm_back(saved1, shared[0], grad_normed1)
    input_grad = grad_resid1 + back1

    def column_sum(a):
        return jnp.sum(wide(a), axis=0)

    shared_grad = jnp.stack(
        [
            gain1,
            shift1,
            gain2,
            shift2,
            gain3,
            shift3,
            jnp.sum(grad_resid1, axis=0),
            jnp.sum(grad_resid2, axis=0),
            column_sum(grad_out),
        ]
    )
    split_grad = [
        jnp.concatenate(
            [
                jnp.stack([column_sum(grad_q[h]), column_sum(grad_v[h]), column_sum(grad_cq[h]), column_sum(grad_mv[h])]),
                up_bias[h],
            ]
        )
        for h in both
    ]
    first = jnp.where(core == 0, split_grad[0], split_grad[1])
    second = jnp.where(core == 0, split_grad[1], split_grad[0])
    vectors = jnp.concatenate([shared_grad, jnp.concatenate([first, second], axis=1)], axis=0)
    vectors = all_sum(vectors, parts)
    shared_sum = vectors[:9]
    split_sum = vectors[9:]

    def blocks(piece):
        m, rows_in, width = piece.shape
        return (
            piece.reshape(m, rows_in, width // BS, BS).transpose(0, 2, 1, 3).reshape(-1, rows_in, BS)
        )

    pieces = jnp.concatenate(
        [
            blocks(self_piece),
            blocks(cross_piece),
            blocks(up_piece),
            blocks(row_piece),
            blocks(down_piece),
        ],
        axis=0,
    )
    square = all_sum(jnp.sum(wide(pieces) * wide(pieces)).reshape(1, 1), parts)[0, 0]
    owned = slot_first.shape[0]
    sent = jnp.take(pieces, slot_order(block_slot), axis=0).reshape(parts, owned, BS // parts, BS)
    came = lax.all_to_all(sent, "dp", 0, 0, tiled=True)
    mine = wide(came).transpose(1, 0, 2, 3).reshape(owned, BS, BS)
    grad_norm = jnp.sqrt(square + jnp.sum(shared_sum * shared_sum) + jnp.sum(split_sum * split_sum))
    clip = clip_limit / jnp.maximum(grad_norm, clip_limit)

    def flat(a):
        return a.reshape(owned, BS, BS)

    updated = soap(
        clip,
        mine,
        flat(slot_first),
        flat(slot_second),
        flat(slot_master),
        flat(slot_left),
        flat(slot_right),
        flat(left_basis),
        flat(right_basis),
    )
    first_moment, second_moment, master_weight, master_copy, left_stat, right_stat, left_rotation, right_rotation = (
        a.reshape(slot_first.shape) for a in updated
    )
    shared_mean, shared_square, shared_values = adam_step(
        shared_sum * clip, shared_first, shared_second, shared_vectors, shared_rate
    )
    split_own = lax.dynamic_slice_in_dim(split_sum, core * half, half, axis=1)
    split_mean, split_square, split_values = adam_step(
        split_own * clip, split_first, split_second, split_vectors, split_rate
    )
    return (
        output,
        input_grad,
        memory_grad,
        first_moment,
        second_moment,
        master_weight,
        master_copy,
        left_stat,
        right_stat,
        left_rotation,
        right_rotation,
        shared_mean,
        shared_square,
        shared_values,
        split_mean,
        split_square,
        split_values,
        grad_norm,
    )


def solution(mesh):
    rows = P(("dp", "mp"), None)
    slots = P("dp", "mp", None, None)
    split = P(None, "mp")
    placed = (
        (rows, rows, rows, P("dp"), P("dp", None), P("dp", None), P())
        + (P(None, None, "mp"), P(None, "mp", None), P(), split, P(), P(), split, split)
        + (slots,) * 7
    )
    return jax.shard_map(
        partial(on_device, mesh.shape["dp"]),
        mesh=mesh,
        in_specs=placed,
        out_specs=(rows,) * 3 + (slots,) * 8 + (P(),) * 3 + (split,) * 3 + (P(),),
        check_vma=False,
    )
```

```python
from functools import partial

import jax
import jax.numpy as jnp
from jax import lax
from jax.experimental import pallas as pl
from jax.experimental.pallas import tpu as pltpu
from jax.sharding import PartitionSpec as P

HEAD_DIM=64; TQ=256
SCALE=HEAD_DIM**-0.5
EXPC=SCALE*1.4426950408889634
NEG=-1e30
NT=(((1,),(1,)),((),()))
NN=(((1,),(0,)),((),()))

def tail_mask(causal, limit):
    r=lax.broadcasted_iota(jnp.int32,(TQ,TQ),0)
    if causal:
        return r<=lax.broadcasted_iota(jnp.int32,(TQ,TQ),1)
    return r<limit

def fwd_kernel(causal, tiles, plan, q_ref, k_ref, v_ref, o_ref, l_ref, vt_ref):
    i=pl.program_id(1)
    start=plan[0,i]; count=plan[1,i]; limit=plan[2,i]
    @pl.when(i==0)
    def _():
        vt_ref[...]=v_ref[...].astype(jnp.float32).T.astype(jnp.bfloat16)
    for n in range(1,tiles+1):
        @pl.when(count==n)
        def _(n=n):
            outs=[]; logs=[]
            for h in range(2):
                cols=slice(h*HEAD_DIM,(h+1)*HEAD_DIM)
                q=q_ref[:,cols]
                parts=[]
                for j in range(n):
                    k=k_ref[pl.ds(pl.multiple_of((start+j)*TQ,TQ),TQ),cols]
                    s=lax.dot_general(k,q,NT,preferred_element_type=jnp.float32)
                    if j==n-1:
                        s=jnp.where(tail_mask(causal,limit),s,NEG)
                    parts.append(s)
                top=parts[0].max(axis=0,keepdims=True)
                for s in parts[1:]: top=jnp.maximum(top,s.max(axis=0,keepdims=True))
                total=None; acc=None
                for j,s in enumerate(parts):
                    p=jnp.exp2((s-top)*EXPC)
                    t=p.sum(axis=0,keepdims=True)
                    total=t if total is None else total+t
                    vt=vt_ref[cols,pl.ds(pl.multiple_of((start+j)*TQ,TQ),TQ)]
                    a=lax.dot_general(vt,p.astype(jnp.bfloat16),NN,preferred_element_type=jnp.float32)
                    acc=a if acc is None else acc+a
                outs.append(acc*(1.0/total))
                logs.append(top+jnp.log2(total)*(1.0/EXPC))
            o_ref[...]=jnp.concatenate(outs,axis=0).T.astype(o_ref.dtype)
            l_ref[0]=jnp.concatenate(logs,axis=0)

def attention(q,k,v,plan,causal):
    T,W=q.shape; M=k.shape[0]; pairs=W//128; tiles=M//TQ
    return pl.pallas_call(
        partial(fwd_kernel,causal,tiles),
        out_shape=(jax.ShapeDtypeStruct((T,W),jnp.bfloat16),jax.ShapeDtypeStruct((pairs,2,T),jnp.float32)),
        grid_spec=pltpu.PrefetchScalarGridSpec(num_scalar_prefetch=1,grid=(pairs,T//TQ),
            in_specs=[pl.BlockSpec((TQ,128),lambda h,i,_:(i,h)),
                      pl.BlockSpec((M,128),lambda h,i,_:(0,h)),
                      pl.BlockSpec((M,128),lambda h,i,_:(0,h))],
            out_specs=[pl.BlockSpec((TQ,128),lambda h,i,_:(i,h)),
                       pl.BlockSpec((1,2,TQ),lambda h,i,_:(h,0,i))],
            scratch_shapes=[pltpu.VMEM((128,M),jnp.bfloat16)]),
        compiler_params=pltpu.CompilerParams(vmem_limit_bytes=48*1024*1024),
        cost_estimate=pl.CostEstimate(flops=4*T*M*W//2,bytes_accessed=8*T*W,transcendentals=T*M*W//128),
    )(plan,q,k,v)

def bwd_kernel(causal, tiles, plan, q_ref, k_ref, v_ref, g_ref, l_ref, dq_ref, dk_ref, dv_ref, kt_ref, dk_acc, dv_acc):
    i=pl.program_id(1)
    start=plan[0,i]; count=plan[1,i]; limit=plan[2,i]
    @pl.when(i==0)
    def _():
        kt_ref[...]=k_ref[...].astype(jnp.float32).T.astype(jnp.bfloat16)
        dk_acc[...]=jnp.zeros_like(dk_acc)
        dv_acc[...]=jnp.zeros_like(dv_acc)
    for n in range(1,tiles+1):
        @pl.when(count==n)
        def _(n=n):
            outs=[]
            for h in range(2):
                cols=slice(h*HEAD_DIM,(h+1)*HEAD_DIM)
                q=q_ref[:,cols]; g=g_ref[:,cols]
                log=l_ref[0,h:h+1,:]
                ps=[]; ts=[]; delta=None
                for j in range(n):
                    rows=pl.ds(pl.multiple_of((start+j)*TQ,TQ),TQ)
                    s=lax.dot_general(k_ref[rows,cols],q,NT,preferred_element_type=jnp.float32)
                    p=jnp.exp2((s-log)*EXPC)
                    if j==n-1:
                        p=jnp.where(tail_mask(causal,limit),p,0.0)
                    dp=lax.dot_general(v_ref[rows,cols],g,NT,preferred_element_type=jnp.float32)
                    t=p*dp
                    d=t.sum(axis=0,keepdims=True)
                    delta=d if delta is None else delta+d
                    ps.append(p); ts.append(t)
                    dv_acc[rows,cols]+=lax.dot_general(p.astype(jnp.bfloat16),g,NN,preferred_element_type=jnp.float32)
                acc=None
                for j in range(n):
                    rows=pl.ds(pl.multiple_of((start+j)*TQ,TQ),TQ)
                    ds=(ts[j]-ps[j]*delta).astype(jnp.bfloat16)
                    dk_acc[rows,cols]+=lax.dot_general(ds,q,NN,preferred_element_type=jnp.float32)
                    a=lax.dot_general(kt_ref[cols,rows],ds,NN,preferred_element_type=jnp.float32)
                    acc=a if acc is None else acc+a
                outs.append(acc*SCALE)
            dq_ref[...]=jnp.concatenate(outs,axis=0).T.astype(dq_ref.dtype)
    @pl.when(i==pl.num_programs(1)-1)
    def _():
        dk_ref[...]=(dk_acc[...]*SCALE).astype(dk_ref.dtype)
        dv_ref[...]=dv_acc[...].astype(dv_ref.dtype)

def attention_back(q,k,v,g,logs,plan,causal):
    T,W=q.shape; M=k.shape[0]; pairs=W//128; tiles=M//TQ
    return pl.pallas_call(
        partial(bwd_kernel,causal,tiles),
        out_shape=(jax.ShapeDtypeStruct((T,W),jnp.bfloat16),jax.ShapeDtypeStruct((M,W),jnp.bfloat16),jax.ShapeDtypeStruct((M,W),jnp.bfloat16)),
        grid_spec=pltpu.PrefetchScalarGridSpec(num_scalar_prefetch=1,grid=(pairs,T//TQ),
            in_specs=[pl.BlockSpec((TQ,128),lambda h,i,_:(i,h)),
                      pl.BlockSpec((M,128),lambda h,i,_:(0,h)),
                      pl.BlockSpec((M,128),lambda h,i,_:(0,h)),
                      pl.BlockSpec((TQ,128),lambda h,i,_:(i,h)),
                      pl.BlockSpec((1,2,TQ),lambda h,i,_:(h,0,i))],
            out_specs=[pl.BlockSpec((TQ,128),lambda h,i,_:(i,h)),
                       pl.BlockSpec((M,128),lambda h,i,_:(0,h)),
                       pl.BlockSpec((M,128),lambda h,i,_:(0,h))],
            scratch_shapes=[pltpu.VMEM((128,M),jnp.bfloat16),pltpu.VMEM((M,128),jnp.float32),pltpu.VMEM((M,128),jnp.float32)]),
        compiler_params=pltpu.CompilerParams(vmem_limit_bytes=48*1024*1024),
        cost_estimate=pl.CostEstimate(flops=10*T*M*W//2,bytes_accessed=14*T*W,transcendentals=T*M*W//128),
    )(plan,q,k,v,g,logs)

def self_plan(bucket,T):
    i=jnp.arange(T//TQ,dtype=jnp.int32)
    seg=(T//TQ)//jnp.left_shift(jnp.int32(1),bucket)
    start=i//seg*seg
    return jnp.stack([start,i-start+1,jnp.full_like(i,TQ)])

def cross_plan(bucket,lengths,T,M):
    i=jnp.arange(T//TQ,dtype=jnp.int32)
    qseg=(T//TQ)//jnp.left_shift(jnp.int32(1),bucket)
    mseg=(M//TQ)//jnp.left_shift(jnp.int32(1),bucket)
    seq=i//qseg
    length=jnp.sum(jnp.where(seq[:,None]==jnp.arange(lengths.shape[0],dtype=jnp.int32)[None,:],lengths[None,:],0),axis=1)
    count=(length+TQ-1)//TQ
    return jnp.stack([seq*mseg,count,length-(count-1)*TQ])

BS=256; STEP=10
weight_rate=0.03; weight_decay=0.01
HI=lax.Precision.HIGHEST
def hdot(a,b,dims,precision=HI):
    return lax.dot_general(a,b,(dims,((),())),precision=precision,preferred_element_type=jnp.float32)
DIM_NN=((1,),(0,)); DIM_NT=((1,),(1,)); DIM_TN=((0,),(0,))

def parts2(a):
    top=a.astype(jnp.bfloat16)
    return top,(a-top.astype(jnp.float32)).astype(jnp.bfloat16)

def dot1(a,b,dims):
    return lax.dot_general(a,b,(dims,((),())),preferred_element_type=jnp.float32)

def dot3(a,b,dims):
    a0,a1=a; b0,b1=b
    return dot1(a0,b0,dims)+(dot1(a0,b1,dims)+dot1(a1,b0,dims))

def soap_kernel(clip_ref,g_ref,first,second,master,left,right,ql_ref,qr_ref,
                first_o,second_o,master_o,copy_o,left_o,right_o,al_o,ar_o,ml_o,mr_o):
    clip=clip_ref[0,0]
    g=g_ref[0]
    ql=ql_ref[0]; qr=qr_ref[0]
    scale=0.05*clip*clip
    left_new=0.95*left[0]+scale*dot1(g,g,DIM_NT)
    left_o[0]=left_new
    al=hdot(left_new,ql,DIM_NN); al_o[0]=al
    ml_o[0]=hdot(al,al,DIM_TN)
    right_new=0.95*right[0]+scale*dot1(g,g,DIM_TN)
    right_o[0]=right_new
    ar=hdot(right_new,qr,DIM_NN); ar_o[0]=ar
    mr_o[0]=hdot(ar,ar,DIM_TN)
    ql2=parts2(ql); qr2=parts2(qr)
    half=dot1(ql2[0],g,DIM_TN)+dot1(ql2[1],g,DIM_TN)
    rot=clip*dot3(parts2(half),qr2,DIM_NN)
    f=0.9*first[0]+0.1*rot; first_o[0]=f
    s=0.99*second[0]+0.01*rot*rot; second_o[0]=s
    ratio=f/(1.0-0.9**STEP)/(jnp.sqrt(s/(1.0-0.99**STEP))+1e-8)
    stepped=dot3(parts2(dot3(ql2,parts2(ratio),DIM_NN)),qr2,DIM_NT)
    m=master[0]-weight_rate*(stepped+weight_decay*master[0])
    master_o[0]=m; copy_o[0]=m.astype(jnp.bfloat16)

def soap_stage(clip,g,first,second,master,left,right,ql,qr):
    n=g.shape[0]
    spec=pl.BlockSpec((1,BS,BS),lambda i:(i,0,0))
    f32=jax.ShapeDtypeStruct((n,BS,BS),jnp.float32)
    return pl.pallas_call(soap_kernel,grid=(n,),
        out_shape=(f32,f32,f32,jax.ShapeDtypeStruct((n,BS,BS),jnp.bfloat16),f32,f32,f32,f32,f32,f32),
        in_specs=[pl.BlockSpec(memory_space=pltpu.SMEM)]+[spec]*8,
        out_specs=[spec]*10,
        compiler_params=pltpu.CompilerParams(vmem_limit_bytes=48*1024*1024),
    )(clip.reshape(1,1),g,first,second,master,left,right,ql,qr)

PW=64
def chol_kernel(al_ref,ar_ref,ml_ref,mr_ref,ql_o,qr_o,work,tile,pivot):
    n=al_ref.shape[0]; pairs=n
    def load(m,_):
        work[m]=ml_ref[m]; work[n+m]=mr_ref[m]
        return 0
    lax.fori_loop(0,n,load,0)
    lane=lax.broadcasted_iota(jnp.int32,(1,2*PW),1)
    base=lane//PW*PW
    bigcol=lax.broadcasted_iota(jnp.int32,(PW,BS),1)
    bigrow=lax.broadcasted_iota(jnp.int32,(PW,BS),0)
    lower=lax.broadcasted_iota(jnp.int32,(PW,2*PW),1)%PW<=lax.broadcasted_iota(jnp.int32,(PW,2*PW),0)
    for p in range(BS//PW):
        lo=p*PW; at=slice(lo,lo+PW)
        for j in range(pairs):
            tile[j]=jnp.concatenate([work[2*j,at,at],work[2*j+1,at,at]],axis=1)
        for quarter in range(4):
            top=quarter*PW//4; height=PW-top
            rows=lax.broadcasted_iota(jnp.int32,(height,2*PW),0)+top
            def step(k,_):
                here=lane-base==k
                below=rows>k
                fill=jnp.where(rows==k,1.0,0.0)
                t=tile[:,top:,:]
                r=tile[:,pl.ds(k,1),:]
                flat=pairs*height
                c=jnp.take_along_axis(t.reshape(flat,2*PW),jnp.broadcast_to(base+k,(flat,2*PW)),axis=1).reshape(pairs,height,2*PW)
                wide_r=jnp.broadcast_to(r[0],(8,2*PW)) if pairs==1 else r.reshape(pairs,2*PW)
                d=jnp.take_along_axis(wide_r,jnp.broadcast_to(base+k,wide_r.shape),axis=1)[:pairs].reshape(pairs,1,2*PW)
                r=jnp.where(here[None],1.0,r)*(1.0/d)
                pivot[:,pl.ds(k,1),:]=d
                tile[:,top:,:]=jnp.where(here[None],fill[None],t)-jnp.where(below[None],c,0.0)*r
                return 0
            lax.fori_loop(top,top+PW//4,step,0)
        for j in range(pairs):
            tile[j]=jnp.where(lower,tile[j]*lax.rsqrt(pivot[j]),0.0)
        inside=(bigcol>=lo)&(bigcol<lo+PW)
        eye=jnp.where(bigcol-lo==bigrow,1.0,0.0)
        def apply(j,_):
            both=tile[j]
            for s in range(2):
                m=2*j+s
                r=hdot(both[:,s*PW:(s+1)*PW],jnp.where(inside,eye,work[m,at,:]),DIM_NN)
                work[m,at,:]=r
                if p<BS//PW-1:
                    rest=jnp.where(inside[0:1],0.0,work[m,lo+PW:,:])
                    work[m,lo+PW:,:]=rest-hdot(r[:,lo+PW:],r,DIM_TN)
            return 0
        lax.fori_loop(0,pairs,apply,0)
    keep=lax.broadcasted_iota(jnp.int32,(BS,BS),1)<=lax.broadcasted_iota(jnp.int32,(BS,BS),0)
    def final(m,_):
        ql_o[m]=hdot(al_ref[m],jnp.where(keep,work[m],0.0),DIM_NT)
        qr_o[m]=hdot(ar_ref[m],jnp.where(keep,work[n+m],0.0),DIM_NT)
        return 0
    lax.fori_loop(0,n,final,0)

def chol_stage(al,ar,ml,mr):
    n=al.shape[0]
    f32=jax.ShapeDtypeStruct((n,BS,BS),jnp.float32)
    vm=pl.BlockSpec(memory_space=pltpu.VMEM)
    return pl.pallas_call(chol_kernel,out_shape=(f32,f32),in_specs=[vm]*4,out_specs=[vm]*2,
        scratch_shapes=[pltpu.VMEM((2*n,BS,BS),jnp.float32),pltpu.VMEM((n,PW,2*PW),jnp.float32),pltpu.VMEM((n,PW,2*PW),jnp.float32)],
        compiler_params=pltpu.CompilerParams(vmem_limit_bytes=56*1024*1024))(al,ar,ml,mr)

def soap(clip,g,first,second,master,left,right,ql,qr):
    f,s,m,c,l,r,al,ar,ml,mr=soap_stage(clip,g,first,second,master,left,right,ql,qr)
    lr,rr=chol_stage(al,ar,ml,mr)
    return f,s,m,c,l,r,lr,rr


LEN = 1024
shared_rate = 0.6
split_rate = 0.2
clip_limit = 1.0
SWAP = [(0, 1), (1, 0)]


def adam_step(gradient, first_state, second_state, values, step_rate):
    first_new = 0.9 * first_state + 0.1 * gradient
    second_new = 0.99 * second_state + 0.01 * gradient * gradient
    ratio = first_new / (1.0 - 0.9**STEP) / (jnp.sqrt(second_new / (1.0 - 0.99**STEP)) + 1e-08)
    return (first_new, second_new, values - step_rate * ratio)


def norm_forward(values, gain, shift):
    centered = values - jnp.mean(values, axis=-1, keepdims=True)
    inverse = lax.rsqrt(jnp.mean(centered * centered, axis=-1, keepdims=True) + 1e-05)
    hat = centered * inverse
    return (hat * gain + shift).astype(jnp.bfloat16), (values, inverse)


def norm_back(saved, gain, grad):
    values, inverse = saved
    hat = (values - jnp.mean(values, axis=-1, keepdims=True)) * inverse
    inner = grad * gain
    back = inverse * (
        inner
        - jnp.mean(inner, axis=-1, keepdims=True)
        - hat * jnp.mean(inner * hat, axis=-1, keepdims=True)
    )
    return back, jnp.sum(grad * hat, axis=0), jnp.sum(grad, axis=0)


def dot32(a, b):
    return jnp.dot(a, b, preferred_element_type=jnp.float32)


def low(a):
    return a.astype(jnp.bfloat16)


def wide(a):
    return a.astype(jnp.float32)


def up_kernel(x_ref, w_ref, b_ref, h_ref, d_ref):
    rows = 256
    for r in range(x_ref.shape[0] // rows):
        at = slice(r * rows, (r + 1) * rows)
        v = jnp.dot(x_ref[at, :], w_ref[0], preferred_element_type=jnp.float32) + b_ref[0]
        z = jnp.abs(v)
        t = 1.0 / (1.0 + (0.3275911 * 0.7071067811865476) * z)
        e = jnp.exp2(v * v * (-0.5 * 1.4426950408889634))
        poly = t * (
            0.5 * 0.254829592
            + t * (0.5 * -0.284496736 + t * (0.5 * 1.421413741 + t * (0.5 * -1.453152027 + t * (0.5 * 1.061405429))))
        )
        tail = poly * e
        phi = jnp.where(v >= 0.0, 1.0 - tail, tail)
        h_ref[0, at, :] = (v * phi).astype(h_ref.dtype)
        d_ref[0, at, :] = (phi + v * e * 0.3989422804014327).astype(d_ref.dtype)


def up_project(x, col, bias):
    rows, depth = x.shape
    width = col.shape[2]
    shape = jax.ShapeDtypeStruct((4, rows, width), jnp.bfloat16)
    return pl.pallas_call(
        up_kernel,
        grid=(4,),
        out_shape=(shape, shape),
        in_specs=[
            pl.BlockSpec((rows, depth), lambda s: (0, 0)),
            pl.BlockSpec((1, depth, width), lambda s: (s + 6, 0, 0)),
            pl.BlockSpec((1, 1, width), lambda s: (s, 0, 0)),
        ],
        out_specs=[pl.BlockSpec((1, rows, width), lambda s: (s, 0, 0))] * 2,
        compiler_params=pltpu.CompilerParams(vmem_limit_bytes=48 * 1024 * 1024),
        cost_estimate=pl.CostEstimate(
            flops=8 * rows * depth * width, bytes_accessed=24 * rows * width, transcendentals=8 * rows * width
        ),
    )(x, col, bias[4:8, None, :])


def exchange(array):
    return lax.ppermute(array, "mp", SWAP)


def to_parts(array, parts):
    stacked, height, width = array.shape
    return array.reshape(stacked * height // BS, parts, BS // parts, width)


def tie(*arrays):
    return lax.optimization_barrier(arrays)


class Staged:
    def __init__(self, array, first_bits):
        self.array = array
        parts = array.shape[1]
        bits = parts.bit_length() - 1
        self.parts = parts
        self.array = array.reshape((array.shape[0],) + (2,) * bits + array.shape[2:])
        self.left = list(range(bits - 1, -1, -1))
        self.order = [b for b in first_bits if b < bits] + [b for b in range(bits) if b not in first_bits]
        self.got = None

    def send(self):
        if not self.order:
            return
        b = self.order.pop(0)
        axis = 1 + self.left.index(b)
        self.left.remove(b)
        mine = (lax.axis_index("dp") >> b) & 1
        self.keep = lax.dynamic_index_in_dim(self.array, mine, axis, keepdims=False)
        give = lax.dynamic_index_in_dim(self.array, 1 - mine, axis, keepdims=False)
        self.got = lax.ppermute(give, "dp", [(i, i ^ (1 << b)) for i in range(self.parts)])

    def take(self):
        if self.got is not None:
            self.array = low(wide(self.keep) + wide(self.got))
            self.got = None

    def finish(self):
        self.take()
        while self.order:
            self.send()
            self.take()
        return self.array


def checkpoint(anchor, *sums):
    waiting = [s for s in sums if s.got is not None]
    anchor, *got = tie(anchor, *[s.got for s in waiting])
    for s, g in zip(waiting, got):
        s.got = g
        s.take()
        s.send()
    return anchor


def all_sum(array, parts):
    array = array + lax.ppermute(array, "mp", SWAP)
    for b in range(parts.bit_length() - 1):
        array = array + lax.ppermute(array, "dp", [(i, i ^ (1 << b)) for i in range(parts)])
    return array


def slot_order(block_slot):
    numbers = jnp.arange(block_slot.shape[0], dtype=jnp.int32)
    return jnp.sum(jnp.where(block_slot[None, :] == numbers[:, None], numbers[None, :], 0), axis=1)


def on_device(
    parts,
    tokens,
    memory,
    cotangent,
    bucket,
    target_lengths,
    memory_lengths,
    block_slot,
    col_weights,
    row_weights,
    shared_vectors,
    split_vectors,
    shared_first,
    shared_second,
    split_first,
    split_second,
    slot_first,
    slot_second,
    slot_master,
    slot_left,
    slot_right,
    left_basis,
    right_basis,
):
    core = lax.axis_index("mp")
    half = col_weights.shape[2]
    shared = shared_vectors
    own_bucket = lax.dynamic_index_in_dim(bucket, core, 0, keepdims=False)
    own_target = lax.dynamic_index_in_dim(target_lengths, core, 0, keepdims=False)
    own_memory = lax.dynamic_index_in_dim(memory_lengths, core, 0, keepdims=False)
    rows = tokens.shape[0]
    self_at = self_plan(own_bucket, rows)
    cross_at = cross_plan(own_bucket, own_memory, rows, memory.shape[0])
    places = jnp.arange(rows, dtype=jnp.int32)
    size = rows // jnp.left_shift(jnp.int32(1), own_bucket)
    segment = places // size
    live = jnp.any(
        (segment[:, None] == jnp.arange(4, dtype=jnp.int32)[None, :])
        & ((places - segment * size)[:, None] < own_target[None, :]),
        axis=1,
    )
    cols = (col_weights, exchange(col_weights))
    rws = (row_weights, exchange(row_weights))
    splits = (split_vectors, exchange(split_vectors))
    both = (0, 1)

    tokens_wide = wide(tokens)
    normed1, saved1 = norm_forward(tokens_wide, shared[0], shared[1])
    query, key, value, mem_key, mem_value, self_out, self_log = ([], [], [], [], [], [], [])
    for h in both:
        query.append(low(dot32(normed1, cols[h][0]) + splits[h][0]))
        key.append(low(dot32(normed1, cols[h][1])))
        value.append(low(dot32(normed1, cols[h][2]) + splits[h][1]))
        mem_key.append(low(dot32(memory, cols[h][4])))
        mem_value.append(low(dot32(memory, cols[h][5]) + splits[h][3]))
        out, log = attention(query[h], key[h], value[h], self_at, True)
        self_out.append(out)
        self_log.append(log)
    resid1 = tokens_wide + (dot32(self_out[0], rws[0][0]) + dot32(self_out[1], rws[1][0])) + shared[6]
    normed2, saved2 = norm_forward(resid1, shared[2], shared[3])
    cross_query, cross_out, cross_log = ([], [], [])
    for h in both:
        cross_query.append(low(dot32(normed2, cols[h][3]) + splits[h][2]))
        out, log = attention(cross_query[h], mem_key[h], mem_value[h], cross_at, False)
        cross_out.append(out)
        cross_log.append(log)
    resid2 = resid1 + (dot32(cross_out[0], rws[0][1]) + dot32(cross_out[1], rws[1][1])) + shared[7]
    normed3, saved3 = norm_forward(resid2, shared[4], shared[5])
    hidden, slope = ([], [])
    for h in both:
        a, b = up_project(normed3, cols[h], splits[h])
        hidden.append(a)
        slope.append(b)
    down = sum(
        jnp.einsum("ste,sed->td", hidden[h], rws[h][2:6], preferred_element_type=jnp.float32) for h in both
    )
    output = low(resid2 + down + shared[8])

    grad_out = jnp.where(live[:, None], cotangent, jnp.zeros_like(cotangent))
    dims = "ste,td->sed"
    down_peer = exchange(low(jnp.einsum(dims, hidden[1], grad_out, preferred_element_type=jnp.float32)))
    down_own = jnp.einsum(dims, hidden[0], grad_out, preferred_element_type=jnp.float32)
    grad_pre = []
    for h in both:
        back = jnp.einsum("td,sed->ste", grad_out, rws[h][2:6], preferred_element_type=jnp.float32)
        grad_pre.append(low(wide(low(back)) * wide(slope[h])))
    grad_pre[0], down_peer = tie(grad_pre[0], down_peer)
    down_sum = Staged(to_parts(low(down_own + wide(down_peer)), parts), (1, 0))
    down_sum.send()
    dims = "td,ste->sde"
    up_peer = exchange(low(jnp.einsum(dims, normed3, grad_pre[1], preferred_element_type=jnp.float32)))
    up_own = jnp.einsum(dims, normed3, grad_pre[0], preferred_element_type=jnp.float32)
    up_bias = [jnp.sum(wide(grad_pre[h]), axis=1) for h in both]
    grad_normed3 = sum(
        jnp.einsum("ste,sde->td", grad_pre[h], cols[h][6:10], preferred_element_type=jnp.float32) for h in both
    )
    back3, gain3, shift3 = norm_back(saved3, shared[4], grad_normed3)
    grad_resid2 = wide(grad_out) + back3
    grad2 = low(grad_resid2)
    grad2, up_peer = tie(grad2, up_peer)
    up_sum = Staged(to_parts(low(up_own + wide(up_peer)), parts), (0, 1))
    up_sum.send()

    def outer(x, g):
        return jnp.einsum("td,te->de", x, g, preferred_element_type=jnp.float32)

    def inner(g, w):
        return jnp.einsum("te,de->td", g, w, preferred_element_type=jnp.float32)

    cross_row = [outer(cross_out[h], grad2) for h in both]
    cross_row_peer = exchange(low(cross_row[1]))
    grad_cq, grad_mk, grad_mv = ([], [], [])
    for h in both:
        grad = low(jnp.einsum("td,fd->tf", grad2, rws[h][1], preferred_element_type=jnp.float32))
        if h == 1:
            grad = checkpoint(grad, down_sum)
        a, b, c = attention_back(cross_query[h], mem_key[h], mem_value[h], grad, cross_log[h], cross_at, False)
        grad_cq.append(a)
        grad_mk.append(b)
        grad_mv.append(c)
    grad_cq[1] = checkpoint(grad_cq[1], down_sum, up_sum)
    cross_peer = exchange(
        low(jnp.stack([outer(normed2, grad_cq[1]), outer(memory, grad_mk[1]), outer(memory, grad_mv[1])]))
    )
    cross_own = jnp.stack([outer(normed2, grad_cq[0]), outer(memory, grad_mk[0]), outer(memory, grad_mv[0])])
    grad_cq[0], cross_peer, cross_row_peer = tie(grad_cq[0], cross_peer, cross_row_peer)
    cross_sum = Staged(to_parts(low(cross_own + wide(cross_peer)), parts), (0, 1))
    row1_sum = Staged(to_parts(low(cross_row[0] + wide(cross_row_peer))[None], parts), (1, 0))
    cross_sum.send()
    row1_sum.send()
    grad_normed2 = sum(inner(grad_cq[h], cols[h][3]) for h in both)
    back2, gain2, shift2 = norm_back(saved2, shared[2], grad_normed2)
    grad_resid1 = grad_resid2 + back2
    grad1 = low(grad_resid1)
    grad1 = checkpoint(grad1, down_sum, up_sum)
    self_row = [outer(self_out[h], grad1) for h in both]
    self_row_peer = exchange(low(self_row[1]))
    grad_q, grad_k, grad_v = ([], [], [])
    for h in both:
        grad = low(jnp.einsum("td,fd->tf", grad1, rws[h][0], preferred_element_type=jnp.float32))
        if h == 1:
            grad = checkpoint(grad, up_sum, cross_sum, row1_sum)
        a, b, c = attention_back(query[h], key[h], value[h], grad, self_log[h], self_at, True)
        grad_q.append(a)
        grad_k.append(b)
        grad_v.append(c)
    row0_sum = Staged(to_parts(low(self_row[0] + wide(self_row_peer))[None], parts), (1, 0))
    row0_sum.send()
    grad_q[1] = checkpoint(grad_q[1], up_sum, cross_sum, row1_sum)
    self_peer = exchange(
        low(jnp.stack([outer(normed1, grad_q[1]), outer(normed1, grad_k[1]), outer(normed1, grad_v[1])]))
    )
    self_own = jnp.stack([outer(normed1, grad_q[0]), outer(normed1, grad_k[0]), outer(normed1, grad_v[0])])
    grad_q[0], self_peer = tie(grad_q[0], self_peer)
    self_all = to_parts(low(self_own + wide(self_peer)), parts)
    middle = self_all.shape[0] // 2
    self_sums = [Staged(self_all[:middle], (0, 1)), Staged(self_all[middle:], (1, 0))]
    for a in self_sums:
        a.send()
    grad_normed1 = sum(
        inner(grad_q[h], cols[h][0]) + inner(grad_k[h], cols[h][1]) + inner(grad_v[h], cols[h][2]) for h in both
    )
    back1, gain1, shift1 = norm_back(saved1, shared[0], grad_normed1)
    input_grad = grad_resid1 + back1
    memory_grad = sum(inner(grad_mk[h], cols[h][4]) + inner(grad_mv[h], cols[h][5]) for h in both)
    self_piece = jnp.concatenate([a.finish() for a in self_sums], axis=0)
    cross_piece = cross_sum.finish()
    up_piece = up_sum.finish()
    down_piece = down_sum.finish()
    row_piece = jnp.concatenate([row0_sum.finish(), row1_sum.finish()], axis=0)

    def column_sum(a):
        return jnp.sum(wide(a), axis=0)

    shared_grad = jnp.stack(
        [
            gain1,
            shift1,
            gain2,
            shift2,
            gain3,
            shift3,
            jnp.sum(grad_resid1, axis=0),
            jnp.sum(grad_resid2, axis=0),
            column_sum(grad_out),
        ]
    )
    split_grad = [
        jnp.concatenate(
            [
                jnp.stack([column_sum(grad_q[h]), column_sum(grad_v[h]), column_sum(grad_cq[h]), column_sum(grad_mv[h])]),
                up_bias[h],
            ]
        )
        for h in both
    ]
    first = jnp.where(core == 0, split_grad[0], split_grad[1])
    second = jnp.where(core == 0, split_grad[1], split_grad[0])
    vectors = jnp.concatenate([shared_grad, jnp.concatenate([first, second], axis=1)], axis=0)
    vectors = all_sum(vectors, parts)
    shared_sum = vectors[:9]
    split_sum = vectors[9:]

    def blocks(piece):
        m, rows_in, width = piece.shape
        return (
            piece.reshape(m, rows_in, width // BS, BS).transpose(0, 2, 1, 3).reshape(-1, rows_in, BS)
        )

    pieces = jnp.concatenate(
        [
            blocks(self_piece),
            blocks(cross_piece),
            blocks(up_piece),
            blocks(row_piece),
            blocks(down_piece),
        ],
        axis=0,
    )
    square = all_sum(jnp.sum(wide(pieces) * wide(pieces)).reshape(1, 1), parts)[0, 0]
    owned = slot_first.shape[0]
    sent = jnp.take(pieces, slot_order(block_slot), axis=0).reshape(parts, owned, BS // parts, BS)
    came = lax.all_to_all(sent, "dp", 0, 0, tiled=True)
    mine = came.transpose(1, 0, 2, 3).reshape(owned, BS, BS)
    grad_norm = jnp.sqrt(square + jnp.sum(shared_sum * shared_sum) + jnp.sum(split_sum * split_sum))
    clip = clip_limit / jnp.maximum(grad_norm, clip_limit)

    def flat(a):
        return a.reshape(owned, BS, BS)

    updated = soap(
        clip,
        mine,
        flat(slot_first),
        flat(slot_second),
        flat(slot_master),
        flat(slot_left),
        flat(slot_right),
        flat(left_basis),
        flat(right_basis),
    )
    first_moment, second_moment, master_weight, master_copy, left_stat, right_stat, left_rotation, right_rotation = (
        a.reshape(slot_first.shape) for a in updated
    )
    shared_mean, shared_square, shared_values = adam_step(
        shared_sum * clip, shared_first, shared_second, shared_vectors, shared_rate
    )
    split_own = lax.dynamic_slice_in_dim(split_sum, core * half, half, axis=1)
    split_mean, split_square, split_values = adam_step(
        split_own * clip, split_first, split_second, split_vectors, split_rate
    )
    return (
        output,
        input_grad,
        memory_grad,
        first_moment,
        second_moment,
        master_weight,
        master_copy,
        left_stat,
        right_stat,
        left_rotation,
        right_rotation,
        shared_mean,
        shared_square,
        shared_values,
        split_mean,
        split_square,
        split_values,
        grad_norm,
    )


def solution(mesh):
    rows = P(("dp", "mp"), None)
    slots = P("dp", "mp", None, None)
    split = P(None, "mp")
    placed = (
        (rows, rows, rows, P("dp"), P("dp", None), P("dp", None), P())
        + (P(None, None, "mp"), P(None, "mp", None), P(), split, P(), P(), split, split)
        + (slots,) * 7
    )
    return jax.shard_map(
        partial(on_device, mesh.shape["dp"]),
        mesh=mesh,
        in_specs=placed,
        out_specs=(rows,) * 3 + (slots,) * 8 + (P(),) * 3 + (split,) * 3 + (P(),),
        check_vma=False,
    )
```

```python
from functools import partial

import jax
import jax.numpy as jnp
from jax import lax
from jax.experimental import pallas as pl
from jax.experimental.pallas import tpu as pltpu
from jax.sharding import PartitionSpec as P

HEAD_DIM=64; TQ=256
SCALE=HEAD_DIM**-0.5
EXPC=SCALE*1.4426950408889634
NEG=-1e30
NT=(((1,),(1,)),((),()))
NN=(((1,),(0,)),((),()))

def tail_mask(causal, limit):
    r=lax.broadcasted_iota(jnp.int32,(TQ,TQ),0)
    if causal:
        return r<=lax.broadcasted_iota(jnp.int32,(TQ,TQ),1)
    return r<limit

def rows_of(i,n=1):
    return slice(i*TQ,(i+n)*TQ)

def head_cols(h):
    return slice(h*HEAD_DIM,(h+1)*HEAD_DIM)

def each_case(causal,plan,tiles,emit):
    for b in range(3):
        count=1<<b; size=tiles//count
        if causal:
            @pl.when(plan[0]==b)
            def _(count=count,size=size):
                emit([(s*size,size,s*size,size,None) for s in range(count)])
        elif size==1:
            @pl.when(plan[0]==b)
            def _(count=count,size=size):
                emit([(s,1,s,1,plan[1+s]) for s in range(count)])
        else:
            for s in range(count):
                length=plan[1+s]
                for n in range(1,size+1):
                    @pl.when((plan[0]==b)&(length>(n-1)*TQ)&(length<=n*TQ))
                    def _(s=s,n=n,size=size,length=length):
                        emit([(s*size,size,s*size,n,length-(n-1)*TQ)])

def tile_items(causal,segments):
    out=[]
    for q0,qn,k0,kn,limit in segments:
        for i in range(qn):
            out.append((q0+i,k0,i+1 if causal else kn,limit))
    return out

def fwd_kernel(causal, tiles, plan, q_ref, k_ref, v_ref, o_ref, l_ref, vt_ref):
    vt_ref[...]=v_ref[...].astype(jnp.float32).T.astype(jnp.bfloat16)
    def emit(segments):
        items=[(t,h) for t in tile_items(causal,segments) for h in range(2)]
        def scores(item):
            (i,k0,n,limit),h=item
            q=q_ref[rows_of(i),head_cols(h)]
            parts=[]
            for j in range(n):
                s=lax.dot_general(k_ref[rows_of(k0+j),head_cols(h)],q,NT,preferred_element_type=jnp.float32)
                if j==n-1:
                    s=jnp.where(tail_mask(causal,limit),s,NEG)
                parts.append(s)
            return parts
        ahead=scores(items[0])
        held=None
        for c,((i,k0,n,limit),h) in enumerate(items):
            parts=ahead
            if c+1<len(items): ahead=scores(items[c+1])
            top=parts[0].max(axis=0,keepdims=True)
            for s in parts[1:]: top=jnp.maximum(top,s.max(axis=0,keepdims=True))
            total=None; acc=None
            for j,s in enumerate(parts):
                p=jnp.exp2((s-top)*EXPC)
                t=p.sum(axis=0,keepdims=True)
                total=t if total is None else total+t
                a=lax.dot_general(vt_ref[head_cols(h),rows_of(k0+j)],p.astype(jnp.bfloat16),NN,preferred_element_type=jnp.float32)
                acc=a if acc is None else acc+a
            acc=acc*(1.0/total)
            l_ref[0,h:h+1,rows_of(i)]=top+jnp.log2(total)*(1.0/EXPC)
            if h==0: held=acc
            else: o_ref[rows_of(i),:]=jnp.concatenate([held,acc],axis=0).T.astype(o_ref.dtype)
    each_case(causal,plan,tiles,emit)

def attention(q,k,v,plan,causal):
    T,W=q.shape; M=k.shape[0]; pairs=W//128; tiles=T//TQ
    return pl.pallas_call(
        partial(fwd_kernel,causal,tiles),
        out_shape=(jax.ShapeDtypeStruct((T,W),jnp.bfloat16),jax.ShapeDtypeStruct((pairs,2,T),jnp.float32)),
        grid_spec=pltpu.PrefetchScalarGridSpec(num_scalar_prefetch=1,grid=(pairs,),
            in_specs=[pl.BlockSpec((T,128),lambda h,_:(0,h)),
                      pl.BlockSpec((M,128),lambda h,_:(0,h)),
                      pl.BlockSpec((M,128),lambda h,_:(0,h))],
            out_specs=[pl.BlockSpec((T,128),lambda h,_:(0,h)),
                       pl.BlockSpec((1,2,T),lambda h,_:(h,0,0))],
            scratch_shapes=[pltpu.VMEM((128,M),jnp.bfloat16)]),
        compiler_params=pltpu.CompilerParams(vmem_limit_bytes=48*1024*1024),
        cost_estimate=pl.CostEstimate(flops=4*T*M*W//2,bytes_accessed=8*T*W,transcendentals=T*M*W//128),
    )(plan,q,k,v)

def bwd_kernel(causal, tiles, plan, q_ref, k_ref, v_ref, g_ref, o_ref, l_ref, dq_ref, dk_ref, dv_ref, kt_ref, p_ref, s_ref, d_ref):
    kt_ref[...]=k_ref[...].astype(jnp.float32).T.astype(jnp.bfloat16)
    if not causal:
        dk_ref[...]=jnp.zeros_like(dk_ref)
        dv_ref[...]=jnp.zeros_like(dv_ref)
    ones=jnp.ones((8,HEAD_DIM),jnp.bfloat16)
    for h in range(2):
        prod=g_ref[:,head_cols(h)].astype(jnp.float32)*o_ref[:,head_cols(h)].astype(jnp.float32)
        top=prod.astype(jnp.bfloat16)
        rest=(prod-top.astype(jnp.float32)).astype(jnp.bfloat16)
        d_ref[h]=lax.dot_general(ones,top,NT,preferred_element_type=jnp.float32)+lax.dot_general(ones,rest,NT,preferred_element_type=jnp.float32)
    def emit(segments):
        items=[(i,k0+j,j,n,limit,h) for h in range(2) for i,k0,n,limit in tile_items(causal,segments) for j in range(n)]
        def products(item):
            i,k,j,n,limit,h=item
            return (lax.dot_general(k_ref[rows_of(k),head_cols(h)],q_ref[rows_of(i),head_cols(h)],NT,preferred_element_type=jnp.float32),
                    lax.dot_general(v_ref[rows_of(k),head_cols(h)],g_ref[rows_of(i),head_cols(h)],NT,preferred_element_type=jnp.float32))
        def key_side(h):
            work=[]
            for q0,qn,k0,kn,limit in segments:
                for j in range(kn):
                    first=q0+j if causal else q0
                    def one(k=k0+j,cols=slice(first*TQ,(q0+qn)*TQ)):
                        a=lax.dot_general(p_ref[h,rows_of(k),cols],g_ref[cols,head_cols(h)],NN,preferred_element_type=jnp.float32)
                        dv_ref[rows_of(k),head_cols(h)]=a.astype(dv_ref.dtype)
                        b=lax.dot_general(s_ref[h,rows_of(k),cols],q_ref[cols,head_cols(h)],NN,preferred_element_type=jnp.float32)
                        dk_ref[rows_of(k),head_cols(h)]=(b*SCALE).astype(dk_ref.dtype)
                    work.append(one)
            return work
        ahead=products(items[0])
        later=[]
        acc=None
        for c,(i,k,j,n,limit,h) in enumerate(items):
            s,dp=ahead
            if c+1<len(items): ahead=products(items[c+1])
            p=jnp.exp2((s-l_ref[0,h:h+1,rows_of(i)])*EXPC)
            if j==n-1: p=jnp.where(tail_mask(causal,limit),p,0.0)
            p_ref[h,rows_of(k),rows_of(i)]=p.astype(jnp.bfloat16)
            ds=(p*(dp-d_ref[h,0:1,rows_of(i)])).astype(jnp.bfloat16)
            s_ref[h,rows_of(k),rows_of(i)]=ds
            a=lax.dot_general(kt_ref[head_cols(h),rows_of(k)],ds,NN,preferred_element_type=jnp.float32)
            acc=a if j==0 else acc+a
            if j==n-1:
                dq_ref[rows_of(i),head_cols(h)]=(acc*SCALE).T.astype(dq_ref.dtype)
                if later: later.pop(0)()
            if c+1==len(items)//2: later=key_side(0)
        for one in later+key_side(1): one()
    each_case(causal,plan,tiles,emit)

def attention_back(q,k,v,g,out,logs,plan,causal):
    T,W=q.shape; M=k.shape[0]; pairs=W//128; tiles=T//TQ
    narrow=pl.BlockSpec((T,128),lambda h,_:(0,h))
    wide=pl.BlockSpec((M,128),lambda h,_:(0,h))
    return pl.pallas_call(
        partial(bwd_kernel,causal,tiles),
        out_shape=(jax.ShapeDtypeStruct((T,W),jnp.bfloat16),jax.ShapeDtypeStruct((M,W),jnp.bfloat16),jax.ShapeDtypeStruct((M,W),jnp.bfloat16)),
        grid_spec=pltpu.PrefetchScalarGridSpec(num_scalar_prefetch=1,grid=(pairs,),
            in_specs=[narrow,wide,wide,narrow,narrow,pl.BlockSpec((1,2,T),lambda h,_:(h,0,0))],
            out_specs=[narrow,wide,wide],
            scratch_shapes=[pltpu.VMEM((128,M),jnp.bfloat16),pltpu.VMEM((2,M,T),jnp.bfloat16),pltpu.VMEM((2,M,T),jnp.bfloat16),pltpu.VMEM((2,8,T),jnp.float32)]),
        compiler_params=pltpu.CompilerParams(vmem_limit_bytes=48*1024*1024),
        cost_estimate=pl.CostEstimate(flops=10*T*M*W//2,bytes_accessed=14*T*W,transcendentals=T*M*W//128),
    )(plan,q,k,v,g,out,logs)

def self_plan(bucket,T):
    return bucket.reshape(1)

def cross_plan(bucket,lengths,T,M):
    return jnp.concatenate([bucket.reshape(1),lengths])

COLS=(((0,),(0,)),((),()))
def prod(a,b,dims):
    return lax.dot_general(a,b,dims,preferred_element_type=jnp.float32)

def gelu_parts(v):
    t=1.0/(1.0+(0.3275911*0.7071067811865476)*jnp.abs(v))
    e=jnp.exp2(v*v*(-0.5*1.4426950408889634))
    poly=t*(0.5*0.254829592+t*(0.5*-0.284496736+t*(0.5*1.421413741+t*(0.5*-1.453152027+t*(0.5*1.061405429)))))
    tail=poly*e
    phi=jnp.where(v>=0.0,1.0-tail,tail)
    return v*phi,phi+v*e*0.3989422804014327

def feed_kernel(x_ref,g_ref,up_ref,dn_ref,b_ref,down_ref,back_ref,gu_ref,gd_ref,gb_ref,hid_ref,pre_ref):
    rows=x_ref.shape[0]; step=256
    first=pl.program_id(0)==0
    @pl.when(first)
    def _():
        down_ref[...]=jnp.zeros_like(down_ref)
        back_ref[...]=jnp.zeros_like(back_ref)
    up=up_ref[0]; dn=dn_ref[0]; bias=b_ref[0]
    def ahead(r):
        at=slice(r*step,(r+1)*step)
        return prod(x_ref[at,:],up,NN),prod(g_ref[at,:],dn,NT)
    count=rows//step
    nxt=ahead(0)
    total=None
    for r in range(count):
        at=slice(r*step,(r+1)*step)
        pre,gh=nxt
        if r+1<count: nxt=ahead(r+1)
        hidden,slope=gelu_parts(pre+bias)
        hidden=hidden.astype(jnp.bfloat16)
        hid_ref[at,:]=hidden
        gp=(gh.astype(jnp.bfloat16).astype(jnp.float32)*slope).astype(jnp.bfloat16)
        pre_ref[at,:]=gp
        s=jnp.sum(gp.astype(jnp.float32),axis=0,keepdims=True)
        total=s if total is None else total+s
        down_ref[at,:]+=prod(hidden,dn,NN)
        back_ref[at,:]+=prod(gp,up,NT)
    gb_ref[0]=total
    gu_ref[0]=prod(x_ref[...],pre_ref[...],COLS).astype(gu_ref.dtype)
    gd_ref[0]=prod(hid_ref[...],g_ref[...],COLS).astype(gd_ref.dtype)

def feed_forward(x,g,col,row,bias):
    T,D=x.shape; H=col.shape[2]
    f32=jnp.float32; bf=jnp.bfloat16
    once=pl.BlockSpec((T,D),lambda s:(0,0),pipeline_mode=pl.Buffered(1))
    whole=pl.BlockSpec((T,D),lambda s:(0,0))
    return pl.pallas_call(feed_kernel,grid=(4,),
        out_shape=(jax.ShapeDtypeStruct((T,D),f32),jax.ShapeDtypeStruct((T,D),f32),jax.ShapeDtypeStruct((4,D,H),bf),
                   jax.ShapeDtypeStruct((4,H,D),bf),jax.ShapeDtypeStruct((4,1,H),f32)),
        in_specs=[once,once,pl.BlockSpec((1,D,H),lambda s:(s+6,0,0)),pl.BlockSpec((1,H,D),lambda s:(s+2,0,0)),pl.BlockSpec((1,1,H),lambda s:(s,0,0))],
        out_specs=[whole,whole,pl.BlockSpec((1,D,H),lambda s:(s,0,0)),pl.BlockSpec((1,H,D),lambda s:(s,0,0)),pl.BlockSpec((1,1,H),lambda s:(s,0,0))],
        scratch_shapes=[pltpu.VMEM((T,H),bf),pltpu.VMEM((T,H),bf)],
        compiler_params=pltpu.CompilerParams(vmem_limit_bytes=56*1024*1024),
        cost_estimate=pl.CostEstimate(flops=6*2*4*T*D*H,bytes_accessed=4*T*D+8*T*D+16*D*H*2,transcendentals=8*T*H),
    )(x,g,col,row,bias[4:8,None,:])

MESH=pl.DeviceIdType.MESH

def share_kernel(parts, cores, sent_ref, square_ref, vec_ref, came_ref, norm_ref, squares, own_sem, send_sem, recv_sem, tile_send, tile_recv):
    here=lax.axis_index("dp"); core=lax.axis_index("mp")
    me=here*cores+core
    everyone=parts*cores
    barrier=pltpu.get_barrier_semaphore()
    def other(k):
        at=lax.rem(me+k,everyone)
        return (lax.div(at,cores),lax.rem(at,cores))
    def greet(k,_):
        pl.semaphore_signal(barrier,inc=1,device_id=other(k),device_id_type=MESH)
        return 0
    lax.fori_loop(1,everyone,greet,0)
    squares[me]=square_ref[...]
    own=pltpu.make_async_copy(sent_ref.at[here],came_ref.at[here],own_sem)
    own.start()
    pl.semaphore_wait(barrier,everyone-1)
    def block(k):
        to=lax.rem(here+k,parts)
        return pltpu.make_async_remote_copy(src_ref=sent_ref.at[to],dst_ref=came_ref.at[here],send_sem=send_sem.at[to],recv_sem=recv_sem.at[here],
            device_id=(to,core),device_id_type=MESH)
    def tile(k):
        return pltpu.make_async_remote_copy(src_ref=squares.at[me],dst_ref=squares.at[me],send_sem=tile_send.at[k],recv_sem=tile_recv.at[me],
            device_id=other(k),device_id_type=MESH)
    def start_tile(k,_):
        tile(k).start(); return 0
    lax.fori_loop(1,everyone,start_tile,0)
    def start_block(k,_):
        block(k).start(); return 0
    lax.fori_loop(1,parts,start_block,0)
    def wait_tile(k,_):
        tile(k).wait_send()
        at=lax.rem(me+k,everyone)
        pltpu.make_async_copy(squares.at[at],squares.at[at],tile_recv.at[at]).wait()
        return 0
    lax.fori_loop(1,everyone,wait_tile,0)
    vec=vec_ref[...]
    total=jnp.sum(squares[...],keepdims=True).reshape(1,1)+jnp.sum(vec*vec,keepdims=True).reshape(1,1)
    norm_ref[...]=jnp.broadcast_to(jnp.sqrt(total),norm_ref.shape)
    def wait_block(k,_):
        block(k).wait_send()
        at=lax.rem(here+k,parts)
        pltpu.make_async_copy(came_ref.at[at],came_ref.at[at],recv_sem.at[at]).wait()
        return 0
    lax.fori_loop(1,parts,wait_block,0)
    own.wait()

def share(sent,square,vectors,cores):
    parts,rows,width=sent.shape
    tile=jnp.zeros((8,128),jnp.float32).at[0,0].set(square)
    vm=pl.BlockSpec(memory_space=pltpu.VMEM)
    came,norm=pl.pallas_call(partial(share_kernel,parts,cores),
        out_shape=(jax.ShapeDtypeStruct(sent.shape,sent.dtype),jax.ShapeDtypeStruct((8,128),jnp.float32)),
        in_specs=[vm,vm,vm],out_specs=[vm,vm],
        scratch_shapes=[pltpu.VMEM((parts*cores,8,128),jnp.float32),pltpu.SemaphoreType.DMA,
            pltpu.SemaphoreType.DMA((parts,)),pltpu.SemaphoreType.DMA((parts,)),
            pltpu.SemaphoreType.DMA((parts*cores,)),pltpu.SemaphoreType.DMA((parts*cores,))],
        compiler_params=pltpu.CompilerParams(collective_id=0,has_side_effects=True,vmem_limit_bytes=16*1024*1024),
    )(sent,tile,vectors)
    return came,norm[0,0]

BS=256; STEP=10
weight_rate=0.03; weight_decay=0.01
HI=lax.Precision.HIGHEST
def hdot(a,b,dims,precision=HI):
    return lax.dot_general(a,b,(dims,((),())),precision=precision,preferred_element_type=jnp.float32)
DIM_NN=((1,),(0,)); DIM_NT=((1,),(1,)); DIM_TN=((0,),(0,))

def parts2(a):
    top=a.astype(jnp.bfloat16)
    return top,(a-top.astype(jnp.float32)).astype(jnp.bfloat16)

def dot1(a,b,dims):
    return lax.dot_general(a,b,(dims,((),())),preferred_element_type=jnp.float32)

def dot3(a,b,dims):
    a0,a1=a; b0,b1=b
    return dot1(a0,b0,dims)+(dot1(a0,b1,dims)+dot1(a1,b0,dims))

def soap_kernel(clip_ref,g_ref,first,second,master,left,right,ql_ref,qr_ref,
                first_o,second_o,master_o,copy_o,left_o,right_o,al_o,ar_o,ml_o,mr_o):
    clip=clip_ref[0,0]
    g=g_ref[0]
    ql=ql_ref[0]; qr=qr_ref[0]
    scale=0.05*clip*clip
    left_new=0.95*left[0]+scale*dot1(g,g,DIM_NT)
    left_o[0]=left_new
    al=hdot(left_new,ql,DIM_NN); al_o[0]=al
    ml_o[0]=hdot(al,al,DIM_TN)
    right_new=0.95*right[0]+scale*dot1(g,g,DIM_TN)
    right_o[0]=right_new
    ar=hdot(right_new,qr,DIM_NN); ar_o[0]=ar
    mr_o[0]=hdot(ar,ar,DIM_TN)
    ql2=parts2(ql); qr2=parts2(qr)
    half=dot1(ql2[0],g,DIM_TN)+dot1(ql2[1],g,DIM_TN)
    rot=clip*dot3(parts2(half),qr2,DIM_NN)
    f=0.9*first[0]+0.1*rot; first_o[0]=f
    s=0.99*second[0]+0.01*rot*rot; second_o[0]=s
    ratio=f/(1.0-0.9**STEP)/(jnp.sqrt(s/(1.0-0.99**STEP))+1e-8)
    stepped=dot3(parts2(dot3(ql2,parts2(ratio),DIM_NN)),qr2,DIM_NT)
    m=master[0]-weight_rate*(stepped+weight_decay*master[0])
    master_o[0]=m; copy_o[0]=m.astype(jnp.bfloat16)

def soap_stage(clip,g,first,second,master,left,right,ql,qr):
    n=g.shape[0]
    spec=pl.BlockSpec((1,BS,BS),lambda i:(i,0,0))
    f32=jax.ShapeDtypeStruct((n,BS,BS),jnp.float32)
    return pl.pallas_call(soap_kernel,grid=(n,),
        out_shape=(f32,f32,f32,jax.ShapeDtypeStruct((n,BS,BS),jnp.bfloat16),f32,f32,f32,f32,f32,f32),
        in_specs=[pl.BlockSpec(memory_space=pltpu.SMEM)]+[spec]*8,
        out_specs=[spec]*10,
        compiler_params=pltpu.CompilerParams(vmem_limit_bytes=48*1024*1024),
    )(clip.reshape(1,1),g,first,second,master,left,right,ql,qr)

PW=64
def chol_kernel(al_ref,ar_ref,ml_ref,mr_ref,ql_o,qr_o,work,tile,pivot):
    n=al_ref.shape[0]; pairs=n
    def load(m,_):
        work[m]=ml_ref[m]; work[n+m]=mr_ref[m]
        return 0
    lax.fori_loop(0,n,load,0)
    lane=lax.broadcasted_iota(jnp.int32,(1,2*PW),1)
    base=lane//PW*PW
    bigcol=lax.broadcasted_iota(jnp.int32,(PW,BS),1)
    bigrow=lax.broadcasted_iota(jnp.int32,(PW,BS),0)
    lower=lax.broadcasted_iota(jnp.int32,(PW,2*PW),1)%PW<=lax.broadcasted_iota(jnp.int32,(PW,2*PW),0)
    for p in range(BS//PW):
        lo=p*PW; at=slice(lo,lo+PW)
        for j in range(pairs):
            tile[j]=jnp.concatenate([work[2*j,at,at],work[2*j+1,at,at]],axis=1)
        for quarter in range(4):
            top=quarter*PW//4; height=PW-top
            rows=lax.broadcasted_iota(jnp.int32,(height,2*PW),0)+top
            def step(k,_):
                here=lane-base==k
                below=rows>k
                fill=jnp.where(rows==k,1.0,0.0)
                t=tile[:,top:,:]
                r=tile[:,pl.ds(k,1),:]
                flat=pairs*height
                c=jnp.take_along_axis(t.reshape(flat,2*PW),jnp.broadcast_to(base+k,(flat,2*PW)),axis=1).reshape(pairs,height,2*PW)
                wide_r=jnp.broadcast_to(r[0],(8,2*PW)) if pairs==1 else r.reshape(pairs,2*PW)
                d=jnp.take_along_axis(wide_r,jnp.broadcast_to(base+k,wide_r.shape),axis=1)[:pairs].reshape(pairs,1,2*PW)
                r=jnp.where(here[None],1.0,r)*(1.0/d)
                pivot[:,pl.ds(k,1),:]=d
                tile[:,top:,:]=jnp.where(here[None],fill[None],t)-jnp.where(below[None],c,0.0)*r
                return 0
            lax.fori_loop(top,top+PW//4,step,0)
        for j in range(pairs):
            tile[j]=jnp.where(lower,tile[j]*lax.rsqrt(pivot[j]),0.0)
        inside=(bigcol>=lo)&(bigcol<lo+PW)
        eye=jnp.where(bigcol-lo==bigrow,1.0,0.0)
        def apply(j,_):
            both=tile[j]
            for s in range(2):
                m=2*j+s
                r=hdot(both[:,s*PW:(s+1)*PW],jnp.where(inside,eye,work[m,at,:]),DIM_NN)
                work[m,at,:]=r
                if p<BS//PW-1:
                    rest=jnp.where(inside[0:1],0.0,work[m,lo+PW:,:])
                    work[m,lo+PW:,:]=rest-hdot(r[:,lo+PW:],r,DIM_TN)
            return 0
        lax.fori_loop(0,pairs,apply,0)
    keep=lax.broadcasted_iota(jnp.int32,(BS,BS),1)<=lax.broadcasted_iota(jnp.int32,(BS,BS),0)
    def final(m,_):
        ql_o[m]=hdot(al_ref[m],jnp.where(keep,work[m],0.0),DIM_NT)
        qr_o[m]=hdot(ar_ref[m],jnp.where(keep,work[n+m],0.0),DIM_NT)
        return 0
    lax.fori_loop(0,n,final,0)

def chol_stage(al,ar,ml,mr):
    n=al.shape[0]
    f32=jax.ShapeDtypeStruct((n,BS,BS),jnp.float32)
    vm=pl.BlockSpec(memory_space=pltpu.VMEM)
    return pl.pallas_call(chol_kernel,out_shape=(f32,f32),in_specs=[vm]*4,out_specs=[vm]*2,
        scratch_shapes=[pltpu.VMEM((2*n,BS,BS),jnp.float32),pltpu.VMEM((n,PW,2*PW),jnp.float32),pltpu.VMEM((n,PW,2*PW),jnp.float32)],
        compiler_params=pltpu.CompilerParams(vmem_limit_bytes=56*1024*1024))(al,ar,ml,mr)

def soap(clip,g,first,second,master,left,right,ql,qr):
    f,s,m,c,l,r,al,ar,ml,mr=soap_stage(clip,g,first,second,master,left,right,ql,qr)
    lr,rr=chol_stage(al,ar,ml,mr)
    return f,s,m,c,l,r,lr,rr


LEN = 1024
shared_rate = 0.6
split_rate = 0.2
clip_limit = 1.0
SWAP = [(0, 1), (1, 0)]


def adam_step(gradient, first_state, second_state, values, step_rate):
    first_new = 0.9 * first_state + 0.1 * gradient
    second_new = 0.99 * second_state + 0.01 * gradient * gradient
    ratio = first_new / (1.0 - 0.9**STEP) / (jnp.sqrt(second_new / (1.0 - 0.99**STEP)) + 1e-08)
    return (first_new, second_new, values - step_rate * ratio)


def norm_forward(values, gain, shift):
    centered = values - jnp.mean(values, axis=-1, keepdims=True)
    inverse = lax.rsqrt(jnp.mean(centered * centered, axis=-1, keepdims=True) + 1e-05)
    hat = centered * inverse
    return (hat * gain + shift).astype(jnp.bfloat16), (values, inverse)


def norm_back(saved, gain, grad):
    values, inverse = saved
    hat = (values - jnp.mean(values, axis=-1, keepdims=True)) * inverse
    inner = grad * gain
    back = inverse * (
        inner
        - jnp.mean(inner, axis=-1, keepdims=True)
        - hat * jnp.mean(inner * hat, axis=-1, keepdims=True)
    )
    return back, jnp.sum(grad * hat, axis=0), jnp.sum(grad, axis=0)


def dot32(a, b):
    return jnp.dot(a, b, preferred_element_type=jnp.float32)


def low(a):
    return a.astype(jnp.bfloat16)


def wide(a):
    return a.astype(jnp.float32)


def exchange(array):
    return lax.ppermute(array, "mp", SWAP)


def to_parts(array, parts):
    stacked, height, width = array.shape
    return array.reshape(stacked * height // BS, parts, BS // parts, width)


def tie(*arrays):
    return lax.optimization_barrier(arrays)


class Staged:
    def __init__(self, array, first_bits):
        self.array = array
        parts = array.shape[1]
        bits = parts.bit_length() - 1
        self.parts = parts
        self.array = array.reshape((array.shape[0],) + (2,) * bits + array.shape[2:])
        self.left = list(range(bits - 1, -1, -1))
        self.order = [b for b in first_bits if b < bits] + [b for b in range(bits) if b not in first_bits]
        self.got = None

    def send(self):
        if not self.order:
            return
        b = self.order.pop(0)
        axis = 1 + self.left.index(b)
        self.left.remove(b)
        mine = (lax.axis_index("dp") >> b) & 1
        self.keep = lax.dynamic_index_in_dim(self.array, mine, axis, keepdims=False)
        give = lax.dynamic_index_in_dim(self.array, 1 - mine, axis, keepdims=False)
        self.got = lax.ppermute(give, "dp", [(i, i ^ (1 << b)) for i in range(self.parts)])

    def take(self):
        if self.got is not None:
            self.array = low(wide(self.keep) + wide(self.got))
            self.got = None

    def finish(self):
        self.take()
        while self.order:
            self.send()
            self.take()
        return self.array


def checkpoint(anchor, *sums):
    waiting = [s for s in sums if s.got is not None]
    anchor, *got = tie(anchor, *[s.got for s in waiting])
    for s, g in zip(waiting, got):
        s.got = g
        s.take()
        s.send()
    return anchor


def all_sum(array, parts):
    array = array + lax.ppermute(array, "mp", SWAP)
    for b in range(parts.bit_length() - 1):
        array = array + lax.ppermute(array, "dp", [(i, i ^ (1 << b)) for i in range(parts)])
    return array


def slot_order(block_slot):
    numbers = jnp.arange(block_slot.shape[0], dtype=jnp.int32)
    return jnp.sum(jnp.where(block_slot[None, :] == numbers[:, None], numbers[None, :], 0), axis=1)


def on_device(
    parts,
    mp_size,
    tokens,
    memory,
    cotangent,
    bucket,
    target_lengths,
    memory_lengths,
    block_slot,
    col_weights,
    row_weights,
    shared_vectors,
    split_vectors,
    shared_first,
    shared_second,
    split_first,
    split_second,
    slot_first,
    slot_second,
    slot_master,
    slot_left,
    slot_right,
    left_basis,
    right_basis,
):
    core = lax.axis_index("mp")
    half = col_weights.shape[2]
    shared = shared_vectors
    own_bucket = lax.dynamic_index_in_dim(bucket, core, 0, keepdims=False)
    own_target = lax.dynamic_index_in_dim(target_lengths, core, 0, keepdims=False)
    own_memory = lax.dynamic_index_in_dim(memory_lengths, core, 0, keepdims=False)
    rows = tokens.shape[0]
    self_at = self_plan(own_bucket, rows)
    cross_at = cross_plan(own_bucket, own_memory, rows, memory.shape[0])
    places = jnp.arange(rows, dtype=jnp.int32)
    size = rows // jnp.left_shift(jnp.int32(1), own_bucket)
    segment = places // size
    live = jnp.any(
        (segment[:, None] == jnp.arange(4, dtype=jnp.int32)[None, :])
        & ((places - segment * size)[:, None] < own_target[None, :]),
        axis=1,
    )
    cols = (col_weights, exchange(col_weights))
    rws = (row_weights, exchange(row_weights))
    splits = (split_vectors, exchange(split_vectors))
    both = (0, 1)

    tokens_wide = wide(tokens)
    normed1, saved1 = norm_forward(tokens_wide, shared[0], shared[1])
    query, key, value, mem_key, mem_value, self_out, self_log = ([], [], [], [], [], [], [])
    for h in both:
        query.append(low(dot32(normed1, cols[h][0]) + splits[h][0]))
        key.append(low(dot32(normed1, cols[h][1])))
        value.append(low(dot32(normed1, cols[h][2]) + splits[h][1]))
        mem_key.append(low(dot32(memory, cols[h][4])))
        mem_value.append(low(dot32(memory, cols[h][5]) + splits[h][3]))
        out, log = attention(query[h], key[h], value[h], self_at, True)
        self_out.append(out)
        self_log.append(log)
    resid1 = tokens_wide + (dot32(self_out[0], rws[0][0]) + dot32(self_out[1], rws[1][0])) + shared[6]
    normed2, saved2 = norm_forward(resid1, shared[2], shared[3])
    cross_query, cross_out, cross_log = ([], [], [])
    for h in both:
        cross_query.append(low(dot32(normed2, cols[h][3]) + splits[h][2]))
        out, log = attention(cross_query[h], mem_key[h], mem_value[h], cross_at, False)
        cross_out.append(out)
        cross_log.append(log)
    resid2 = resid1 + (dot32(cross_out[0], rws[0][1]) + dot32(cross_out[1], rws[1][1])) + shared[7]
    normed3, saved3 = norm_forward(resid2, shared[4], shared[5])
    grad_out = jnp.where(live[:, None], cotangent, jnp.zeros_like(cotangent))
    down_peer, back_peer, up_grad, down_grad, up_bias_peer = feed_forward(normed3, grad_out, cols[1], rws[1], splits[1])
    up_peer = exchange(up_grad)
    down_grad_peer = exchange(down_grad)
    down_own, back_own, up_grad, down_grad, up_bias_own = feed_forward(normed3, grad_out, cols[0], rws[0], splits[0])
    output = low(resid2 + (down_own + down_peer) + shared[8])
    up_bias = [up_bias_own[:, 0], up_bias_peer[:, 0]]
    back_own, up_peer, down_grad_peer = tie(back_own, up_peer, down_grad_peer)
    down_sum = Staged(to_parts(low(wide(down_grad) + wide(down_grad_peer)), parts), (1, 0))
    up_sum = Staged(to_parts(low(wide(up_grad) + wide(up_peer)), parts), (0, 1))
    down_sum.send()
    up_sum.send()
    grad_normed3 = back_own + back_peer
    back3, gain3, shift3 = norm_back(saved3, shared[4], grad_normed3)
    grad_resid2 = wide(grad_out) + back3
    grad2 = low(grad_resid2)

    def outer(x, g):
        return jnp.einsum("td,te->de", x, g, preferred_element_type=jnp.float32)

    def inner(g, w):
        return jnp.einsum("te,de->td", g, w, preferred_element_type=jnp.float32)

    cross_row = [outer(cross_out[h], grad2) for h in both]
    cross_row_peer = exchange(low(cross_row[1]))
    grad_cq, grad_mk, grad_mv = ([], [], [])
    for h in both:
        grad = low(jnp.einsum("td,fd->tf", grad2, rws[h][1], preferred_element_type=jnp.float32))
        if h == 1:
            grad = checkpoint(grad, down_sum, up_sum)
        a, b, c = attention_back(
            cross_query[h], mem_key[h], mem_value[h], grad, cross_out[h], cross_log[h], cross_at, False
        )
        grad_cq.append(a)
        grad_mk.append(b)
        grad_mv.append(c)
    grad_cq[1] = checkpoint(grad_cq[1], down_sum, up_sum)
    cross_peer = exchange(
        low(jnp.stack([outer(normed2, grad_cq[1]), outer(memory, grad_mk[1]), outer(memory, grad_mv[1])]))
    )
    cross_own = jnp.stack([outer(normed2, grad_cq[0]), outer(memory, grad_mk[0]), outer(memory, grad_mv[0])])
    grad_cq[0], cross_peer, cross_row_peer = tie(grad_cq[0], cross_peer, cross_row_peer)
    cross_sum = Staged(to_parts(low(cross_own + wide(cross_peer)), parts), (0, 1))
    row1_sum = Staged(to_parts(low(cross_row[0] + wide(cross_row_peer))[None], parts), (1, 0))
    cross_sum.send()
    row1_sum.send()
    grad_normed2 = sum(inner(grad_cq[h], cols[h][3]) for h in both)
    back2, gain2, shift2 = norm_back(saved2, shared[2], grad_normed2)
    grad_resid1 = grad_resid2 + back2
    grad1 = low(grad_resid1)
    grad1 = checkpoint(grad1, down_sum, up_sum)
    self_row = [outer(self_out[h], grad1) for h in both]
    self_row_peer = exchange(low(self_row[1]))
    grad_q, grad_k, grad_v = ([], [], [])
    for h in both:
        grad = low(jnp.einsum("td,fd->tf", grad1, rws[h][0], preferred_element_type=jnp.float32))
        if h == 1:
            grad = checkpoint(grad, up_sum, cross_sum, row1_sum)
        a, b, c = attention_back(query[h], key[h], value[h], grad, self_out[h], self_log[h], self_at, True)
        grad_q.append(a)
        grad_k.append(b)
        grad_v.append(c)
    row0_sum = Staged(to_parts(low(self_row[0] + wide(self_row_peer))[None], parts), (1, 0))
    row0_sum.send()
    grad_q[1] = checkpoint(grad_q[1], up_sum, cross_sum, row1_sum)
    self_peer = exchange(
        low(jnp.stack([outer(normed1, grad_q[1]), outer(normed1, grad_k[1]), outer(normed1, grad_v[1])]))
    )
    self_own = jnp.stack([outer(normed1, grad_q[0]), outer(normed1, grad_k[0]), outer(normed1, grad_v[0])])
    grad_q[0], self_peer = tie(grad_q[0], self_peer)
    self_all = to_parts(low(self_own + wide(self_peer)), parts)
    middle = self_all.shape[0] // 2
    self_sums = [Staged(self_all[:middle], (0, 1)), Staged(self_all[middle:], (1, 0))]
    for a in self_sums:
        a.send()
    grad_normed1 = sum(
        inner(grad_q[h], cols[h][0]) + inner(grad_k[h], cols[h][1]) + inner(grad_v[h], cols[h][2]) for h in both
    )
    back1, gain1, shift1 = norm_back(saved1, shared[0], grad_normed1)
    input_grad = grad_resid1 + back1
    memory_grad = sum(inner(grad_mk[h], cols[h][4]) + inner(grad_mv[h], cols[h][5]) for h in both)
    self_piece = jnp.concatenate([a.finish() for a in self_sums], axis=0)
    cross_piece = cross_sum.finish()
    up_piece = up_sum.finish()
    down_piece = down_sum.finish()
    row_piece = jnp.concatenate([row0_sum.finish(), row1_sum.finish()], axis=0)

    def column_sum(a):
        return jnp.sum(wide(a), axis=0)

    shared_grad = jnp.stack(
        [
            gain1,
            shift1,
            gain2,
            shift2,
            gain3,
            shift3,
            jnp.sum(grad_resid1, axis=0),
            jnp.sum(grad_resid2, axis=0),
            column_sum(grad_out),
        ]
    )
    split_grad = [
        jnp.concatenate(
            [
                jnp.stack([column_sum(grad_q[h]), column_sum(grad_v[h]), column_sum(grad_cq[h]), column_sum(grad_mv[h])]),
                up_bias[h],
            ]
        )
        for h in both
    ]
    first = jnp.where(core == 0, split_grad[0], split_grad[1])
    second = jnp.where(core == 0, split_grad[1], split_grad[0])
    vectors = jnp.concatenate([shared_grad, jnp.concatenate([first, second], axis=1)], axis=0)
    vectors = all_sum(vectors, parts)
    shared_sum = vectors[:9]
    split_sum = vectors[9:]

    def blocks(piece):
        m, rows_in, width = piece.shape
        return (
            piece.reshape(m, rows_in, width // BS, BS).transpose(0, 2, 1, 3).reshape(-1, rows_in, BS)
        )

    pieces = jnp.concatenate(
        [
            blocks(self_piece),
            blocks(cross_piece),
            blocks(up_piece),
            blocks(row_piece),
            blocks(down_piece),
        ],
        axis=0,
    )
    square = jnp.sum(wide(pieces) * wide(pieces))
    owned = slot_first.shape[0]
    part_rows = BS // parts
    sent = jnp.take(pieces, slot_order(block_slot), axis=0)
    if part_rows % 16 == 0:
        came, grad_norm = share(sent.reshape(parts, owned * part_rows, BS), square, vectors, mp_size)
    else:
        came = lax.all_to_all(sent.reshape(parts, owned, part_rows, BS), "dp", 0, 0, tiled=True)
        grad_norm = jnp.sqrt(all_sum(square.reshape(1, 1), parts)[0, 0] + jnp.sum(vectors * vectors))
    mine = came.reshape(parts, owned, part_rows, BS).transpose(1, 0, 2, 3).reshape(owned, BS, BS)
    clip = clip_limit / jnp.maximum(grad_norm, clip_limit)

    def flat(a):
        return a.reshape(owned, BS, BS)

    updated = soap(
        clip,
        mine,
        flat(slot_first),
        flat(slot_second),
        flat(slot_master),
        flat(slot_left),
        flat(slot_right),
        flat(left_basis),
        flat(right_basis),
    )
    first_moment, second_moment, master_weight, master_copy, left_stat, right_stat, left_rotation, right_rotation = (
        a.reshape(slot_first.shape) for a in updated
    )
    shared_mean, shared_square, shared_values = adam_step(
        shared_sum * clip, shared_first, shared_second, shared_vectors, shared_rate
    )
    split_own = lax.dynamic_slice_in_dim(split_sum, core * half, half, axis=1)
    split_mean, split_square, split_values = adam_step(
        split_own * clip, split_first, split_second, split_vectors, split_rate
    )
    return (
        output,
        input_grad,
        memory_grad,
        first_moment,
        second_moment,
        master_weight,
        master_copy,
        left_stat,
        right_stat,
        left_rotation,
        right_rotation,
        shared_mean,
        shared_square,
        shared_values,
        split_mean,
        split_square,
        split_values,
        grad_norm,
    )


def solution(mesh):
    rows = P(("dp", "mp"), None)
    slots = P("dp", "mp", None, None)
    split = P(None, "mp")
    placed = (
        (rows, rows, rows, P("dp"), P("dp", None), P("dp", None), P())
        + (P(None, None, "mp"), P(None, "mp", None), P(), split, P(), P(), split, split)
        + (slots,) * 7
    )
    return jax.shard_map(
        partial(on_device, mesh.shape["dp"], mesh.shape["mp"]),
        mesh=mesh,
        in_specs=placed,
        out_specs=(rows,) * 3 + (slots,) * 8 + (P(),) * 3 + (split,) * 3 + (P(),),
        check_vma=False,
    )
```

```python
from functools import partial

import jax
import jax.numpy as jnp
from jax import lax
from jax.experimental import pallas as pl
from jax.experimental.pallas import tpu as pltpu
from jax.sharding import PartitionSpec as P

HEAD_DIM=64; TQ=256
SCALE=HEAD_DIM**-0.5
EXPC=SCALE*1.4426950408889634
NEG=-1e30
NT=(((1,),(1,)),((),()))
NN=(((1,),(0,)),((),()))

def rows_of(i,n=1):
    if isinstance(i,int): return slice(i*TQ,(i+n)*TQ)
    return pl.ds(pl.multiple_of(i*TQ,TQ),n*TQ)

def head_cols(h):
    return slice(h*HEAD_DIM,(h+1)*HEAD_DIM)

def lanes_of(pair):
    return pl.ds(pl.multiple_of(pair*128,128),128)

def allowed(causal,limit,j):
    r=lax.broadcasted_iota(jnp.int32,(TQ,TQ),0)
    if causal: return r<=lax.broadcasted_iota(jnp.int32,(TQ,TQ),1)
    return r<limit-j*TQ

def each_case(causal,plan,tiles,pairs,emit):
    def over(n,body):
        def step(i,_):
            body(i)
            return 0
        lax.fori_loop(0,n,step,0)
    for b in range(3):
        count=1<<b; size=tiles>>b
        if b==0 and not causal:
            for n in (size,size//2):
                fits=plan[1]>TQ*size//2 if n==size else plan[1]<=TQ*size//2
                @pl.when((plan[0]==b)&fits)
                def _(n=n):
                    over(pairs,lambda pair: emit(pair,[(0,size,n,plan[1],n-size//2)]))
        else:
            @pl.when(plan[0]==b)
            def _(count=count,size=size):
                if count==1: over(pairs,lambda pair: emit(pair,[(0,size,size,None,size-1)]))
                else: over(pairs,lambda pair: over(count,lambda s: emit(pair,[(s*size,size,size,None if causal else plan[1+s],0)])))

def tile_items(causal,segments):
    out=[]
    for t0,qn,kn,limit,masked in segments:
        for i in range(qn):
            n=i+1 if causal else kn
            out.append((t0+i,t0,n,limit,n-1 if causal else masked))
    return out

def fwd_kernel(causal, tiles, plan, q_ref, k_ref, v_ref, o_ref, l_ref, vt_ref):
    pairs=q_ref.shape[1]//128
    def turn(pair,_):
        vt_ref[pair]=v_ref[:,lanes_of(pair)].astype(jnp.float32).T.astype(jnp.bfloat16)
        return 0
    lax.fori_loop(0,pairs,turn,0)
    def emit(pair,segments):
        lanes=lanes_of(pair)
        items=[(t,h) for t in tile_items(causal,segments) for h in range(2)]
        def scores(item):
            (i,k0,n,limit,masked),h=item
            q=q_ref[rows_of(i),lanes][:,head_cols(h)]
            parts=[]
            for j in range(n):
                s=lax.dot_general(k_ref[rows_of(k0+j),lanes][:,head_cols(h)],q,NT,preferred_element_type=jnp.float32)
                if j>=masked:
                    s=jnp.where(allowed(causal,limit,j),s,NEG)
                parts.append(s)
            return parts
        ahead=scores(items[0])
        held=None
        for c,((i,k0,n,limit,masked),h) in enumerate(items):
            parts=ahead
            if c+1<len(items): ahead=scores(items[c+1])
            top=parts[0].max(axis=0,keepdims=True)
            for s in parts[1:]: top=jnp.maximum(top,s.max(axis=0,keepdims=True))
            total=None; acc=None
            for j,s in enumerate(parts):
                p=jnp.exp2((s-top)*EXPC)
                t=p.sum(axis=0,keepdims=True)
                total=t if total is None else total+t
                a=lax.dot_general(vt_ref[pair,head_cols(h),rows_of(k0+j)],p.astype(jnp.bfloat16),NN,preferred_element_type=jnp.float32)
                acc=a if acc is None else acc+a
            acc=acc*(1.0/total)
            l_ref[pair,h:h+1,rows_of(i)]=top+jnp.log2(total)*(1.0/EXPC)
            if h==0: held=acc
            else: o_ref[rows_of(i),lanes]=jnp.concatenate([held,acc],axis=0).T.astype(o_ref.dtype)
    each_case(causal,plan,tiles,pairs,emit)

VM=pl.BlockSpec(memory_space=pltpu.VMEM)
SM=pl.BlockSpec(memory_space=pltpu.SMEM)

def attention(q,k,v,plan,causal):
    T,W=q.shape; M=k.shape[0]; pairs=W//128; tiles=T//TQ
    return pl.pallas_call(
        partial(fwd_kernel,causal,tiles),
        out_shape=(jax.ShapeDtypeStruct((T,W),jnp.bfloat16),jax.ShapeDtypeStruct((pairs,2,T),jnp.float32)),
        in_specs=[SM,VM,VM,VM],out_specs=[VM,VM],
        scratch_shapes=[pltpu.VMEM((pairs,128,M),jnp.bfloat16)],
        compiler_params=pltpu.CompilerParams(vmem_limit_bytes=32*1024*1024),
        cost_estimate=pl.CostEstimate(flops=4*T*M*W//2,bytes_accessed=8*T*W,transcendentals=T*M*W//128),
    )(plan,q,k,v)

def bwd_kernel(causal, tiles, plan, q_ref, k_ref, v_ref, g_ref, o_ref, l_ref, dq_ref, dk_ref, dv_ref, kt_ref, p_ref, s_ref, d_ref):
    pairs=q_ref.shape[1]//128
    ones=jnp.ones((8,HEAD_DIM),jnp.bfloat16)
    def turn(pair,_):
        lanes=lanes_of(pair)
        kt_ref[pair]=k_ref[:,lanes].astype(jnp.float32).T.astype(jnp.bfloat16)
        prod=g_ref[:,lanes].astype(jnp.float32)*o_ref[:,lanes].astype(jnp.float32)
        top=prod.astype(jnp.bfloat16)
        rest=(prod-top.astype(jnp.float32)).astype(jnp.bfloat16)
        for h in range(2):
            d_ref[pair,h]=(lax.dot_general(ones,top[:,head_cols(h)],NT,preferred_element_type=jnp.float32)
                +lax.dot_general(ones,rest[:,head_cols(h)],NT,preferred_element_type=jnp.float32))
        return 0
    lax.fori_loop(0,pairs,turn,0)
    def emit(pair,segments):
        lanes=lanes_of(pair)
        items=[(i,k0,j,n,limit,masked,h) for i,k0,n,limit,masked in tile_items(causal,segments) for j in range(n) for h in range(2)]
        def products(item):
            i,k0,j,n,limit,masked,h=item
            return (lax.dot_general(k_ref[rows_of(k0+j),lanes][:,head_cols(h)],q_ref[rows_of(i),lanes][:,head_cols(h)],NT,preferred_element_type=jnp.float32),
                    lax.dot_general(v_ref[rows_of(k0+j),lanes][:,head_cols(h)],g_ref[rows_of(i),lanes][:,head_cols(h)],NT,preferred_element_type=jnp.float32))
        ahead=products(items[0])
        acc=[None,None]
        for c,(i,k0,j,n,limit,masked,h) in enumerate(items):
            s,dp=ahead
            if c+1<len(items): ahead=products(items[c+1])
            p=jnp.exp2((s-l_ref[pair,h:h+1,rows_of(i)])*EXPC)
            if j>=masked: p=jnp.where(allowed(causal,limit,j),p,0.0)
            p_ref[h,rows_of(k0+j),rows_of(i)]=p.astype(jnp.bfloat16)
            ds=(p*(dp-d_ref[pair,h,0:1,rows_of(i)])).astype(jnp.bfloat16)
            s_ref[h,rows_of(k0+j),rows_of(i)]=ds
            a=lax.dot_general(kt_ref[pair,head_cols(h),rows_of(k0+j)],ds,NN,preferred_element_type=jnp.float32)
            acc[h]=a if j==0 else acc[h]+a
            if j==n-1 and h==1:
                dq_ref[rows_of(i),lanes]=(jnp.concatenate(acc,axis=0)*SCALE).T.astype(dq_ref.dtype)
        for t0,qn,kn,limit,masked in segments:
            for j in range(qn):
                if j>=kn:
                    dk_ref[rows_of(t0+j),lanes]=jnp.zeros((TQ,128),dk_ref.dtype)
                    dv_ref[rows_of(t0+j),lanes]=jnp.zeros((TQ,128),dv_ref.dtype)
                    continue
                cols=rows_of(t0+j,qn-j) if causal else rows_of(t0,qn)
                both=[]
                for h in range(2):
                    both.append((lax.dot_general(p_ref[h,rows_of(t0+j),cols],g_ref[cols,lanes][:,head_cols(h)],NN,preferred_element_type=jnp.float32),
                                 lax.dot_general(s_ref[h,rows_of(t0+j),cols],q_ref[cols,lanes][:,head_cols(h)],NN,preferred_element_type=jnp.float32)))
                dv_ref[rows_of(t0+j),lanes]=jnp.concatenate([a for a,b in both],axis=1).astype(dv_ref.dtype)
                dk_ref[rows_of(t0+j),lanes]=(jnp.concatenate([b for a,b in both],axis=1)*SCALE).astype(dk_ref.dtype)
    each_case(causal,plan,tiles,pairs,emit)

def attention_back(q,k,v,g,out,logs,plan,causal):
    T,W=q.shape; M=k.shape[0]; pairs=W//128; tiles=T//TQ
    narrow=jax.ShapeDtypeStruct((T,W),jnp.bfloat16)
    return pl.pallas_call(
        partial(bwd_kernel,causal,tiles),
        out_shape=(narrow,jax.ShapeDtypeStruct((M,W),jnp.bfloat16),jax.ShapeDtypeStruct((M,W),jnp.bfloat16)),
        in_specs=[SM]+[VM]*6,out_specs=[VM]*3,
        scratch_shapes=[pltpu.VMEM((pairs,128,M),jnp.bfloat16),pltpu.VMEM((2,M,T),jnp.bfloat16),pltpu.VMEM((2,M,T),jnp.bfloat16),pltpu.VMEM((pairs,2,8,T),jnp.float32)],
        compiler_params=pltpu.CompilerParams(vmem_limit_bytes=40*1024*1024),
        cost_estimate=pl.CostEstimate(flops=10*T*M*W//2,bytes_accessed=14*T*W,transcendentals=T*M*W//128),
    )(plan,q,k,v,g,out,logs)

def self_plan(bucket,T):
    return bucket.reshape(1)

def cross_plan(bucket,lengths,T,M):
    return jnp.concatenate([bucket.reshape(1),lengths])

CHUNK=256
JOIN=pltpu.CompilerParams(vmem_limit_bytes=48*1024*1024)

def hat_of(values):
    centered=values-jnp.mean(values,axis=-1,keepdims=True)
    inverse=lax.rsqrt(jnp.mean(centered*centered,axis=-1,keepdims=True)+1e-05)
    return centered*inverse,inverse

def join_kernel(v_ref,a_ref,b_ref,wa_ref,wb_ref,r_ref,sum_ref,norm_ref):
    product=(lax.dot_general(a_ref[...],wa_ref[0],NN,preferred_element_type=jnp.float32)
        +lax.dot_general(b_ref[...],wb_ref[0],NN,preferred_element_type=jnp.float32))
    values=v_ref[...].astype(jnp.float32)+product+r_ref[0:1,:]
    sum_ref[...]=values
    hat,_=hat_of(values)
    norm_ref[...]=(hat*r_ref[1:2,:]+r_ref[2:3,:]).astype(norm_ref.dtype)

def join_forward(values,halves,rows,index,shift,gain,bias):
    T,D=values.shape; H=halves[0].shape[1]
    part=pl.BlockSpec((CHUNK,D),lambda i:(i,0)); narrow=pl.BlockSpec((CHUNK,H),lambda i:(i,0))
    weight=pl.BlockSpec((1,H,D),lambda i:(index,0,0))
    return pl.pallas_call(join_kernel,grid=(T//CHUNK,),
        out_shape=(jax.ShapeDtypeStruct((T,D),jnp.float32),jax.ShapeDtypeStruct((T,D),jnp.bfloat16)),
        in_specs=[part,narrow,narrow,weight,weight,pl.BlockSpec((3,D),lambda i:(0,0))],out_specs=[part,part],
        compiler_params=JOIN,cost_estimate=pl.CostEstimate(flops=4*T*D*H,bytes_accessed=10*T*D+4*T*H+4*H*D,transcendentals=T),
    )(values,*halves,*rows,jnp.stack([shift,gain,bias]))

def back_kernel(terms,extras,norm,low_too,*refs):
    refs=list(refs)
    take=lambda n: [refs.pop(0) for _ in range(n)]
    gs=take(2*terms); ws=take(2 if terms else 0); ex=take(extras)
    acc=None
    for h in range(2 if terms else 0):
        for s in range(terms):
            a=lax.dot_general(gs[h*terms+s][...],ws[h][s],NT,preferred_element_type=jnp.float32)
            acc=a if acc is None else acc+a
    for e in ex:
        acc=e[...] if acc is None else acc+e[...]
    if not norm:
        refs.pop(0)[...]=acc
        return
    v_ref,g_ref,gain_ref=take(3)
    hat,inverse=hat_of(v_ref[...].astype(jnp.float32))
    inner=acc*gain_ref[...]
    back=inverse*(inner-jnp.mean(inner,axis=-1,keepdims=True)-hat*jnp.mean(inner*hat,axis=-1,keepdims=True))
    new=g_ref[...].astype(jnp.float32)+back
    refs.pop(0)[...]=new
    if low_too: refs.pop(0)[...]=new.astype(jnp.bfloat16)
    sums=refs.pop(0)
    @pl.when(pl.program_id(0)==0)
    def _(): sums[...]=jnp.zeros_like(sums)
    sums[0:1,:]+=jnp.sum(acc*hat,axis=0,keepdims=True)
    sums[1:2,:]+=jnp.sum(acc,axis=0,keepdims=True)
    sums[2:3,:]+=jnp.sum(new,axis=0,keepdims=True)

def join_back(gs,cols,index,extras=(),norm=None,low_too=False):
    terms=len(gs[0]) if gs else 0
    T,D=extras[0].shape if extras else (gs[0][0].shape[0],cols[0].shape[1])
    part=pl.BlockSpec((CHUNK,D),lambda i:(i,0))
    args=[]; specs=[]
    if terms:
        H=gs[0][0].shape[1]
        for h in range(2):
            for g in gs[h]: args.append(g); specs.append(pl.BlockSpec((CHUNK,H),lambda i:(i,0)))
        for w in cols: args.append(w); specs.append(pl.BlockSpec((terms,D,H),lambda i:(index,0,0),pipeline_mode=pl.Buffered(1)))
    for e in extras: args.append(e); specs.append(part)
    full=jax.ShapeDtypeStruct((T,D),jnp.float32)
    outs=[full]; out_specs=[part]
    if norm:
        values,grad,gain=norm
        args+=[values,grad,gain[None]]; specs+=[part,part,pl.BlockSpec((1,D),lambda i:(0,0))]
        if low_too: outs.append(jax.ShapeDtypeStruct((T,D),jnp.bfloat16)); out_specs.append(part)
        outs.append(jax.ShapeDtypeStruct((8,D),jnp.float32)); out_specs.append(pl.BlockSpec((8,D),lambda i:(0,0)))
    return pl.pallas_call(partial(back_kernel,terms,len(extras),norm is not None,low_too),grid=(T//CHUNK,),
        out_shape=tuple(outs),in_specs=specs,out_specs=tuple(out_specs),compiler_params=JOIN,
        cost_estimate=pl.CostEstimate(flops=4*terms*T*D*512+T*D*20,bytes_accessed=20*T*D+4*terms*D*512,transcendentals=T),
    )(*args)

COLS=(((0,),(0,)),((),()))
def prod(a,b,dims):
    return lax.dot_general(a,b,dims,preferred_element_type=jnp.float32)

def gelu_parts(v):
    t=1.0/(1.0+(0.3275911*0.7071067811865476)*jnp.abs(v))
    e=jnp.exp2(v*v*(-0.5*1.4426950408889634))
    poly=t*(0.5*0.254829592+t*(0.5*-0.284496736+t*(0.5*1.421413741+t*(0.5*-1.453152027+t*(0.5*1.061405429)))))
    tail=poly*e
    phi=jnp.where(v>=0.0,1.0-tail,tail)
    return v*phi,phi+v*e*0.3989422804014327

def feed_kernel(x_ref,g_ref,up_ref,dn_ref,b_ref,down_ref,back_ref,gu_ref,gd_ref,gb_ref,hid_ref,pre_ref):
    rows=x_ref.shape[0]; step=256
    first=pl.program_id(0)==0
    @pl.when(first)
    def _():
        down_ref[...]=jnp.zeros_like(down_ref)
        back_ref[...]=jnp.zeros_like(back_ref)
    up=up_ref[0]; dn=dn_ref[0]; bias=b_ref[0]
    def ahead(r):
        at=slice(r*step,(r+1)*step)
        return prod(x_ref[at,:],up,NN),prod(g_ref[at,:],dn,NT)
    count=rows//step
    nxt=ahead(0)
    total=None
    for r in range(count):
        at=slice(r*step,(r+1)*step)
        pre,gh=nxt
        if r+1<count: nxt=ahead(r+1)
        hidden,slope=gelu_parts(pre+bias)
        hidden=hidden.astype(jnp.bfloat16)
        hid_ref[at,:]=hidden
        gp=(gh.astype(jnp.bfloat16).astype(jnp.float32)*slope).astype(jnp.bfloat16)
        pre_ref[at,:]=gp
        s=jnp.sum(gp.astype(jnp.float32),axis=0,keepdims=True)
        total=s if total is None else total+s
        down_ref[at,:]+=prod(hidden,dn,NN)
        back_ref[at,:]+=prod(gp,up,NT)
    gb_ref[0]=total
    gu_ref[0]=prod(x_ref[...],pre_ref[...],COLS).astype(gu_ref.dtype)
    gd_ref[0]=prod(hid_ref[...],g_ref[...],COLS).astype(gd_ref.dtype)

def feed_forward(x,g,col,row,bias):
    T,D=x.shape; H=col.shape[2]
    f32=jnp.float32; bf=jnp.bfloat16
    once=pl.BlockSpec((T,D),lambda s:(0,0),pipeline_mode=pl.Buffered(1))
    whole=pl.BlockSpec((T,D),lambda s:(0,0))
    return pl.pallas_call(feed_kernel,grid=(4,),
        out_shape=(jax.ShapeDtypeStruct((T,D),f32),jax.ShapeDtypeStruct((T,D),f32),jax.ShapeDtypeStruct((4,D,H),bf),
                   jax.ShapeDtypeStruct((4,H,D),bf),jax.ShapeDtypeStruct((4,1,H),f32)),
        in_specs=[once,once,pl.BlockSpec((1,D,H),lambda s:(s+6,0,0)),pl.BlockSpec((1,H,D),lambda s:(s+2,0,0)),pl.BlockSpec((1,1,H),lambda s:(s,0,0))],
        out_specs=[whole,whole,pl.BlockSpec((1,D,H),lambda s:(s,0,0)),pl.BlockSpec((1,H,D),lambda s:(s,0,0)),pl.BlockSpec((1,1,H),lambda s:(s,0,0))],
        scratch_shapes=[pltpu.VMEM((T,H),bf),pltpu.VMEM((T,H),bf)],
        compiler_params=pltpu.CompilerParams(vmem_limit_bytes=56*1024*1024),
        cost_estimate=pl.CostEstimate(flops=6*2*4*T*D*H,bytes_accessed=4*T*D+8*T*D+16*D*H*2,transcendentals=8*T*H),
    )(x,g,col,row,bias[4:8,None,:])

MESH=pl.DeviceIdType.MESH

def share_kernel(parts, cores, sent_ref, rows_ref, came_ref, total_ref, norm_ref, arrived, own_sem, send_sem, recv_sem, up_send, up_recv, down_send, down_recv):
    here=lax.axis_index("dp"); core=lax.axis_index("mp")
    me=here*cores+core
    everyone=parts*cores
    count=rows_ref.shape[0]
    barrier=pltpu.get_barrier_semaphore()
    def place(at):
        return (at//cores,at%cores)
    def others(n,mine,body):
        for at in range(n):
            @pl.when(mine!=at)
            def _(at=at): body(at)
    others(everyone,me,lambda at: pl.semaphore_signal(barrier,inc=1,device_id=place(at),device_id_type=MESH))
    own=pltpu.make_async_copy(sent_ref.at[here],came_ref.at[here],own_sem)
    own.start()
    pl.semaphore_wait(barrier,everyone-1)
    def up(to):
        return pltpu.make_async_remote_copy(src_ref=rows_ref.at[to],dst_ref=arrived.at[me],send_sem=up_send.at[to],recv_sem=up_recv.at[me],
            device_id=place(to),device_id_type=MESH)
    def down(to):
        return pltpu.make_async_remote_copy(src_ref=total_ref.at[me],dst_ref=total_ref.at[me],send_sem=down_send.at[to],recv_sem=down_recv.at[me],
            device_id=place(to),device_id_type=MESH)
    def block(to):
        return pltpu.make_async_remote_copy(src_ref=sent_ref.at[to],dst_ref=came_ref.at[here],send_sem=send_sem.at[to],recv_sem=recv_sem.at[here],
            device_id=(to,core),device_id_type=MESH)
    def landed(ref,sem,at):
        pltpu.make_async_copy(ref.at[at],ref.at[at],sem.at[at]).wait()
    others(count,me,lambda to: up(to).start())
    others(parts,here,lambda to: block(to).start())
    @pl.when(me<count)
    def _():
        arrived[me]=rows_ref[me]
        others(everyone,me,lambda at: landed(arrived,up_recv,at))
        total_ref[me]=jnp.sum(arrived[...],axis=0)
        others(everyone,me,lambda to: down(to).start())
    others(count,me,lambda to: up(to).wait_send())
    others(count,me,lambda at: landed(total_ref,down_recv,at))
    vectors=total_ref[0:count-1]
    square=jnp.sum(vectors*vectors,axis=0)+total_ref[count-1]
    norm_ref[...]=jnp.broadcast_to(jnp.sqrt(jnp.sum(square,keepdims=True)),norm_ref.shape)
    @pl.when(me<count)
    def _(): others(everyone,me,lambda to: down(to).wait_send())
    def end_block(at):
        block(at).wait_send()
        landed(came_ref,recv_sem,at)
    others(parts,here,end_block)
    own.wait()

def share(sent,square,vectors,cores):
    parts,rows,width=sent.shape
    count=vectors.shape[0]+1
    everyone=parts*cores
    rows_in=jnp.concatenate([vectors,jnp.zeros_like(vectors[:1]).at[0,0].set(square)]).reshape(count,8,-1)
    tile=rows_in.shape[1:]
    vm=pl.BlockSpec(memory_space=pltpu.VMEM)
    dma=pltpu.SemaphoreType.DMA
    came,total,norm=pl.pallas_call(partial(share_kernel,parts,cores),
        out_shape=(jax.ShapeDtypeStruct(sent.shape,sent.dtype),jax.ShapeDtypeStruct(rows_in.shape,jnp.float32),jax.ShapeDtypeStruct((8,128),jnp.float32)),
        in_specs=[vm,vm],out_specs=[vm,vm,vm],
        scratch_shapes=[pltpu.VMEM((everyone,)+tile,jnp.float32),dma,dma((parts,)),dma((parts,)),
            dma((everyone,)),dma((everyone,)),dma((everyone,)),dma((everyone,))],
        compiler_params=pltpu.CompilerParams(collective_id=0,has_side_effects=True,vmem_limit_bytes=16*1024*1024),
    )(sent,rows_in)
    return came,total.reshape(count,-1)[:-1],norm[0,0]

BS=256; STEP=10
weight_rate=0.03; weight_decay=0.01
HI=lax.Precision.HIGHEST
def hdot(a,b,dims,precision=HI):
    return lax.dot_general(a,b,(dims,((),())),precision=precision,preferred_element_type=jnp.float32)
DIM_NN=((1,),(0,)); DIM_NT=((1,),(1,)); DIM_TN=((0,),(0,))

def parts2(a):
    top=a.astype(jnp.bfloat16)
    return top,(a-top.astype(jnp.float32)).astype(jnp.bfloat16)

def dot1(a,b,dims):
    return lax.dot_general(a,b,(dims,((),())),preferred_element_type=jnp.float32)

def dot3(a,b,dims):
    a0,a1=a; b0,b1=b
    return dot1(a0,b0,dims)+(dot1(a0,b1,dims)+dot1(a1,b0,dims))

def soap_kernel(clip_ref,g_ref,first,second,master,left,right,ql_ref,qr_ref,
                first_o,second_o,master_o,copy_o,left_o,right_o,al_o,ar_o,ml_o,mr_o):
    clip=clip_ref[0,0]
    g=g_ref[0]
    ql=ql_ref[0]; qr=qr_ref[0]
    scale=0.05*clip*clip
    left_new=0.95*left[0]+scale*dot1(g,g,DIM_NT)
    left_o[0]=left_new
    al=hdot(left_new,ql,DIM_NN); al_o[0]=al
    ml_o[0]=hdot(al,al,DIM_TN)
    right_new=0.95*right[0]+scale*dot1(g,g,DIM_TN)
    right_o[0]=right_new
    ar=hdot(right_new,qr,DIM_NN); ar_o[0]=ar
    mr_o[0]=hdot(ar,ar,DIM_TN)
    ql2=parts2(ql); qr2=parts2(qr)
    half=dot1(ql2[0],g,DIM_TN)+dot1(ql2[1],g,DIM_TN)
    rot=clip*dot3(parts2(half),qr2,DIM_NN)
    f=0.9*first[0]+0.1*rot; first_o[0]=f
    s=0.99*second[0]+0.01*rot*rot; second_o[0]=s
    ratio=f/(1.0-0.9**STEP)/(jnp.sqrt(s/(1.0-0.99**STEP))+1e-8)
    stepped=dot3(parts2(dot3(ql2,parts2(ratio),DIM_NN)),qr2,DIM_NT)
    m=master[0]-weight_rate*(stepped+weight_decay*master[0])
    master_o[0]=m; copy_o[0]=m.astype(jnp.bfloat16)

def soap_stage(clip,g,first,second,master,left,right,ql,qr):
    n=g.shape[0]
    spec=pl.BlockSpec((1,BS,BS),lambda i:(i,0,0))
    f32=jax.ShapeDtypeStruct((n,BS,BS),jnp.float32)
    return pl.pallas_call(soap_kernel,grid=(n,),
        out_shape=(f32,f32,f32,jax.ShapeDtypeStruct((n,BS,BS),jnp.bfloat16),f32,f32,f32,f32,f32,f32),
        in_specs=[pl.BlockSpec(memory_space=pltpu.SMEM)]+[spec]*8,
        out_specs=[spec]*10,
        compiler_params=pltpu.CompilerParams(vmem_limit_bytes=48*1024*1024),
    )(clip.reshape(1,1),g,first,second,master,left,right,ql,qr)

PW=64
def chol_kernel(al_ref,ar_ref,ml_ref,mr_ref,ql_o,qr_o,work,tile,pivot):
    n=al_ref.shape[0]; pairs=n
    def load(m,_):
        work[m]=ml_ref[m]; work[n+m]=mr_ref[m]
        return 0
    lax.fori_loop(0,n,load,0)
    lane=lax.broadcasted_iota(jnp.int32,(1,2*PW),1)
    base=lane//PW*PW
    bigcol=lax.broadcasted_iota(jnp.int32,(PW,BS),1)
    bigrow=lax.broadcasted_iota(jnp.int32,(PW,BS),0)
    lower=lax.broadcasted_iota(jnp.int32,(PW,2*PW),1)%PW<=lax.broadcasted_iota(jnp.int32,(PW,2*PW),0)
    for p in range(BS//PW):
        lo=p*PW; at=slice(lo,lo+PW)
        for j in range(pairs):
            tile[j]=jnp.concatenate([work[2*j,at,at],work[2*j+1,at,at]],axis=1)
        for quarter in range(4):
            top=quarter*PW//4; height=PW-top
            rows=lax.broadcasted_iota(jnp.int32,(height,2*PW),0)+top
            def step(k,_):
                here=lane-base==k
                below=rows>k
                fill=jnp.where(rows==k,1.0,0.0)
                t=tile[:,top:,:]
                r=tile[:,pl.ds(k,1),:]
                flat=pairs*height
                c=jnp.take_along_axis(t.reshape(flat,2*PW),jnp.broadcast_to(base+k,(flat,2*PW)),axis=1).reshape(pairs,height,2*PW)
                wide_r=jnp.broadcast_to(r[0],(8,2*PW)) if pairs==1 else r.reshape(pairs,2*PW)
                d=jnp.take_along_axis(wide_r,jnp.broadcast_to(base+k,wide_r.shape),axis=1)[:pairs].reshape(pairs,1,2*PW)
                r=jnp.where(here[None],1.0,r)*(1.0/d)
                pivot[:,pl.ds(k,1),:]=d
                tile[:,top:,:]=jnp.where(here[None],fill[None],t)-jnp.where(below[None],c,0.0)*r
                return 0
            lax.fori_loop(top,top+PW//4,step,0)
        for j in range(pairs):
            tile[j]=jnp.where(lower,tile[j]*lax.rsqrt(pivot[j]),0.0)
        inside=(bigcol>=lo)&(bigcol<lo+PW)
        eye=jnp.where(bigcol-lo==bigrow,1.0,0.0)
        def apply(j,_):
            both=tile[j]
            for s in range(2):
                m=2*j+s
                r=hdot(both[:,s*PW:(s+1)*PW],jnp.where(inside,eye,work[m,at,:]),DIM_NN)
                work[m,at,:]=r
                if p<BS//PW-1:
                    rest=jnp.where(inside[0:1],0.0,work[m,lo+PW:,:])
                    work[m,lo+PW:,:]=rest-hdot(r[:,lo+PW:],r,DIM_TN)
            return 0
        lax.fori_loop(0,pairs,apply,0)
    keep=lax.broadcasted_iota(jnp.int32,(BS,BS),1)<=lax.broadcasted_iota(jnp.int32,(BS,BS),0)
    def final(m,_):
        ql_o[m]=hdot(al_ref[m],jnp.where(keep,work[m],0.0),DIM_NT)
        qr_o[m]=hdot(ar_ref[m],jnp.where(keep,work[n+m],0.0),DIM_NT)
        return 0
    lax.fori_loop(0,n,final,0)

def chol_stage(al,ar,ml,mr):
    n=al.shape[0]
    f32=jax.ShapeDtypeStruct((n,BS,BS),jnp.float32)
    vm=pl.BlockSpec(memory_space=pltpu.VMEM)
    return pl.pallas_call(chol_kernel,out_shape=(f32,f32),in_specs=[vm]*4,out_specs=[vm]*2,
        scratch_shapes=[pltpu.VMEM((2*n,BS,BS),jnp.float32),pltpu.VMEM((n,PW,2*PW),jnp.float32),pltpu.VMEM((n,PW,2*PW),jnp.float32)],
        compiler_params=pltpu.CompilerParams(vmem_limit_bytes=56*1024*1024))(al,ar,ml,mr)

def soap(clip,g,first,second,master,left,right,ql,qr):
    f,s,m,c,l,r,al,ar,ml,mr=soap_stage(clip,g,first,second,master,left,right,ql,qr)
    lr,rr=chol_stage(al,ar,ml,mr)
    return f,s,m,c,l,r,lr,rr


LEN = 1024
shared_rate = 0.6
split_rate = 0.2
clip_limit = 1.0
SWAP = [(0, 1), (1, 0)]


def adam_step(gradient, first_state, second_state, values, step_rate):
    first_new = 0.9 * first_state + 0.1 * gradient
    second_new = 0.99 * second_state + 0.01 * gradient * gradient
    ratio = first_new / (1.0 - 0.9**STEP) / (jnp.sqrt(second_new / (1.0 - 0.99**STEP)) + 1e-08)
    return (first_new, second_new, values - step_rate * ratio)


def norm_forward(values, gain, shift):
    hat, _ = hat_of(values)
    return (hat * gain + shift).astype(jnp.bfloat16)


def dot32(a, b):
    return jnp.dot(a, b, preferred_element_type=jnp.float32)


def low(a):
    return a.astype(jnp.bfloat16)


def wide(a):
    return a.astype(jnp.float32)


def exchange(array):
    return lax.ppermute(array, "mp", SWAP)


def to_parts(array, parts):
    stacked, height, width = array.shape
    return array.reshape(stacked * height // BS, parts, BS // parts, width)


def tie(*arrays):
    return lax.optimization_barrier(arrays)


class Staged:
    def __init__(self, terms, first_bits):
        parts = terms[0].shape[1]
        bits = parts.bit_length() - 1
        self.parts = parts
        self.terms = [a.reshape((a.shape[0],) + (2,) * bits + a.shape[2:]) for a in terms]
        self.left = list(range(bits - 1, -1, -1))
        self.order = [b for b in first_bits if b < bits] + [b for b in range(bits) if b not in first_bits]
        self.got = None

    def send(self):
        if not self.order:
            return
        b = self.order.pop(0)
        axis = 1 + self.left.index(b)
        self.left.remove(b)
        mine = (lax.axis_index("dp") >> b) & 1
        give = [lax.dynamic_index_in_dim(a, 1 - mine, axis, keepdims=False) for a in self.terms]
        give = give[0] if len(give) == 1 else low(sum(wide(a) for a in give))
        self.got = lax.ppermute(give, "dp", [(i, i ^ (1 << b)) for i in range(self.parts)])
        self.terms = [lax.dynamic_index_in_dim(a, mine, axis, keepdims=False) for a in self.terms]

    def take(self):
        if self.got is not None:
            self.terms.append(self.got)
            self.terms = [low(sum(wide(a) for a in self.terms))]
            self.got = None

    def finish(self):
        self.take()
        while self.order:
            self.send()
            self.take()
        return self.terms[0]


def checkpoint(anchor, *sums):
    waiting = [s for s in sums if s.got is not None]
    anchor, *got = tie(anchor, *[s.got for s in waiting])
    for s, g in zip(waiting, got):
        s.got = g
        s.take()
        s.send()
    return anchor


def all_sum(array, parts):
    array = array + lax.ppermute(array, "mp", SWAP)
    for b in range(parts.bit_length() - 1):
        array = array + lax.ppermute(array, "dp", [(i, i ^ (1 << b)) for i in range(parts)])
    return array


def slot_order(block_slot):
    numbers = jnp.arange(block_slot.shape[0], dtype=jnp.int32)
    return jnp.sum(jnp.where(block_slot[None, :] == numbers[:, None], numbers[None, :], 0), axis=1)


def on_device(
    parts,
    mp_size,
    tokens,
    memory,
    cotangent,
    bucket,
    target_lengths,
    memory_lengths,
    block_slot,
    col_weights,
    row_weights,
    shared_vectors,
    split_vectors,
    shared_first,
    shared_second,
    split_first,
    split_second,
    slot_first,
    slot_second,
    slot_master,
    slot_left,
    slot_right,
    left_basis,
    right_basis,
):
    core = lax.axis_index("mp")
    half = col_weights.shape[2]
    shared = shared_vectors
    own_bucket = lax.dynamic_index_in_dim(bucket, core, 0, keepdims=False)
    own_target = lax.dynamic_index_in_dim(target_lengths, core, 0, keepdims=False)
    own_memory = lax.dynamic_index_in_dim(memory_lengths, core, 0, keepdims=False)
    rows = tokens.shape[0]
    self_at = self_plan(own_bucket, rows)
    cross_at = cross_plan(own_bucket, own_memory, rows, memory.shape[0])
    places = jnp.arange(rows, dtype=jnp.int32)
    size = rows // jnp.left_shift(jnp.int32(1), own_bucket)
    segment = places // size
    live = jnp.any(
        (segment[:, None] == jnp.arange(4, dtype=jnp.int32)[None, :])
        & ((places - segment * size)[:, None] < own_target[None, :]),
        axis=1,
    )
    cols = (col_weights, exchange(col_weights))
    rws = (row_weights, exchange(row_weights))
    splits = (split_vectors, exchange(split_vectors))
    both = (0, 1)

    tokens_wide = wide(tokens)
    normed1 = norm_forward(tokens_wide, shared[0], shared[1])
    query, key, value, mem_key, mem_value, self_out, self_log = ([], [], [], [], [], [], [])
    for h in both:
        query.append(low(dot32(normed1, cols[h][0]) + splits[h][0]))
        key.append(low(dot32(normed1, cols[h][1])))
        value.append(low(dot32(normed1, cols[h][2]) + splits[h][1]))
        mem_key.append(low(dot32(memory, cols[h][4])))
        mem_value.append(low(dot32(memory, cols[h][5]) + splits[h][3]))
        out, log = attention(query[h], key[h], value[h], self_at, True)
        self_out.append(out)
        self_log.append(log)
    resid1, normed2 = join_forward(tokens, self_out, rws, 0, shared[6], shared[2], shared[3])
    cross_query, cross_out, cross_log = ([], [], [])
    for h in both:
        cross_query.append(low(dot32(normed2, cols[h][3]) + splits[h][2]))
        out, log = attention(cross_query[h], mem_key[h], mem_value[h], cross_at, False)
        cross_out.append(out)
        cross_log.append(log)
    resid2, normed3 = join_forward(resid1, cross_out, rws, 1, shared[7], shared[4], shared[5])
    grad_out = jnp.where(live[:, None], cotangent, jnp.zeros_like(cotangent))
    down_peer, back_peer, up_grad, down_grad, up_bias_peer = feed_forward(normed3, grad_out, cols[1], rws[1], splits[1])
    up_peer = exchange(up_grad)
    down_grad_peer = exchange(down_grad)
    down_own, back_own, up_grad, down_grad, up_bias_own = feed_forward(normed3, grad_out, cols[0], rws[0], splits[0])
    output = low(resid2 + (down_own + down_peer) + shared[8])
    up_bias = [up_bias_own[:, 0], up_bias_peer[:, 0]]
    back_own, up_peer, down_grad_peer = tie(back_own, up_peer, down_grad_peer)
    down_sum = Staged([to_parts(down_grad, parts), to_parts(down_grad_peer, parts)], (1, 0))
    up_sum = Staged([to_parts(up_grad, parts), to_parts(up_peer, parts)], (0, 1))
    down_sum.send()
    up_sum.send()
    grad_resid2, grad2, sums3 = join_back(
        None, None, 0, (back_own, back_peer), (resid2, grad_out, shared[4]), low_too=True
    )

    def outer(x, g):
        return low(jnp.einsum("td,te->de", x, g, preferred_element_type=jnp.float32))

    row1_peer = exchange(outer(cross_out[1], grad2))
    row1_own = outer(cross_out[0], grad2)

    def cross_back(h, grad):
        return attention_back(
            cross_query[h], mem_key[h], mem_value[h], grad, cross_out[h], cross_log[h], cross_at, False
        )

    grad_cq, grad_mk, grad_mv = ([None, None], [None, None], [None, None])
    grad = [low(jnp.einsum("td,fd->tf", grad2, rws[h][1], preferred_element_type=jnp.float32)) for h in both]
    grad_cq[1], grad_mk[1], grad_mv[1] = cross_back(1, grad[1])
    cross_peer = exchange(
        jnp.stack([outer(normed2, grad_cq[1]), outer(memory, grad_mk[1]), outer(memory, grad_mv[1])])
    )
    grad[0], cross_peer = tie(checkpoint(grad[0], down_sum, up_sum), cross_peer)
    grad_cq[0], grad_mk[0], grad_mv[0] = cross_back(0, grad[0])
    (grad_cq[0], grad_mk[0], grad_mv[0]), row1_peer = tie(
        checkpoint((grad_cq[0], grad_mk[0], grad_mv[0]), down_sum, up_sum), row1_peer
    )
    cross_own = jnp.stack([outer(normed2, grad_cq[0]), outer(memory, grad_mk[0]), outer(memory, grad_mv[0])])
    cross_sum = Staged([to_parts(cross_own, parts), to_parts(cross_peer, parts)], (0, 1))
    cross_sum.send()
    grad_resid1, grad1, sums2 = join_back(
        [[grad_cq[0]], [grad_cq[1]]], cols, 3, (), (resid1, grad_resid2, shared[2]), low_too=True
    )
    grad1 = checkpoint(grad1, down_sum, up_sum)
    row0_peer = exchange(outer(self_out[1], grad1))
    row0_own = outer(self_out[0], grad1)

    def self_back(h, grad):
        return attention_back(query[h], key[h], value[h], grad, self_out[h], self_log[h], self_at, True)

    grad_q, grad_k, grad_v = ([None, None], [None, None], [None, None])
    grad = [low(jnp.einsum("td,fd->tf", grad1, rws[h][0], preferred_element_type=jnp.float32)) for h in both]
    grad_q[1], grad_k[1], grad_v[1] = self_back(1, grad[1])
    self_peer = exchange(
        jnp.stack([outer(normed1, grad_q[1]), outer(normed1, grad_k[1]), outer(normed1, grad_v[1])])
    )
    row_sum = Staged(
        [
            to_parts(jnp.stack([row0_own, row1_own]), parts),
            to_parts(jnp.stack([row0_peer, row1_peer]), parts),
        ],
        (1, 0),
    )
    row_sum.send()
    grad[0], self_peer = tie(checkpoint(grad[0], down_sum, up_sum, cross_sum), self_peer)
    grad_q[0], grad_k[0], grad_v[0] = self_back(0, grad[0])
    grad_q[0], grad_k[0], grad_v[0] = checkpoint((grad_q[0], grad_k[0], grad_v[0]), cross_sum, row_sum)
    self_own = jnp.stack([outer(normed1, grad_q[0]), outer(normed1, grad_k[0]), outer(normed1, grad_v[0])])
    self_terms = [to_parts(self_own, parts), to_parts(self_peer, parts)]
    middle = self_terms[0].shape[0] // 2
    self_a = Staged([a[:middle] for a in self_terms], (0, 1))
    self_b = Staged([a[middle:] for a in self_terms], (1, 0))
    self_a.send()
    self_b.send()
    (grad_q[0], grad_k[0], grad_v[0]), self_own = tie((grad_q[0], grad_k[0], grad_v[0]), self_own)
    input_grad, sums1 = join_back(
        [[grad_q[h], grad_k[h], grad_v[h]] for h in both], cols, 0, (), (tokens, grad_resid1, shared[0])
    )
    input_grad, sums1, grad_mk[0] = checkpoint(
        (input_grad, sums1, grad_mk[0]), cross_sum, row_sum, self_a, self_b
    )
    (memory_grad,) = join_back([[grad_mk[h], grad_mv[h]] for h in both], cols, 2)
    memory_grad, sums1 = checkpoint((memory_grad, sums1), cross_sum, row_sum, self_a, self_b)
    self_piece = jnp.concatenate([self_a.finish(), self_b.finish()], axis=0)
    cross_piece = cross_sum.finish()
    up_piece = up_sum.finish()
    down_piece = down_sum.finish()
    row_piece = row_sum.finish()

    def column_sum(a):
        return jnp.sum(wide(a), axis=0)

    shared_grad = jnp.concatenate(
        [
            sums1[0:2],
            sums2[0:2],
            sums3[0:2],
            sums2[2:3],
            sums3[2:3],
            column_sum(grad_out)[None],
        ]
    )
    split_grad = [
        jnp.concatenate(
            [
                jnp.stack([column_sum(grad_q[h]), column_sum(grad_v[h]), column_sum(grad_cq[h]), column_sum(grad_mv[h])]),
                up_bias[h],
            ]
        )
        for h in both
    ]
    first = jnp.where(core == 0, split_grad[0], split_grad[1])
    second = jnp.where(core == 0, split_grad[1], split_grad[0])
    vectors = jnp.concatenate([shared_grad, jnp.concatenate([first, second], axis=1)], axis=0)
    def blocks(piece):
        m, rows_in, width = piece.shape
        return (
            piece.reshape(m, rows_in, width // BS, BS).transpose(0, 2, 1, 3).reshape(-1, rows_in, BS)
        )

    pieces = jnp.concatenate(
        [
            blocks(self_piece),
            blocks(cross_piece),
            blocks(up_piece),
            blocks(row_piece),
            blocks(down_piece),
        ],
        axis=0,
    )
    square = jnp.sum(wide(pieces) * wide(pieces))
    owned = slot_first.shape[0]
    part_rows = BS // parts
    sent = jnp.take(pieces, slot_order(block_slot), axis=0)
    if part_rows % 16 == 0 and vectors.shape[0] < parts * mp_size:
        came, vectors, grad_norm = share(sent.reshape(parts, owned * part_rows, BS), square, vectors, mp_size)
    else:
        came = lax.all_to_all(sent.reshape(parts, owned, part_rows, BS), "dp", 0, 0, tiled=True)
        vectors = all_sum(vectors, parts)
        grad_norm = jnp.sqrt(all_sum(square.reshape(1, 1), parts)[0, 0] + jnp.sum(vectors * vectors))
    shared_sum = vectors[:9]
    split_sum = vectors[9:]
    mine = came.reshape(parts, owned, part_rows, BS).transpose(1, 0, 2, 3).reshape(owned, BS, BS)
    clip = clip_limit / jnp.maximum(grad_norm, clip_limit)

    def flat(a):
        return a.reshape(owned, BS, BS)

    updated = soap(
        clip,
        mine,
        flat(slot_first),
        flat(slot_second),
        flat(slot_master),
        flat(slot_left),
        flat(slot_right),
        flat(left_basis),
        flat(right_basis),
    )
    first_moment, second_moment, master_weight, master_copy, left_stat, right_stat, left_rotation, right_rotation = (
        a.reshape(slot_first.shape) for a in updated
    )
    shared_mean, shared_square, shared_values = adam_step(
        shared_sum * clip, shared_first, shared_second, shared_vectors, shared_rate
    )
    split_own = lax.dynamic_slice_in_dim(split_sum, core * half, half, axis=1)
    split_mean, split_square, split_values = adam_step(
        split_own * clip, split_first, split_second, split_vectors, split_rate
    )
    return (
        output,
        input_grad,
        memory_grad,
        first_moment,
        second_moment,
        master_weight,
        master_copy,
        left_stat,
        right_stat,
        left_rotation,
        right_rotation,
        shared_mean,
        shared_square,
        shared_values,
        split_mean,
        split_square,
        split_values,
        grad_norm,
    )


def solution(mesh):
    rows = P(("dp", "mp"), None)
    slots = P("dp", "mp", None, None)
    split = P(None, "mp")
    placed = (
        (rows, rows, rows, P("dp"), P("dp", None), P("dp", None), P())
        + (P(None, None, "mp"), P(None, "mp", None), P(), split, P(), P(), split, split)
        + (slots,) * 7
    )
    return jax.shard_map(
        partial(on_device, mesh.shape["dp"], mesh.shape["mp"]),
        mesh=mesh,
        in_specs=placed,
        out_specs=(rows,) * 3 + (slots,) * 8 + (P(),) * 3 + (split,) * 3 + (P(),),
        check_vma=False,
    )
```

```python
from functools import partial

import jax
import jax.numpy as jnp
from jax import lax
from jax.experimental import pallas as pl
from jax.experimental.pallas import tpu as pltpu
from jax.sharding import PartitionSpec as P

HEAD_DIM=64; TQ=256
SCALE=HEAD_DIM**-0.5
EXPC=SCALE*1.4426950408889634
NEG=-1e30
NT=(((1,),(1,)),((),()))
NN=(((1,),(0,)),((),()))

def rows_of(i,n=1):
    if isinstance(i,int): return slice(i*TQ,(i+n)*TQ)
    return pl.ds(pl.multiple_of(i*TQ,TQ),n*TQ)

def head_cols(h):
    return slice(h*HEAD_DIM,(h+1)*HEAD_DIM)

def lanes_of(pair):
    return pl.ds(pl.multiple_of(pair*128,128),128)

def allowed(causal,limit,j):
    r=lax.broadcasted_iota(jnp.int32,(TQ,TQ),0)
    if causal: return r<=lax.broadcasted_iota(jnp.int32,(TQ,TQ),1)
    return r<limit-j*TQ

def each_case(causal,plan,tiles,pairs,emit):
    def over(n,body):
        def step(i,_):
            body(i)
            return 0
        lax.fori_loop(0,n,step,0)
    for b in range(3):
        count=1<<b; size=tiles>>b
        if b==0 and not causal:
            for n in (size,size//2):
                fits=plan[1]>TQ*size//2 if n==size else plan[1]<=TQ*size//2
                @pl.when((plan[0]==b)&fits)
                def _(n=n):
                    over(pairs,lambda pair: emit(pair,[(0,size,n,plan[1],n-size//2)]))
        else:
            @pl.when(plan[0]==b)
            def _(count=count,size=size):
                if count==1: over(pairs,lambda pair: emit(pair,[(0,size,size,None,size-1)]))
                else: over(pairs,lambda pair: over(count,lambda s: emit(pair,[(s*size,size,size,None if causal else plan[1+s],0)])))

def tile_items(causal,segments):
    out=[]
    for t0,qn,kn,limit,masked in segments:
        for i in range(qn):
            n=i+1 if causal else kn
            out.append((t0+i,t0,n,limit,n-1 if causal else masked))
    return out

def fwd_kernel(causal, tiles, plan, q_ref, k_ref, v_ref, o_ref, l_ref, vt_ref):
    pairs=q_ref.shape[1]//128
    def turn(pair,_):
        vt_ref[pair]=v_ref[:,lanes_of(pair)].astype(jnp.float32).T.astype(jnp.bfloat16)
        return 0
    lax.fori_loop(0,pairs,turn,0)
    def emit(pair,segments):
        lanes=lanes_of(pair)
        items=[(t,h) for t in tile_items(causal,segments) for h in range(2)]
        def scores(item):
            (i,k0,n,limit,masked),h=item
            q=q_ref[rows_of(i),lanes][:,head_cols(h)]
            parts=[]
            for j in range(n):
                s=lax.dot_general(k_ref[rows_of(k0+j),lanes][:,head_cols(h)],q,NT,preferred_element_type=jnp.float32)
                if j>=masked:
                    s=jnp.where(allowed(causal,limit,j),s,NEG)
                parts.append(s)
            return parts
        ahead=scores(items[0])
        held=None
        for c,((i,k0,n,limit,masked),h) in enumerate(items):
            parts=ahead
            if c+1<len(items): ahead=scores(items[c+1])
            top=parts[0].max(axis=0,keepdims=True)
            for s in parts[1:]: top=jnp.maximum(top,s.max(axis=0,keepdims=True))
            total=None; acc=None
            for j,s in enumerate(parts):
                p=jnp.exp2((s-top)*EXPC)
                t=p.sum(axis=0,keepdims=True)
                total=t if total is None else total+t
                a=lax.dot_general(vt_ref[pair,head_cols(h),rows_of(k0+j)],p.astype(jnp.bfloat16),NN,preferred_element_type=jnp.float32)
                acc=a if acc is None else acc+a
            acc=acc*(1.0/total)
            l_ref[pair,h:h+1,rows_of(i)]=top+jnp.log2(total)*(1.0/EXPC)
            if h==0: held=acc
            else: o_ref[rows_of(i),lanes]=jnp.concatenate([held,acc],axis=0).T.astype(o_ref.dtype)
    each_case(causal,plan,tiles,pairs,emit)

VM=pl.BlockSpec(memory_space=pltpu.VMEM)
SM=pl.BlockSpec(memory_space=pltpu.SMEM)

def attention(q,k,v,plan,causal):
    T,W=q.shape; M=k.shape[0]; pairs=W//128; tiles=T//TQ
    return pl.pallas_call(
        partial(fwd_kernel,causal,tiles),
        out_shape=(jax.ShapeDtypeStruct((T,W),jnp.bfloat16),jax.ShapeDtypeStruct((pairs,2,T),jnp.float32)),
        in_specs=[SM,VM,VM,VM],out_specs=[VM,VM],
        scratch_shapes=[pltpu.VMEM((pairs,128,M),jnp.bfloat16)],
        compiler_params=pltpu.CompilerParams(vmem_limit_bytes=8*1024*1024),
        cost_estimate=pl.CostEstimate(flops=4*T*M*W//2,bytes_accessed=8*T*W,transcendentals=T*M*W//128),
    )(plan,q,k,v)

def bwd_kernel(causal, tiles, plan, q_ref, k_ref, v_ref, g_ref, o_ref, l_ref, dq_ref, dk_ref, dv_ref, kt_ref, p_ref, s_ref, d_ref):
    pairs=q_ref.shape[1]//128
    ones=jnp.ones((8,HEAD_DIM),jnp.bfloat16)
    def turn(pair,_):
        lanes=lanes_of(pair)
        kt_ref[pair]=k_ref[:,lanes].astype(jnp.float32).T.astype(jnp.bfloat16)
        prod=g_ref[:,lanes].astype(jnp.float32)*o_ref[:,lanes].astype(jnp.float32)
        top=prod.astype(jnp.bfloat16)
        rest=(prod-top.astype(jnp.float32)).astype(jnp.bfloat16)
        for h in range(2):
            d_ref[pair,h]=(lax.dot_general(ones,top[:,head_cols(h)],NT,preferred_element_type=jnp.float32)
                +lax.dot_general(ones,rest[:,head_cols(h)],NT,preferred_element_type=jnp.float32))
        return 0
    lax.fori_loop(0,pairs,turn,0)
    def emit(pair,segments):
        lanes=lanes_of(pair)
        items=[(i,k0,j,n,limit,masked,h) for i,k0,n,limit,masked in tile_items(causal,segments) for j in range(n) for h in range(2)]
        def products(item):
            i,k0,j,n,limit,masked,h=item
            return (lax.dot_general(k_ref[rows_of(k0+j),lanes][:,head_cols(h)],q_ref[rows_of(i),lanes][:,head_cols(h)],NT,preferred_element_type=jnp.float32),
                    lax.dot_general(v_ref[rows_of(k0+j),lanes][:,head_cols(h)],g_ref[rows_of(i),lanes][:,head_cols(h)],NT,preferred_element_type=jnp.float32))
        ahead=products(items[0])
        acc=[None,None]
        for c,(i,k0,j,n,limit,masked,h) in enumerate(items):
            s,dp=ahead
            if c+1<len(items): ahead=products(items[c+1])
            p=jnp.exp2((s-l_ref[pair,h:h+1,rows_of(i)])*EXPC)
            if j>=masked: p=jnp.where(allowed(causal,limit,j),p,0.0)
            p_ref[h,rows_of(k0+j),rows_of(i)]=p.astype(jnp.bfloat16)
            ds=(p*(dp-d_ref[pair,h,0:1,rows_of(i)])).astype(jnp.bfloat16)
            s_ref[h,rows_of(k0+j),rows_of(i)]=ds
            a=lax.dot_general(kt_ref[pair,head_cols(h),rows_of(k0+j)],ds,NN,preferred_element_type=jnp.float32)
            acc[h]=a if j==0 else acc[h]+a
            if j==n-1 and h==1:
                dq_ref[rows_of(i),lanes]=(jnp.concatenate(acc,axis=0)*SCALE).T.astype(dq_ref.dtype)
        for t0,qn,kn,limit,masked in segments:
            for j in range(qn):
                if j>=kn:
                    dk_ref[rows_of(t0+j),lanes]=jnp.zeros((TQ,128),dk_ref.dtype)
                    dv_ref[rows_of(t0+j),lanes]=jnp.zeros((TQ,128),dv_ref.dtype)
                    continue
                cols=rows_of(t0+j,qn-j) if causal else rows_of(t0,qn)
                both=[]
                for h in range(2):
                    both.append((lax.dot_general(p_ref[h,rows_of(t0+j),cols],g_ref[cols,lanes][:,head_cols(h)],NN,preferred_element_type=jnp.float32),
                                 lax.dot_general(s_ref[h,rows_of(t0+j),cols],q_ref[cols,lanes][:,head_cols(h)],NN,preferred_element_type=jnp.float32)))
                dv_ref[rows_of(t0+j),lanes]=jnp.concatenate([a for a,b in both],axis=1).astype(dv_ref.dtype)
                dk_ref[rows_of(t0+j),lanes]=(jnp.concatenate([b for a,b in both],axis=1)*SCALE).astype(dk_ref.dtype)
    each_case(causal,plan,tiles,pairs,emit)

def attention_back(q,k,v,g,out,logs,plan,causal):
    T,W=q.shape; M=k.shape[0]; pairs=W//128; tiles=T//TQ
    narrow=jax.ShapeDtypeStruct((T,W),jnp.bfloat16)
    return pl.pallas_call(
        partial(bwd_kernel,causal,tiles),
        out_shape=(narrow,jax.ShapeDtypeStruct((M,W),jnp.bfloat16),jax.ShapeDtypeStruct((M,W),jnp.bfloat16)),
        in_specs=[SM]+[VM]*6,out_specs=[VM]*3,
        scratch_shapes=[pltpu.VMEM((pairs,128,M),jnp.bfloat16),pltpu.VMEM((2,M,T),jnp.bfloat16),pltpu.VMEM((2,M,T),jnp.bfloat16),pltpu.VMEM((pairs,2,8,T),jnp.float32)],
        compiler_params=pltpu.CompilerParams(vmem_limit_bytes=14*1024*1024),
        cost_estimate=pl.CostEstimate(flops=10*T*M*W//2,bytes_accessed=14*T*W,transcendentals=T*M*W//128),
    )(plan,q,k,v,g,out,logs)

def self_plan(bucket,T):
    return bucket.reshape(1)

def cross_plan(bucket,lengths,T,M):
    return jnp.concatenate([bucket.reshape(1),lengths])

CHUNK=256
JOIN=pltpu.CompilerParams(vmem_limit_bytes=20*1024*1024)

def hat_of(values):
    centered=values-jnp.mean(values,axis=-1,keepdims=True)
    inverse=lax.rsqrt(jnp.mean(centered*centered,axis=-1,keepdims=True)+1e-05)
    return centered*inverse,inverse

def join_kernel(v_ref,a_ref,b_ref,wa_ref,wb_ref,r_ref,sum_ref,norm_ref):
    product=(lax.dot_general(a_ref[...],wa_ref[0],NN,preferred_element_type=jnp.float32)
        +lax.dot_general(b_ref[...],wb_ref[0],NN,preferred_element_type=jnp.float32))
    values=v_ref[...].astype(jnp.float32)+product+r_ref[0:1,:]
    sum_ref[...]=values
    hat,_=hat_of(values)
    norm_ref[...]=(hat*r_ref[1:2,:]+r_ref[2:3,:]).astype(norm_ref.dtype)

def join_forward(values,halves,rows,index,shift,gain,bias):
    T,D=values.shape; H=halves[0].shape[1]
    part=pl.BlockSpec((CHUNK,D),lambda i:(i,0)); narrow=pl.BlockSpec((CHUNK,H),lambda i:(i,0))
    weight=pl.BlockSpec((1,H,D),lambda i:(index,0,0))
    return pl.pallas_call(join_kernel,grid=(T//CHUNK,),
        out_shape=(jax.ShapeDtypeStruct((T,D),jnp.float32),jax.ShapeDtypeStruct((T,D),jnp.bfloat16)),
        in_specs=[part,narrow,narrow,weight,weight,pl.BlockSpec((3,D),lambda i:(0,0))],out_specs=[part,part],
        compiler_params=JOIN,cost_estimate=pl.CostEstimate(flops=4*T*D*H,bytes_accessed=10*T*D+4*T*H+4*H*D,transcendentals=T),
    )(values,*halves,*rows,jnp.stack([shift,gain,bias]))

def back_kernel(terms,extras,norm,low_too,*refs):
    refs=list(refs)
    take=lambda n: [refs.pop(0) for _ in range(n)]
    gs=take(2*terms); ws=take(2 if terms else 0); ex=take(extras)
    acc=None
    for h in range(2 if terms else 0):
        for s in range(terms):
            a=lax.dot_general(gs[h*terms+s][...],ws[h][s],NT,preferred_element_type=jnp.float32)
            acc=a if acc is None else acc+a
    for e in ex:
        acc=e[...] if acc is None else acc+e[...]
    if not norm:
        refs.pop(0)[...]=acc
        return
    v_ref,g_ref,gain_ref=take(3)
    hat,inverse=hat_of(v_ref[...].astype(jnp.float32))
    inner=acc*gain_ref[...]
    back=inverse*(inner-jnp.mean(inner,axis=-1,keepdims=True)-hat*jnp.mean(inner*hat,axis=-1,keepdims=True))
    new=g_ref[...].astype(jnp.float32)+back
    refs.pop(0)[...]=new
    if low_too: refs.pop(0)[...]=new.astype(jnp.bfloat16)
    sums=refs.pop(0)
    @pl.when(pl.program_id(0)==0)
    def _(): sums[...]=jnp.zeros_like(sums)
    sums[0:1,:]+=jnp.sum(acc*hat,axis=0,keepdims=True)
    sums[1:2,:]+=jnp.sum(acc,axis=0,keepdims=True)
    sums[2:3,:]+=jnp.sum(new,axis=0,keepdims=True)

def join_back(gs,cols,index,extras=(),norm=None,low_too=False):
    terms=len(gs[0]) if gs else 0
    T,D=extras[0].shape if extras else (gs[0][0].shape[0],cols[0].shape[1])
    part=pl.BlockSpec((CHUNK,D),lambda i:(i,0))
    args=[]; specs=[]
    if terms:
        H=gs[0][0].shape[1]
        for h in range(2):
            for g in gs[h]: args.append(g); specs.append(pl.BlockSpec((CHUNK,H),lambda i:(i,0)))
        for w in cols: args.append(w); specs.append(pl.BlockSpec((terms,D,H),lambda i:(index,0,0),pipeline_mode=pl.Buffered(1)))
    for e in extras: args.append(e); specs.append(part)
    full=jax.ShapeDtypeStruct((T,D),jnp.float32)
    outs=[full]; out_specs=[part]
    if norm:
        values,grad,gain=norm
        args+=[values,grad,gain[None]]; specs+=[part,part,pl.BlockSpec((1,D),lambda i:(0,0))]
        if low_too: outs.append(jax.ShapeDtypeStruct((T,D),jnp.bfloat16)); out_specs.append(part)
        outs.append(jax.ShapeDtypeStruct((8,D),jnp.float32)); out_specs.append(pl.BlockSpec((8,D),lambda i:(0,0)))
    return pl.pallas_call(partial(back_kernel,terms,len(extras),norm is not None,low_too),grid=(T//CHUNK,),
        out_shape=tuple(outs),in_specs=specs,out_specs=tuple(out_specs),compiler_params=JOIN,
        cost_estimate=pl.CostEstimate(flops=4*terms*T*D*512+T*D*20,bytes_accessed=20*T*D+4*terms*D*512,transcendentals=T),
    )(*args)

PART=16
def outer_kernel(pick,cuts,dp_ref,*refs):
    refs=list(refs); n=len(pick)
    xs=[refs.pop(0) for _ in range(max(pick)+1)]
    gs=[refs.pop(0) for _ in range(n)]
    recv=refs.pop(0)
    outs=[(refs.pop(0),refs.pop(0)) for _ in cuts]
    held=refs.pop(0)
    parts=BS//PART
    for s in range(n):
        held[s]=(lax.dot_general(xs[pick[s]][...],gs[s][...],(((0,),(0,)),((),())),preferred_element_type=jnp.float32)
            +recv[s].astype(jnp.float32)).astype(held.dtype)
    for (give,keep),(first,last,bit) in zip(outs,cuts):
        mine=(dp_ref[0]>>bit)&1
        for s in range(n):
            for i in range(first,last):
                m=s*(last-first)+i-first
                for kk in range(parts//2):
                    low=(kk>>bit<<(bit+1))|(kk&((1<<bit)-1))
                    at=i*BS+low*PART
                    other=pl.ds(pl.multiple_of(at+(1-mine)*(PART<<bit),PART),PART)
                    own=pl.ds(pl.multiple_of(at+mine*(PART<<bit),PART),PART)
                    give[m,kk]=held[s,other,:]
                    keep[m,kk]=held[s,own,:]

def outer_split(xs,pick,gs,recv,cuts,index):
    n=len(gs); D=xs[0].shape[1]; H=gs[0].shape[1]; parts=BS//PART
    vm=pl.BlockSpec(memory_space=pltpu.VMEM)
    shapes=[]
    for first,last,bit in cuts:
        shapes+=[jax.ShapeDtypeStruct((n*(last-first),parts//2,PART,H),jnp.bfloat16)]*2
    out=pl.pallas_call(partial(outer_kernel,pick,cuts),out_shape=tuple(shapes),
        in_specs=[pl.BlockSpec(memory_space=pltpu.SMEM)]+[vm]*(len(xs)+n+1),out_specs=tuple([vm]*len(shapes)),
        scratch_shapes=[pltpu.VMEM((n,D,H),jnp.bfloat16)],
        compiler_params=pltpu.CompilerParams(vmem_limit_bytes=12*1024*1024),
        cost_estimate=pl.CostEstimate(flops=2*n*xs[0].shape[0]*D*H,bytes_accessed=8*n*D*H,transcendentals=0),
    )(index.reshape(1).astype(jnp.int32),*xs,*gs,recv)
    return [(out[2*i],out[2*i+1]) for i in range(len(cuts))]

COLS=(((0,),(0,)),((),()))
def prod(a,b,dims):
    return lax.dot_general(a,b,dims,preferred_element_type=jnp.float32)

def gelu_parts(v):
    t=1.0/(1.0+(0.3275911*0.7071067811865476)*jnp.abs(v))
    e=jnp.exp2(v*v*(-0.5*1.4426950408889634))
    poly=t*(0.5*0.254829592+t*(0.5*-0.284496736+t*(0.5*1.421413741+t*(0.5*-1.453152027+t*(0.5*1.061405429)))))
    tail=poly*e
    phi=jnp.where(v>=0.0,1.0-tail,tail)
    return v*phi,phi+v*e*0.3989422804014327

def feed_kernel(x_ref,g_ref,up_ref,dn_ref,b_ref,down_ref,back_ref,gu_ref,gd_ref,gb_ref,hid_ref,pre_ref):
    rows=x_ref.shape[0]; step=512
    first=pl.program_id(0)==0
    @pl.when(first)
    def _():
        down_ref[...]=jnp.zeros_like(down_ref)
        back_ref[...]=jnp.zeros_like(back_ref)
    up=up_ref[0]; dn=dn_ref[0]; bias=b_ref[0]
    def ahead(r):
        at=slice(r*step,(r+1)*step)
        return prod(x_ref[at,:],up,NN),prod(g_ref[at,:],dn,NT)
    count=rows//step
    nxt=ahead(0)
    total=None
    for r in range(count):
        at=slice(r*step,(r+1)*step)
        pre,gh=nxt
        if r+1<count: nxt=ahead(r+1)
        hidden,slope=gelu_parts(pre+bias)
        hidden=hidden.astype(jnp.bfloat16)
        hid_ref[at,:]=hidden
        gp=(gh.astype(jnp.bfloat16).astype(jnp.float32)*slope).astype(jnp.bfloat16)
        pre_ref[at,:]=gp
        s=jnp.sum(gp.astype(jnp.float32),axis=0,keepdims=True)
        total=s if total is None else total+s
        down_ref[at,:]+=prod(hidden,dn,NN)
        back_ref[at,:]+=prod(gp,up,NT)
    gb_ref[0]=total
    gu_ref[0]=prod(x_ref[...],pre_ref[...],COLS).astype(gu_ref.dtype)
    gd_ref[0]=prod(hid_ref[...],g_ref[...],COLS).astype(gd_ref.dtype)

def feed_forward(x,g,col,row,bias):
    T,D=x.shape; H=col.shape[2]
    f32=jnp.float32; bf=jnp.bfloat16
    once=pl.BlockSpec((T,D),lambda s:(0,0),pipeline_mode=pl.Buffered(1))
    whole=pl.BlockSpec((T,D),lambda s:(0,0))
    return pl.pallas_call(feed_kernel,grid=(4,),
        out_shape=(jax.ShapeDtypeStruct((T,D),f32),jax.ShapeDtypeStruct((T,D),f32),jax.ShapeDtypeStruct((4,D,H),bf),
                   jax.ShapeDtypeStruct((4,H,D),bf),jax.ShapeDtypeStruct((4,1,H),f32)),
        in_specs=[once,once,pl.BlockSpec((1,D,H),lambda s:(s+6,0,0)),pl.BlockSpec((1,H,D),lambda s:(s+2,0,0)),pl.BlockSpec((1,1,H),lambda s:(s,0,0))],
        out_specs=[whole,whole,pl.BlockSpec((1,D,H),lambda s:(s,0,0)),pl.BlockSpec((1,H,D),lambda s:(s,0,0)),pl.BlockSpec((1,1,H),lambda s:(s,0,0))],
        scratch_shapes=[pltpu.VMEM((T,H),bf),pltpu.VMEM((T,H),bf)],
        compiler_params=pltpu.CompilerParams(vmem_limit_bytes=42*1024*1024),
        cost_estimate=pl.CostEstimate(flops=6*2*4*T*D*H,bytes_accessed=4*T*D+8*T*D+16*D*H*2,transcendentals=8*T*H),
    )(x,g,col,row,bias[4:8,None,:])

MESH=pl.DeviceIdType.MESH

def share_kernel(parts, cores, sent_ref, rows_ref, came_ref, total_ref, norm_ref, arrived, own_sem, send_sem, recv_sem, up_send, up_recv, down_send, down_recv):
    here=lax.axis_index("dp"); core=lax.axis_index("mp")
    me=here*cores+core
    everyone=parts*cores
    count=rows_ref.shape[0]
    barrier=pltpu.get_barrier_semaphore()
    def place(at):
        return (at//cores,at%cores)
    def others(n,mine,body):
        for at in range(n):
            @pl.when(mine!=at)
            def _(at=at): body(at)
    others(everyone,me,lambda at: pl.semaphore_signal(barrier,inc=1,device_id=place(at),device_id_type=MESH))
    own=pltpu.make_async_copy(sent_ref.at[here],came_ref.at[here],own_sem)
    own.start()
    pl.semaphore_wait(barrier,everyone-1)
    def up(to):
        return pltpu.make_async_remote_copy(src_ref=rows_ref.at[to],dst_ref=arrived.at[me],send_sem=up_send.at[to],recv_sem=up_recv.at[me],
            device_id=place(to),device_id_type=MESH)
    def down(to):
        return pltpu.make_async_remote_copy(src_ref=total_ref.at[me],dst_ref=total_ref.at[me],send_sem=down_send.at[to],recv_sem=down_recv.at[me],
            device_id=place(to),device_id_type=MESH)
    def block(to):
        return pltpu.make_async_remote_copy(src_ref=sent_ref.at[to],dst_ref=came_ref.at[here],send_sem=send_sem.at[to],recv_sem=recv_sem.at[here],
            device_id=(to,core),device_id_type=MESH)
    def landed(ref,sem,at):
        pltpu.make_async_copy(ref.at[at],ref.at[at],sem.at[at]).wait()
    others(count,me,lambda to: up(to).start())
    others(parts,here,lambda to: block(to).start())
    @pl.when(me<count)
    def _():
        arrived[me]=rows_ref[me]
        others(everyone,me,lambda at: landed(arrived,up_recv,at))
        total_ref[me]=jnp.sum(arrived[...],axis=0)
        others(everyone,me,lambda to: down(to).start())
    others(count,me,lambda to: up(to).wait_send())
    others(count,me,lambda at: landed(total_ref,down_recv,at))
    vectors=total_ref[0:count-1]
    square=jnp.sum(vectors*vectors,axis=0)+total_ref[count-1]
    norm_ref[...]=jnp.broadcast_to(jnp.sqrt(jnp.sum(square,keepdims=True)),norm_ref.shape)
    @pl.when(me<count)
    def _(): others(everyone,me,lambda to: down(to).wait_send())
    def end_block(at):
        block(at).wait_send()
        landed(came_ref,recv_sem,at)
    others(parts,here,end_block)
    own.wait()

def share(sent,square,vectors,cores):
    parts,rows,width=sent.shape
    count=vectors.shape[0]+1
    everyone=parts*cores
    rows_in=jnp.concatenate([vectors,jnp.zeros_like(vectors[:1]).at[0,0].set(square)]).reshape(count,8,-1)
    tile=rows_in.shape[1:]
    vm=pl.BlockSpec(memory_space=pltpu.VMEM)
    dma=pltpu.SemaphoreType.DMA
    came,total,norm=pl.pallas_call(partial(share_kernel,parts,cores),
        out_shape=(jax.ShapeDtypeStruct(sent.shape,sent.dtype),jax.ShapeDtypeStruct(rows_in.shape,jnp.float32),jax.ShapeDtypeStruct((8,128),jnp.float32)),
        in_specs=[vm,vm],out_specs=[vm,vm,vm],
        scratch_shapes=[pltpu.VMEM((everyone,)+tile,jnp.float32),dma,dma((parts,)),dma((parts,)),
            dma((everyone,)),dma((everyone,)),dma((everyone,)),dma((everyone,))],
        compiler_params=pltpu.CompilerParams(collective_id=0,has_side_effects=True,vmem_limit_bytes=6*1024*1024),
    )(sent,rows_in)
    return came,total.reshape(count,-1)[:-1],norm[0,0]

BS=256; STEP=10
weight_rate=0.03; weight_decay=0.01
HI=lax.Precision.HIGHEST
def hdot(a,b,dims,precision=HI):
    return lax.dot_general(a,b,(dims,((),())),precision=precision,preferred_element_type=jnp.float32)
DIM_NN=((1,),(0,)); DIM_NT=((1,),(1,)); DIM_TN=((0,),(0,))

def parts2(a):
    top=a.astype(jnp.bfloat16)
    return top,(a-top.astype(jnp.float32)).astype(jnp.bfloat16)

def dot1(a,b,dims):
    return lax.dot_general(a,b,(dims,((),())),preferred_element_type=jnp.float32)

def dot3(a,b,dims):
    a0,a1=a; b0,b1=b
    return dot1(a0,b0,dims)+(dot1(a0,b1,dims)+dot1(a1,b0,dims))

def soap_kernel(clip_ref,g_ref,first,second,master,left,right,ql_ref,qr_ref,
                first_o,second_o,master_o,copy_o,left_o,right_o,al_o,ar_o,ml_o,mr_o):
    clip=clip_ref[0,0]
    g=g_ref[0]
    ql=ql_ref[0]; qr=qr_ref[0]
    scale=0.05*clip*clip
    left_new=0.95*left[0]+scale*dot1(g,g,DIM_NT)
    left_o[0]=left_new
    al=hdot(left_new,ql,DIM_NN); al_o[0]=al
    ml_o[0]=hdot(al,al,DIM_TN)
    right_new=0.95*right[0]+scale*dot1(g,g,DIM_TN)
    right_o[0]=right_new
    ar=hdot(right_new,qr,DIM_NN); ar_o[0]=ar
    mr_o[0]=hdot(ar,ar,DIM_TN)
    ql2=parts2(ql); qr2=parts2(qr)
    half=dot1(ql2[0],g,DIM_TN)+dot1(ql2[1],g,DIM_TN)
    rot=clip*dot3(parts2(half),qr2,DIM_NN)
    f=0.9*first[0]+0.1*rot; first_o[0]=f
    s=0.99*second[0]+0.01*rot*rot; second_o[0]=s
    ratio=f/(1.0-0.9**STEP)/(jnp.sqrt(s/(1.0-0.99**STEP))+1e-8)
    stepped=dot3(parts2(dot3(ql2,parts2(ratio),DIM_NN)),qr2,DIM_NT)
    m=master[0]-weight_rate*(stepped+weight_decay*master[0])
    master_o[0]=m; copy_o[0]=m.astype(jnp.bfloat16)

def soap_stage(clip,g,first,second,master,left,right,ql,qr):
    n=g.shape[0]
    spec=pl.BlockSpec((1,BS,BS),lambda i:(i,0,0))
    f32=jax.ShapeDtypeStruct((n,BS,BS),jnp.float32)
    return pl.pallas_call(soap_kernel,grid=(n,),
        out_shape=(f32,f32,f32,jax.ShapeDtypeStruct((n,BS,BS),jnp.bfloat16),f32,f32,f32,f32,f32,f32),
        in_specs=[pl.BlockSpec(memory_space=pltpu.SMEM)]+[spec]*8,
        out_specs=[spec]*10,
        compiler_params=pltpu.CompilerParams(vmem_limit_bytes=20*1024*1024),
    )(clip.reshape(1,1),g,first,second,master,left,right,ql,qr)

PW=64
def chol_kernel(al_ref,ar_ref,ml_ref,mr_ref,ql_o,qr_o,work,tile):
    n=al_ref.shape[0]; pairs=n
    def load(m,_):
        work[m]=ml_ref[m]; work[n+m]=mr_ref[m]
        return 0
    lax.fori_loop(0,n,load,0)
    lane=lax.broadcasted_iota(jnp.int32,(1,2*PW),1)
    base=lane//PW*PW
    bigcol=lax.broadcasted_iota(jnp.int32,(PW,BS),1)
    bigrow=lax.broadcasted_iota(jnp.int32,(PW,BS),0)
    lower=lax.broadcasted_iota(jnp.int32,(PW,2*PW),1)%PW<=lax.broadcasted_iota(jnp.int32,(PW,2*PW),0)
    diag=lane-base==lax.broadcasted_iota(jnp.int32,(PW,2*PW),0)
    for p in range(BS//PW):
        lo=p*PW; at=slice(lo,lo+PW)
        for j in range(pairs):
            tile[j]=jnp.concatenate([work[2*j,at,at],work[2*j+1,at,at]],axis=1)
        for quarter in range(4):
            top=quarter*PW//4; height=PW-top
            rows=lax.broadcasted_iota(jnp.int32,(height,2*PW),0)+top
            def step(k,_):
                below=rows>k
                clear=below&(lane-base==k)
                at=jnp.broadcast_to(base+k,(height,2*PW))
                ts=[tile[j,top:,:] for j in range(pairs)]
                rs=[jnp.broadcast_to(tile[j,pl.ds(k,1),:],(8,2*PW)) for j in range(pairs)]
                cs=[jnp.take_along_axis(t,at,axis=1) for t in ts]
                ds=[jnp.take_along_axis(r,at[:8],axis=1) for r in rs]
                us=[(jnp.where(lane-base==k,1.0,r)*(1.0/d))[0:1] for r,d in zip(rs,ds)]
                new=[jnp.where(clear,0.0,t)-jnp.where(below,c,0.0)*u for t,c,u in zip(ts,cs,us)]
                for j in range(pairs): tile[j,top:,:]=new[j]
                return 0
            lax.fori_loop(top,top+PW//4,step,0)
        for j in range(pairs):
            t=tile[j]
            left=jnp.sum(jnp.where(diag&(lane<PW),t,0.0),axis=1,keepdims=True)
            right=jnp.sum(jnp.where(diag&(lane>=PW),t,0.0),axis=1,keepdims=True)
            tile[j]=jnp.where(lower,jnp.where(diag,1.0,t)*lax.rsqrt(jnp.where(lane<PW,left,right)),0.0)
        inside=(bigcol>=lo)&(bigcol<lo+PW)
        eye=jnp.where(bigcol-lo==bigrow,1.0,0.0)
        def apply(j,_):
            both=tile[j]
            for s in range(2):
                m=2*j+s
                r=hdot(both[:,s*PW:(s+1)*PW],jnp.where(inside,eye,work[m,at,:]),DIM_NN)
                work[m,at,:]=r
                if p<BS//PW-1:
                    rest=jnp.where(inside[0:1],0.0,work[m,lo+PW:,:])
                    work[m,lo+PW:,:]=rest-hdot(r[:,lo+PW:],r,DIM_TN)
            return 0
        lax.fori_loop(0,pairs,apply,0,unroll=2 if pairs%2==0 else 1)
    keep=lax.broadcasted_iota(jnp.int32,(BS,BS),1)<=lax.broadcasted_iota(jnp.int32,(BS,BS),0)
    def final(m,_):
        ql_o[m]=dot3(parts2(al_ref[m]),parts2(jnp.where(keep,work[m],0.0)),DIM_NT)
        qr_o[m]=dot3(parts2(ar_ref[m]),parts2(jnp.where(keep,work[n+m],0.0)),DIM_NT)
        return 0
    lax.fori_loop(0,n,final,0)

def chol_stage(al,ar,ml,mr):
    n=al.shape[0]
    f32=jax.ShapeDtypeStruct((n,BS,BS),jnp.float32)
    vm=pl.BlockSpec(memory_space=pltpu.VMEM)
    return pl.pallas_call(chol_kernel,out_shape=(f32,f32),in_specs=[vm]*4,out_specs=[vm]*2,
        scratch_shapes=[pltpu.VMEM((2*n,BS,BS),jnp.float32),pltpu.VMEM((n,PW,2*PW),jnp.float32)],
        compiler_params=pltpu.CompilerParams(vmem_limit_bytes=32*1024*1024))(al,ar,ml,mr)

def soap(clip,g,first,second,master,left,right,ql,qr):
    f,s,m,c,l,r,al,ar,ml,mr=soap_stage(clip,g,first,second,master,left,right,ql,qr)
    lr,rr=chol_stage(al,ar,ml,mr)
    return f,s,m,c,l,r,lr,rr


LEN = 1024
shared_rate = 0.6
split_rate = 0.2
clip_limit = 1.0
SWAP = [(0, 1), (1, 0)]


def adam_step(gradient, first_state, second_state, values, step_rate):
    first_new = 0.9 * first_state + 0.1 * gradient
    second_new = 0.99 * second_state + 0.01 * gradient * gradient
    ratio = first_new / (1.0 - 0.9**STEP) / (jnp.sqrt(second_new / (1.0 - 0.99**STEP)) + 1e-08)
    return (first_new, second_new, values - step_rate * ratio)


def norm_forward(values, gain, shift):
    hat, _ = hat_of(values)
    return (hat * gain + shift).astype(jnp.bfloat16)


def dot32(a, b):
    return jnp.dot(a, b, preferred_element_type=jnp.float32)


def low(a):
    return a.astype(jnp.bfloat16)


def wide(a):
    return a.astype(jnp.float32)


def exchange(array):
    return lax.ppermute(array, "mp", SWAP)


def to_parts(array, parts):
    stacked, height, width = array.shape
    return array.reshape(stacked * height // BS, parts, BS // parts, width)


def tie(*arrays):
    return lax.optimization_barrier(arrays)


class Staged:
    def __init__(self, terms, first_bits):
        parts = terms[0].shape[1]
        bits = parts.bit_length() - 1
        self.parts = parts
        self.terms = [a.reshape((a.shape[0],) + (2,) * bits + a.shape[2:]) for a in terms]
        self.left = list(range(bits - 1, -1, -1))
        self.order = [b for b in first_bits if b < bits] + [b for b in range(bits) if b not in first_bits]
        self.got = None

    @classmethod
    def begun(cls, give, keep, first_bits, parts):
        bits = parts.bit_length() - 1
        self = cls.__new__(cls)
        self.parts = parts
        shape = (give.shape[0],) + (2,) * (bits - 1) + give.shape[2:]
        self.terms = [keep.reshape(shape)]
        b = first_bits[0]
        self.left = [a for a in range(bits - 1, -1, -1) if a != b]
        self.order = list(first_bits[1:]) + [a for a in range(bits) if a not in first_bits]
        self.got = lax.ppermute(give.reshape(shape), "dp", [(i, i ^ (1 << b)) for i in range(parts)])
        return self

    def send(self):
        if not self.order:
            return
        b = self.order.pop(0)
        axis = 1 + self.left.index(b)
        self.left.remove(b)
        mine = (lax.axis_index("dp") >> b) & 1
        give = [lax.dynamic_index_in_dim(a, 1 - mine, axis, keepdims=False) for a in self.terms]
        give = give[0] if len(give) == 1 else low(sum(wide(a) for a in give))
        self.got = lax.ppermute(give, "dp", [(i, i ^ (1 << b)) for i in range(self.parts)])
        self.terms = [lax.dynamic_index_in_dim(a, mine, axis, keepdims=False) for a in self.terms]

    def take(self):
        if self.got is not None:
            self.terms.append(self.got)
            self.terms = [low(sum(wide(a) for a in self.terms))]
            self.got = None

    def finish(self):
        self.take()
        while self.order:
            self.send()
            self.take()
        return self.terms[0]


def checkpoint(anchor, *sums):
    waiting = [s for s in sums if s.got is not None]
    anchor, *got = tie(anchor, *[s.got for s in waiting])
    for s, g in zip(waiting, got):
        s.got = g
        s.take()
        s.send()
    return anchor


def all_sum(array, parts):
    array = array + lax.ppermute(array, "mp", SWAP)
    for b in range(parts.bit_length() - 1):
        array = array + lax.ppermute(array, "dp", [(i, i ^ (1 << b)) for i in range(parts)])
    return array


def slot_order(block_slot):
    numbers = jnp.arange(block_slot.shape[0], dtype=jnp.int32)
    return jnp.sum(jnp.where(block_slot[None, :] == numbers[:, None], numbers[None, :], 0), axis=1)


def on_device(
    parts,
    mp_size,
    tokens,
    memory,
    cotangent,
    bucket,
    target_lengths,
    memory_lengths,
    block_slot,
    col_weights,
    row_weights,
    shared_vectors,
    split_vectors,
    shared_first,
    shared_second,
    split_first,
    split_second,
    slot_first,
    slot_second,
    slot_master,
    slot_left,
    slot_right,
    left_basis,
    right_basis,
):
    core = lax.axis_index("mp")
    aligned = BS // parts == PART
    half = col_weights.shape[2]
    shared = shared_vectors
    own_bucket = lax.dynamic_index_in_dim(bucket, core, 0, keepdims=False)
    own_target = lax.dynamic_index_in_dim(target_lengths, core, 0, keepdims=False)
    own_memory = lax.dynamic_index_in_dim(memory_lengths, core, 0, keepdims=False)
    rows = tokens.shape[0]
    self_at = self_plan(own_bucket, rows)
    cross_at = cross_plan(own_bucket, own_memory, rows, memory.shape[0])
    places = jnp.arange(rows, dtype=jnp.int32)
    size = rows // jnp.left_shift(jnp.int32(1), own_bucket)
    segment = places // size
    live = jnp.any(
        (segment[:, None] == jnp.arange(4, dtype=jnp.int32)[None, :])
        & ((places - segment * size)[:, None] < own_target[None, :]),
        axis=1,
    )
    cols = (col_weights, exchange(col_weights))
    rws = (row_weights, exchange(row_weights))
    splits = (split_vectors, exchange(split_vectors))
    both = (0, 1)

    tokens_wide = wide(tokens)
    normed1 = norm_forward(tokens_wide, shared[0], shared[1])
    query, key, value, mem_key, mem_value, self_out, self_log = ([], [], [], [], [], [], [])
    for h in both:
        query.append(low(dot32(normed1, cols[h][0]) + splits[h][0]))
        key.append(low(dot32(normed1, cols[h][1])))
        value.append(low(dot32(normed1, cols[h][2]) + splits[h][1]))
        mem_key.append(low(dot32(memory, cols[h][4])))
        mem_value.append(low(dot32(memory, cols[h][5]) + splits[h][3]))
        out, log = attention(query[h], key[h], value[h], self_at, True)
        self_out.append(out)
        self_log.append(log)
    resid1, normed2 = join_forward(tokens, self_out, rws, 0, shared[6], shared[2], shared[3])
    cross_query, cross_out, cross_log = ([], [], [])
    for h in both:
        cross_query.append(low(dot32(normed2, cols[h][3]) + splits[h][2]))
        out, log = attention(cross_query[h], mem_key[h], mem_value[h], cross_at, False)
        cross_out.append(out)
        cross_log.append(log)
    resid2, normed3 = join_forward(resid1, cross_out, rws, 1, shared[7], shared[4], shared[5])
    grad_out = jnp.where(live[:, None], cotangent, jnp.zeros_like(cotangent))
    down_peer, back_peer, up_grad, down_grad, up_bias_peer = feed_forward(normed3, grad_out, cols[1], rws[1], splits[1])
    up_peer = exchange(up_grad)
    down_grad_peer = exchange(down_grad)
    down_own, back_own, up_grad, down_grad, up_bias_own = feed_forward(normed3, grad_out, cols[0], rws[0], splits[0])
    output = low(resid2 + (down_own + down_peer) + shared[8])
    up_bias = [up_bias_own[:, 0], up_bias_peer[:, 0]]
    back_own, up_peer, down_grad_peer = tie(back_own, up_peer, down_grad_peer)
    down_sum = Staged([to_parts(down_grad, parts), to_parts(down_grad_peer, parts)], (1, 2, 0))
    up_sum = Staged([to_parts(up_grad, parts), to_parts(up_peer, parts)], (0, 1))
    down_sum.send()
    up_sum.send()
    grad_resid2, grad2, sums3 = join_back(
        None, None, 0, (back_own, back_peer), (resid2, grad_out, shared[4]), low_too=True
    )

    def outer(x, g):
        return low(jnp.einsum("td,te->de", x, g, preferred_element_type=jnp.float32))

    row1_peer = exchange(outer(cross_out[1], grad2))
    row1_own = outer(cross_out[0], grad2)

    def cross_back(h, grad):
        return attention_back(
            cross_query[h], mem_key[h], mem_value[h], grad, cross_out[h], cross_log[h], cross_at, False
        )

    grad_cq, grad_mk, grad_mv = ([None, None], [None, None], [None, None])
    grad = [low(jnp.einsum("td,fd->tf", grad2, rws[h][1], preferred_element_type=jnp.float32)) for h in both]
    grad_cq[1], grad_mk[1], grad_mv[1] = cross_back(1, grad[1])
    cross_peer = exchange(
        jnp.stack([outer(normed2, grad_cq[1]), outer(memory, grad_mk[1]), outer(memory, grad_mv[1])])
    )
    grad[0], cross_peer = tie(checkpoint(grad[0], down_sum, up_sum), cross_peer)
    grad_cq[0], grad_mk[0], grad_mv[0] = cross_back(0, grad[0])
    (grad_cq[0], grad_mk[0], grad_mv[0]), row1_peer = tie(
        checkpoint((grad_cq[0], grad_mk[0], grad_mv[0]), down_sum, up_sum), row1_peer
    )
    if aligned:
        ((give, keep),) = outer_split(
            (normed2, memory), (0, 1, 1), (grad_cq[0], grad_mk[0], grad_mv[0]), cross_peer, ((0, 4, 0),), lax.axis_index("dp")
        )
        cross_sum = Staged.begun(give, keep, (0, 1), parts)
    else:
        cross_own = jnp.stack([outer(normed2, grad_cq[0]), outer(memory, grad_mk[0]), outer(memory, grad_mv[0])])
        cross_sum = Staged([to_parts(cross_own, parts), to_parts(cross_peer, parts)], (0, 1))
        cross_sum.send()
    grad_resid1, grad1, sums2 = join_back(
        [[grad_cq[0]], [grad_cq[1]]], cols, 3, (), (resid1, grad_resid2, shared[2]), low_too=True
    )
    grad1 = checkpoint(grad1, down_sum, up_sum)
    row0_peer = exchange(outer(self_out[1], grad1))
    row0_own = outer(self_out[0], grad1)

    def self_back(h, grad):
        return attention_back(query[h], key[h], value[h], grad, self_out[h], self_log[h], self_at, True)

    grad_q, grad_k, grad_v = ([None, None], [None, None], [None, None])
    grad = [low(jnp.einsum("td,fd->tf", grad1, rws[h][0], preferred_element_type=jnp.float32)) for h in both]
    grad[1], row0_peer = tie(grad[1], row0_peer)
    row_sum = Staged(
        [
            to_parts(jnp.stack([row0_own, row1_own]), parts),
            to_parts(jnp.stack([row0_peer, row1_peer]), parts),
        ],
        (1, 0),
    )
    row_sum.send()
    grad_q[1], grad_k[1], grad_v[1] = self_back(1, grad[1])
    self_peer = exchange(
        jnp.stack([outer(normed1, grad_q[1]), outer(normed1, grad_k[1]), outer(normed1, grad_v[1])])
    )
    grad[0], self_peer = tie(checkpoint(grad[0], down_sum, up_sum, cross_sum, row_sum), self_peer)
    grad_q[0], grad_k[0], grad_v[0] = self_back(0, grad[0])
    grad_q[0], grad_k[0], grad_v[0] = checkpoint((grad_q[0], grad_k[0], grad_v[0]), cross_sum, row_sum)
    if aligned:
        (a, b) = outer_split(
            (normed1,), (0, 0, 0), (grad_q[0], grad_k[0], grad_v[0]), self_peer, ((0, 2, 0), (2, 4, 1)), lax.axis_index("dp")
        )
        (grad_q[0], grad_k[0], grad_v[0]), *a = tie((grad_q[0], grad_k[0], grad_v[0]), *a)
        self_a = Staged.begun(*a, (0, 1), parts)
        self_b = Staged.begun(*b, (1, 0), parts)
    else:
        self_own = jnp.stack([outer(normed1, grad_q[0]), outer(normed1, grad_k[0]), outer(normed1, grad_v[0])])
        self_terms = [to_parts(self_own, parts), to_parts(self_peer, parts)]
        self_terms = [a.reshape((3, 2, -1) + a.shape[1:]).swapaxes(0, 1) for a in self_terms]
        self_terms = [a.reshape((2, -1) + a.shape[3:]) for a in self_terms]
        self_a = Staged([a[0] for a in self_terms], (0, 1))
        self_b = Staged([a[1] for a in self_terms], (1, 0))
        self_a.send()
        self_b.send()
    input_grad, sums1 = join_back(
        [[grad_q[h], grad_k[h], grad_v[h]] for h in both], cols, 0, (), (tokens, grad_resid1, shared[0])
    )
    input_grad, sums1, grad_mk[0] = checkpoint(
        (input_grad, sums1, grad_mk[0]), cross_sum, row_sum, self_a, self_b
    )
    (memory_grad,) = join_back([[grad_mk[h], grad_mv[h]] for h in both], cols, 2)
    memory_grad, sums1 = checkpoint((memory_grad, sums1), cross_sum, row_sum, self_a, self_b)
    self_piece = jnp.stack([a.finish().reshape((3, -1) + (BS // parts, half)) for a in (self_a, self_b)], axis=1)
    self_piece = self_piece.reshape((-1, BS // parts, half))
    cross_piece = cross_sum.finish()
    up_piece = up_sum.finish()
    down_piece = down_sum.finish()
    row_piece = row_sum.finish()

    def column_sum(a):
        return jnp.sum(wide(a), axis=0)

    shared_grad = jnp.concatenate(
        [
            sums1[0:2],
            sums2[0:2],
            sums3[0:2],
            sums2[2:3],
            sums3[2:3],
            column_sum(grad_out)[None],
        ]
    )
    split_grad = [
        jnp.concatenate(
            [
                jnp.stack([column_sum(grad_q[h]), column_sum(grad_v[h]), column_sum(grad_cq[h]), column_sum(grad_mv[h])]),
                up_bias[h],
            ]
        )
        for h in both
    ]
    first = jnp.where(core == 0, split_grad[0], split_grad[1])
    second = jnp.where(core == 0, split_grad[1], split_grad[0])
    vectors = jnp.concatenate([shared_grad, jnp.concatenate([first, second], axis=1)], axis=0)
    def blocks(piece):
        m, rows_in, width = piece.shape
        return (
            piece.reshape(m, rows_in, width // BS, BS).transpose(0, 2, 1, 3).reshape(-1, rows_in, BS)
        )

    pieces = jnp.concatenate(
        [
            blocks(self_piece),
            blocks(cross_piece),
            blocks(up_piece),
            blocks(row_piece),
            blocks(down_piece),
        ],
        axis=0,
    )
    square = jnp.sum(wide(pieces) * wide(pieces))
    owned = slot_first.shape[0]
    part_rows = BS // parts
    sent = jnp.take(pieces, slot_order(block_slot), axis=0)
    if part_rows % 16 == 0 and vectors.shape[0] < parts * mp_size:
        came, vectors, grad_norm = share(sent.reshape(parts, owned * part_rows, BS), square, vectors, mp_size)
    else:
        came = lax.all_to_all(sent.reshape(parts, owned, part_rows, BS), "dp", 0, 0, tiled=True)
        vectors = all_sum(vectors, parts)
        grad_norm = jnp.sqrt(all_sum(square.reshape(1, 1), parts)[0, 0] + jnp.sum(vectors * vectors))
    shared_sum = vectors[:9]
    split_sum = vectors[9:]
    mine = came.reshape(parts, owned, part_rows, BS).transpose(1, 0, 2, 3).reshape(owned, BS, BS)
    clip = clip_limit / jnp.maximum(grad_norm, clip_limit)

    def flat(a):
        return a.reshape(owned, BS, BS)

    updated = soap(
        clip,
        mine,
        flat(slot_first),
        flat(slot_second),
        flat(slot_master),
        flat(slot_left),
        flat(slot_right),
        flat(left_basis),
        flat(right_basis),
    )
    first_moment, second_moment, master_weight, master_copy, left_stat, right_stat, left_rotation, right_rotation = (
        a.reshape(slot_first.shape) for a in updated
    )
    shared_mean, shared_square, shared_values = adam_step(
        shared_sum * clip, shared_first, shared_second, shared_vectors, shared_rate
    )
    split_own = lax.dynamic_slice_in_dim(split_sum, core * half, half, axis=1)
    split_mean, split_square, split_values = adam_step(
        split_own * clip, split_first, split_second, split_vectors, split_rate
    )
    return (
        output,
        input_grad,
        memory_grad,
        first_moment,
        second_moment,
        master_weight,
        master_copy,
        left_stat,
        right_stat,
        left_rotation,
        right_rotation,
        shared_mean,
        shared_square,
        shared_values,
        split_mean,
        split_square,
        split_values,
        grad_norm,
    )


def solution(mesh):
    rows = P(("dp", "mp"), None)
    slots = P("dp", "mp", None, None)
    split = P(None, "mp")
    placed = (
        (rows, rows, rows, P("dp"), P("dp", None), P("dp", None), P())
        + (P(None, None, "mp"), P(None, "mp", None), P(), split, P(), P(), split, split)
        + (slots,) * 7
    )
    return jax.shard_map(
        partial(on_device, mesh.shape["dp"], mesh.shape["mp"]),
        mesh=mesh,
        in_specs=placed,
        out_specs=(rows,) * 3 + (slots,) * 8 + (P(),) * 3 + (split,) * 3 + (P(),),
        check_vma=False,
    )
```

```python
from functools import partial

import jax
import jax.numpy as jnp
from jax import lax
from jax.experimental import pallas as pl
from jax.experimental.pallas import tpu as pltpu
from jax.sharding import PartitionSpec as P

HEAD_DIM=64; TQ=256
SCALE=HEAD_DIM**-0.5
EXPC=SCALE*1.4426950408889634
NEG=-1e30
NT=(((1,),(1,)),((),()))
NN=(((1,),(0,)),((),()))

def rows_of(i,n=1):
    if isinstance(i,int): return slice(i*TQ,(i+n)*TQ)
    return pl.ds(pl.multiple_of(i*TQ,TQ),n*TQ)

def head_cols(h):
    return slice(h*HEAD_DIM,(h+1)*HEAD_DIM)

def lanes_of(pair):
    return pl.ds(pl.multiple_of(pair*128,128),128)

def allowed(causal,limit,j):
    r=lax.broadcasted_iota(jnp.int32,(TQ,TQ),0)
    if causal: return r<=lax.broadcasted_iota(jnp.int32,(TQ,TQ),1)
    return r<limit-j*TQ

def each_case(causal,plan,tiles,pairs,emit):
    def over(n,body):
        def step(i,_):
            body(i)
            return 0
        lax.fori_loop(0,n,step,0)
    for b in range(3):
        count=1<<b; size=tiles>>b
        if b==0 and not causal:
            for n in (size,size//2):
                fits=plan[1]>TQ*size//2 if n==size else plan[1]<=TQ*size//2
                @pl.when((plan[0]==b)&fits)
                def _(n=n):
                    over(pairs,lambda pair: emit(pair,[(0,size,n,plan[1],n-size//2)]))
        else:
            @pl.when(plan[0]==b)
            def _(count=count,size=size):
                if count==1: over(pairs,lambda pair: emit(pair,[(0,size,size,None,size-1)]))
                else: over(pairs,lambda pair: over(count,lambda s: emit(pair,[(s*size,size,size,None if causal else plan[1+s],0)])))

def tile_items(causal,segments):
    out=[]
    for t0,qn,kn,limit,masked in segments:
        for i in range(qn):
            n=i+1 if causal else kn
            out.append((t0+i,t0,n,limit,n-1 if causal else masked))
    return out

def fwd_kernel(causal, tiles, plan, q_ref, k_ref, v_ref, o_ref, l_ref, vt_ref):
    pairs=q_ref.shape[1]//128
    def turn(pair,_):
        vt_ref[pair]=v_ref[:,lanes_of(pair)].astype(jnp.float32).T.astype(jnp.bfloat16)
        return 0
    lax.fori_loop(0,pairs,turn,0)
    def emit(pair,segments):
        lanes=lanes_of(pair)
        items=[(t,h) for t in tile_items(causal,segments) for h in range(2)]
        def scores(item):
            (i,k0,n,limit,masked),h=item
            q=q_ref[rows_of(i),lanes][:,head_cols(h)]
            parts=[]
            for j in range(n):
                s=lax.dot_general(k_ref[rows_of(k0+j),lanes][:,head_cols(h)],q,NT,preferred_element_type=jnp.float32)
                if j>=masked:
                    s=jnp.where(allowed(causal,limit,j),s,NEG)
                parts.append(s)
            return parts
        ahead=scores(items[0])
        held=None
        for c,((i,k0,n,limit,masked),h) in enumerate(items):
            parts=ahead
            if c+1<len(items): ahead=scores(items[c+1])
            top=parts[0].max(axis=0,keepdims=True)
            for s in parts[1:]: top=jnp.maximum(top,s.max(axis=0,keepdims=True))
            total=None; acc=None
            for j,s in enumerate(parts):
                p=jnp.exp2((s-top)*EXPC)
                t=p.sum(axis=0,keepdims=True)
                total=t if total is None else total+t
                a=lax.dot_general(vt_ref[pair,head_cols(h),rows_of(k0+j)],p.astype(jnp.bfloat16),NN,preferred_element_type=jnp.float32)
                acc=a if acc is None else acc+a
            acc=acc*(1.0/total)
            l_ref[pair,h:h+1,rows_of(i)]=top+jnp.log2(total)*(1.0/EXPC)
            if h==0: held=acc
            else: o_ref[rows_of(i),lanes]=jnp.concatenate([held,acc],axis=0).T.astype(o_ref.dtype)
    each_case(causal,plan,tiles,pairs,emit)

VM=pl.BlockSpec(memory_space=pltpu.VMEM)
SM=pl.BlockSpec(memory_space=pltpu.SMEM)

def attention(q,k,v,plan,causal):
    T,W=q.shape; M=k.shape[0]; pairs=W//128; tiles=T//TQ
    return pl.pallas_call(
        partial(fwd_kernel,causal,tiles),
        out_shape=(jax.ShapeDtypeStruct((T,W),jnp.bfloat16),jax.ShapeDtypeStruct((pairs,2,T),jnp.float32)),
        in_specs=[SM,VM,VM,VM],out_specs=[VM,VM],
        scratch_shapes=[pltpu.VMEM((pairs,128,M),jnp.bfloat16)],
        compiler_params=pltpu.CompilerParams(vmem_limit_bytes=8*1024*1024),
        cost_estimate=pl.CostEstimate(flops=4*T*M*W//2,bytes_accessed=8*T*W,transcendentals=T*M*W//128),
    )(plan,q,k,v)

def bwd_kernel(causal, tiles, plan, q_ref, k_ref, v_ref, g_ref, o_ref, l_ref, dq_ref, dk_ref, dv_ref, kt_ref, p_ref, s_ref, d_ref):
    pairs=q_ref.shape[1]//128
    ones=jnp.ones((8,HEAD_DIM),jnp.bfloat16)
    def turn(pair,_):
        lanes=lanes_of(pair)
        kt_ref[pair]=k_ref[:,lanes].astype(jnp.float32).T.astype(jnp.bfloat16)
        prod=g_ref[:,lanes].astype(jnp.float32)*o_ref[:,lanes].astype(jnp.float32)
        top=prod.astype(jnp.bfloat16)
        rest=(prod-top.astype(jnp.float32)).astype(jnp.bfloat16)
        for h in range(2):
            d_ref[pair,h]=(lax.dot_general(ones,top[:,head_cols(h)],NT,preferred_element_type=jnp.float32)
                +lax.dot_general(ones,rest[:,head_cols(h)],NT,preferred_element_type=jnp.float32))
        return 0
    lax.fori_loop(0,pairs,turn,0)
    def emit(pair,segments):
        lanes=lanes_of(pair)
        items=[(i,k0,j,n,limit,masked,h) for i,k0,n,limit,masked in tile_items(causal,segments) for j in range(n) for h in range(2)]
        def products(item):
            i,k0,j,n,limit,masked,h=item
            return (lax.dot_general(k_ref[rows_of(k0+j),lanes][:,head_cols(h)],q_ref[rows_of(i),lanes][:,head_cols(h)],NT,preferred_element_type=jnp.float32),
                    lax.dot_general(v_ref[rows_of(k0+j),lanes][:,head_cols(h)],g_ref[rows_of(i),lanes][:,head_cols(h)],NT,preferred_element_type=jnp.float32))
        ahead=products(items[0])
        acc=[None,None]
        for c,(i,k0,j,n,limit,masked,h) in enumerate(items):
            s,dp=ahead
            if c+1<len(items): ahead=products(items[c+1])
            p=jnp.exp2((s-l_ref[pair,h:h+1,rows_of(i)])*EXPC)
            if j>=masked: p=jnp.where(allowed(causal,limit,j),p,0.0)
            p_ref[h,rows_of(k0+j),rows_of(i)]=p.astype(jnp.bfloat16)
            ds=(p*(dp-d_ref[pair,h,0:1,rows_of(i)])).astype(jnp.bfloat16)
            s_ref[h,rows_of(k0+j),rows_of(i)]=ds
            a=lax.dot_general(kt_ref[pair,head_cols(h),rows_of(k0+j)],ds,NN,preferred_element_type=jnp.float32)
            acc[h]=a if j==0 else acc[h]+a
            if j==n-1 and h==1:
                dq_ref[rows_of(i),lanes]=(jnp.concatenate(acc,axis=0)*SCALE).T.astype(dq_ref.dtype)
        for t0,qn,kn,limit,masked in segments:
            for j in range(qn):
                if j>=kn:
                    dk_ref[rows_of(t0+j),lanes]=jnp.zeros((TQ,128),dk_ref.dtype)
                    dv_ref[rows_of(t0+j),lanes]=jnp.zeros((TQ,128),dv_ref.dtype)
                    continue
                cols=rows_of(t0+j,qn-j) if causal else rows_of(t0,qn)
                both=[]
                for h in range(2):
                    both.append((lax.dot_general(p_ref[h,rows_of(t0+j),cols],g_ref[cols,lanes][:,head_cols(h)],NN,preferred_element_type=jnp.float32),
                                 lax.dot_general(s_ref[h,rows_of(t0+j),cols],q_ref[cols,lanes][:,head_cols(h)],NN,preferred_element_type=jnp.float32)))
                dv_ref[rows_of(t0+j),lanes]=jnp.concatenate([a for a,b in both],axis=1).astype(dv_ref.dtype)
                dk_ref[rows_of(t0+j),lanes]=(jnp.concatenate([b for a,b in both],axis=1)*SCALE).astype(dk_ref.dtype)
    each_case(causal,plan,tiles,pairs,emit)

def attention_back(q,k,v,g,out,logs,plan,causal):
    T,W=q.shape; M=k.shape[0]; pairs=W//128; tiles=T//TQ
    narrow=jax.ShapeDtypeStruct((T,W),jnp.bfloat16)
    return pl.pallas_call(
        partial(bwd_kernel,causal,tiles),
        out_shape=(narrow,jax.ShapeDtypeStruct((M,W),jnp.bfloat16),jax.ShapeDtypeStruct((M,W),jnp.bfloat16)),
        in_specs=[SM]+[VM]*6,out_specs=[VM]*3,
        scratch_shapes=[pltpu.VMEM((pairs,128,M),jnp.bfloat16),pltpu.VMEM((2,M,T),jnp.bfloat16),pltpu.VMEM((2,M,T),jnp.bfloat16),pltpu.VMEM((pairs,2,8,T),jnp.float32)],
        compiler_params=pltpu.CompilerParams(vmem_limit_bytes=14*1024*1024),
        cost_estimate=pl.CostEstimate(flops=10*T*M*W//2,bytes_accessed=14*T*W,transcendentals=T*M*W//128),
    )(plan,q,k,v,g,out,logs)

def self_plan(bucket,T):
    return bucket.reshape(1)

def cross_plan(bucket,lengths,T,M):
    return jnp.concatenate([bucket.reshape(1),lengths])

CHUNK=256
JOIN=pltpu.CompilerParams(vmem_limit_bytes=20*1024*1024)

def hat_of(values):
    centered=values-jnp.mean(values,axis=-1,keepdims=True)
    inverse=lax.rsqrt(jnp.mean(centered*centered,axis=-1,keepdims=True)+1e-05)
    return centered*inverse,inverse

def join_kernel(v_ref,a_ref,b_ref,wa_ref,wb_ref,r_ref,sum_ref,norm_ref):
    product=(lax.dot_general(a_ref[...],wa_ref[0],NN,preferred_element_type=jnp.float32)
        +lax.dot_general(b_ref[...],wb_ref[0],NN,preferred_element_type=jnp.float32))
    values=v_ref[...].astype(jnp.float32)+product+r_ref[0:1,:]
    sum_ref[...]=values
    hat,_=hat_of(values)
    norm_ref[...]=(hat*r_ref[1:2,:]+r_ref[2:3,:]).astype(norm_ref.dtype)

def join_forward(values,halves,rows,index,shift,gain,bias):
    T,D=values.shape; H=halves[0].shape[1]
    part=pl.BlockSpec((CHUNK,D),lambda i:(i,0)); narrow=pl.BlockSpec((CHUNK,H),lambda i:(i,0))
    weight=pl.BlockSpec((1,H,D),lambda i:(index,0,0))
    return pl.pallas_call(join_kernel,grid=(T//CHUNK,),
        out_shape=(jax.ShapeDtypeStruct((T,D),jnp.float32),jax.ShapeDtypeStruct((T,D),jnp.bfloat16)),
        in_specs=[part,narrow,narrow,weight,weight,pl.BlockSpec((3,D),lambda i:(0,0))],out_specs=[part,part],
        compiler_params=JOIN,cost_estimate=pl.CostEstimate(flops=4*T*D*H,bytes_accessed=10*T*D+4*T*H+4*H*D,transcendentals=T),
    )(values,*halves,*rows,jnp.stack([shift,gain,bias]))

def back_kernel(terms,extras,norm,low_too,*refs):
    refs=list(refs)
    take=lambda n: [refs.pop(0) for _ in range(n)]
    gs=take(2*terms); ws=take(2 if terms else 0); ex=take(extras)
    acc=None
    for h in range(2 if terms else 0):
        for s in range(terms):
            a=lax.dot_general(gs[h*terms+s][...],ws[h][s],NT,preferred_element_type=jnp.float32)
            acc=a if acc is None else acc+a
    for e in ex:
        acc=e[...] if acc is None else acc+e[...]
    if not norm:
        refs.pop(0)[...]=acc
        return
    v_ref,g_ref,gain_ref=take(3)
    hat,inverse=hat_of(v_ref[...].astype(jnp.float32))
    inner=acc*gain_ref[...]
    back=inverse*(inner-jnp.mean(inner,axis=-1,keepdims=True)-hat*jnp.mean(inner*hat,axis=-1,keepdims=True))
    new=g_ref[...].astype(jnp.float32)+back
    refs.pop(0)[...]=new
    if low_too: refs.pop(0)[...]=new.astype(jnp.bfloat16)
    sums=refs.pop(0)
    @pl.when(pl.program_id(0)==0)
    def _(): sums[...]=jnp.zeros_like(sums)
    sums[0:1,:]+=jnp.sum(acc*hat,axis=0,keepdims=True)
    sums[1:2,:]+=jnp.sum(acc,axis=0,keepdims=True)
    sums[2:3,:]+=jnp.sum(new,axis=0,keepdims=True)

def join_back(gs,cols,index,extras=(),norm=None,low_too=False):
    terms=len(gs[0]) if gs else 0
    T,D=extras[0].shape if extras else (gs[0][0].shape[0],cols[0].shape[1])
    part=pl.BlockSpec((CHUNK,D),lambda i:(i,0))
    args=[]; specs=[]
    if terms:
        H=gs[0][0].shape[1]
        for h in range(2):
            for g in gs[h]: args.append(g); specs.append(pl.BlockSpec((CHUNK,H),lambda i:(i,0)))
        for w in cols: args.append(w); specs.append(pl.BlockSpec((terms,D,H),lambda i:(index,0,0),pipeline_mode=pl.Buffered(1)))
    for e in extras: args.append(e); specs.append(part)
    full=jax.ShapeDtypeStruct((T,D),jnp.float32)
    outs=[full]; out_specs=[part]
    if norm:
        values,grad,gain=norm
        args+=[values,grad,gain[None]]; specs+=[part,part,pl.BlockSpec((1,D),lambda i:(0,0))]
        if low_too: outs.append(jax.ShapeDtypeStruct((T,D),jnp.bfloat16)); out_specs.append(part)
        outs.append(jax.ShapeDtypeStruct((8,D),jnp.float32)); out_specs.append(pl.BlockSpec((8,D),lambda i:(0,0)))
    return pl.pallas_call(partial(back_kernel,terms,len(extras),norm is not None,low_too),grid=(T//CHUNK,),
        out_shape=tuple(outs),in_specs=specs,out_specs=tuple(out_specs),compiler_params=JOIN,
        cost_estimate=pl.CostEstimate(flops=4*terms*T*D*512+T*D*20,bytes_accessed=20*T*D+4*terms*D*512,transcendentals=T),
    )(*args)

PART=16
def outer_kernel(pick,cuts,dp_ref,*refs):
    refs=list(refs); n=len(pick)
    xs=[refs.pop(0) for _ in range(max(pick)+1)]
    gs=[refs.pop(0) for _ in range(n)]
    recv=refs.pop(0)
    outs=[(refs.pop(0),refs.pop(0)) for _ in cuts]
    held=refs.pop(0)
    parts=BS//PART
    for s in range(n):
        held[s]=(lax.dot_general(xs[pick[s]][...],gs[s][...],(((0,),(0,)),((),())),preferred_element_type=jnp.float32)
            +recv[s].astype(jnp.float32)).astype(held.dtype)
    for (give,keep),(first,last,bit) in zip(outs,cuts):
        mine=(dp_ref[0]>>bit)&1
        for s in range(n):
            for i in range(first,last):
                m=s*(last-first)+i-first
                for kk in range(parts//2):
                    low=(kk>>bit<<(bit+1))|(kk&((1<<bit)-1))
                    at=i*BS+low*PART
                    other=pl.ds(pl.multiple_of(at+(1-mine)*(PART<<bit),PART),PART)
                    own=pl.ds(pl.multiple_of(at+mine*(PART<<bit),PART),PART)
                    give[kk,m]=held[s,other,:]
                    keep[kk,m]=held[s,own,:]

def outer_split(xs,pick,gs,recv,cuts,index):
    n=len(gs); D=xs[0].shape[1]; H=gs[0].shape[1]; parts=BS//PART
    vm=pl.BlockSpec(memory_space=pltpu.VMEM)
    shapes=[]
    for first,last,bit in cuts:
        shapes+=[jax.ShapeDtypeStruct((parts//2,n*(last-first),PART,H),jnp.bfloat16)]*2
    out=pl.pallas_call(partial(outer_kernel,pick,cuts),out_shape=tuple(shapes),
        in_specs=[pl.BlockSpec(memory_space=pltpu.SMEM)]+[vm]*(len(xs)+n+1),out_specs=tuple([vm]*len(shapes)),
        scratch_shapes=[pltpu.VMEM((n,D,H),jnp.bfloat16)],
        compiler_params=pltpu.CompilerParams(vmem_limit_bytes=12*1024*1024),
        cost_estimate=pl.CostEstimate(flops=2*n*xs[0].shape[0]*D*H,bytes_accessed=8*n*D*H,transcendentals=0),
    )(index.reshape(1).astype(jnp.int32),*xs,*gs,recv)
    return [(out[2*i],out[2*i+1]) for i in range(len(cuts))]

def plain_kernel(pick,*refs):
    xs,gs,out=refs[:max(pick)+1],refs[max(pick)+1:-1],refs[-1]
    for s,x in enumerate(pick):
        out[s]=lax.dot_general(xs[x][...],gs[s][...],(((0,),(0,)),((),())),preferred_element_type=jnp.float32).astype(out.dtype)

def outer_plain(xs,pick,gs):
    n=len(gs); D=xs[0].shape[1]; H=gs[0].shape[1]
    vm=pl.BlockSpec(memory_space=pltpu.VMEM)
    return pl.pallas_call(partial(plain_kernel,pick),out_shape=jax.ShapeDtypeStruct((n,D,H),jnp.bfloat16),
        in_specs=[vm]*(len(xs)+n),out_specs=vm,compiler_params=pltpu.CompilerParams(vmem_limit_bytes=12*1024*1024),
        cost_estimate=pl.CostEstimate(flops=2*n*xs[0].shape[0]*D*H,bytes_accessed=8*n*D*H,transcendentals=0),
    )(*xs,*gs)

COLS=(((0,),(0,)),((),()))
def prod(a,b,dims):
    return lax.dot_general(a,b,dims,preferred_element_type=jnp.float32)

def gelu_parts(v):
    t=1.0/(1.0+(0.3275911*0.7071067811865476)*jnp.abs(v))
    e=jnp.exp2(v*v*(-0.5*1.4426950408889634))
    poly=t*(0.5*0.254829592+t*(0.5*-0.284496736+t*(0.5*1.421413741+t*(0.5*-1.453152027+t*(0.5*1.061405429)))))
    tail=poly*e
    phi=jnp.where(v>=0.0,1.0-tail,tail)
    return v*phi,phi+v*e*0.3989422804014327

UP_BITS=(0,1,2,3)
DOWN_BITS=(1,2,0,3)
def spread(ref,value,order):
    if len(ref.shape)==3:
        ref[0]=value
        return
    for i in range(value.shape[0]//BS):
        for p in range(BS//PART):
            at=i*BS+p*PART
            ref[tuple((p>>b)&1 for b in order)+(0,i)]=value[at:at+PART,:]

def feed_kernel(x_ref,g_ref,up_ref,dn_ref,b_ref,down_ref,back_ref,gu_ref,gd_ref,gb_ref,hid_ref,pre_ref):
    rows=x_ref.shape[0]; step=512
    first=pl.program_id(0)==0
    @pl.when(first)
    def _():
        down_ref[...]=jnp.zeros_like(down_ref)
        back_ref[...]=jnp.zeros_like(back_ref)
    up=up_ref[0]; dn=dn_ref[0]; bias=b_ref[0]
    def ahead(r):
        at=slice(r*step,(r+1)*step)
        return prod(x_ref[at,:],up,NN),prod(g_ref[at,:],dn,NT)
    count=rows//step
    nxt=ahead(0)
    total=None
    for r in range(count):
        at=slice(r*step,(r+1)*step)
        pre,gh=nxt
        if r+1<count: nxt=ahead(r+1)
        hidden,slope=gelu_parts(pre+bias)
        hidden=hidden.astype(jnp.bfloat16)
        hid_ref[at,:]=hidden
        gp=(gh.astype(jnp.bfloat16).astype(jnp.float32)*slope).astype(jnp.bfloat16)
        pre_ref[at,:]=gp
        s=jnp.sum(gp.astype(jnp.float32),axis=0,keepdims=True)
        total=s if total is None else total+s
        down_ref[at,:]+=prod(hidden,dn,NN)
        back_ref[at,:]+=prod(gp,up,NT)
    gb_ref[0]=total
    spread(gu_ref,prod(x_ref[...],pre_ref[...],COLS).astype(gu_ref.dtype),UP_BITS)
    spread(gd_ref,prod(hid_ref[...],g_ref[...],COLS).astype(gd_ref.dtype),DOWN_BITS)

def feed_forward(x,g,col,row,bias,aligned):
    T,D=x.shape; H=col.shape[2]
    f32=jnp.float32; bf=jnp.bfloat16
    once=pl.BlockSpec((T,D),lambda s:(0,0),pipeline_mode=pl.Buffered(1))
    whole=pl.BlockSpec((T,D),lambda s:(0,0))
    def grad(height,width):
        if not aligned: return jax.ShapeDtypeStruct((4,height,width),bf),pl.BlockSpec((1,height,width),lambda s:(s,0,0))
        shape=(2,2,2,2,4,height//BS,PART,width)
        return jax.ShapeDtypeStruct(shape,bf),pl.BlockSpec(shape[:4]+(1,)+shape[5:],lambda s:(0,0,0,0,s,0,0,0))
    (gu,gu_spec),(gd,gd_spec)=grad(D,H),grad(H,D)
    return pl.pallas_call(feed_kernel,grid=(4,),
        out_shape=(jax.ShapeDtypeStruct((T,D),f32),jax.ShapeDtypeStruct((T,D),f32),gu,
                   gd,jax.ShapeDtypeStruct((4,1,H),f32)),
        in_specs=[once,once,pl.BlockSpec((1,D,H),lambda s:(s+6,0,0)),pl.BlockSpec((1,H,D),lambda s:(s+2,0,0)),pl.BlockSpec((1,1,H),lambda s:(s,0,0))],
        out_specs=[whole,whole,gu_spec,gd_spec,pl.BlockSpec((1,1,H),lambda s:(s,0,0))],
        scratch_shapes=[pltpu.VMEM((T,H),bf),pltpu.VMEM((T,H),bf)],
        compiler_params=pltpu.CompilerParams(vmem_limit_bytes=42*1024*1024),
        cost_estimate=pl.CostEstimate(flops=6*2*4*T*D*H,bytes_accessed=4*T*D+8*T*D+16*D*H*2,transcendentals=8*T*H),
    )(x,g,col,row,bias[4:8,None,:])

MESH=pl.DeviceIdType.MESH

def share_kernel(parts, cores, sent_ref, rows_ref, came_ref, total_ref, norm_ref, arrived, own_sem, send_sem, recv_sem, up_send, up_recv, down_send, down_recv):
    here=lax.axis_index("dp"); core=lax.axis_index("mp")
    me=here*cores+core
    everyone=parts*cores
    count=rows_ref.shape[0]
    barrier=pltpu.get_barrier_semaphore()
    def place(at):
        return (at//cores,at%cores)
    def others(n,mine,body):
        for at in range(n):
            @pl.when(mine!=at)
            def _(at=at): body(at)
    others(everyone,me,lambda at: pl.semaphore_signal(barrier,inc=1,device_id=place(at),device_id_type=MESH))
    own=pltpu.make_async_copy(sent_ref.at[here],came_ref.at[here],own_sem)
    own.start()
    pl.semaphore_wait(barrier,everyone-1)
    def up(to):
        return pltpu.make_async_remote_copy(src_ref=rows_ref.at[to],dst_ref=arrived.at[me],send_sem=up_send.at[to],recv_sem=up_recv.at[me],
            device_id=place(to),device_id_type=MESH)
    def down(to):
        return pltpu.make_async_remote_copy(src_ref=total_ref.at[me],dst_ref=total_ref.at[me],send_sem=down_send.at[to],recv_sem=down_recv.at[me],
            device_id=place(to),device_id_type=MESH)
    def block(to):
        return pltpu.make_async_remote_copy(src_ref=sent_ref.at[to],dst_ref=came_ref.at[here],send_sem=send_sem.at[to],recv_sem=recv_sem.at[here],
            device_id=(to,core),device_id_type=MESH)
    def landed(ref,sem,at):
        pltpu.make_async_copy(ref.at[at],ref.at[at],sem.at[at]).wait()
    others(count,me,lambda to: up(to).start())
    others(parts,here,lambda to: block(to).start())
    @pl.when(me<count)
    def _():
        arrived[me]=rows_ref[me]
        others(everyone,me,lambda at: landed(arrived,up_recv,at))
        total_ref[me]=jnp.sum(arrived[...],axis=0)
        others(everyone,me,lambda to: down(to).start())
    others(count,me,lambda to: up(to).wait_send())
    others(count,me,lambda at: landed(total_ref,down_recv,at))
    vectors=total_ref[0:count-1]
    square=jnp.sum(vectors*vectors,axis=0)+total_ref[count-1]
    norm_ref[...]=jnp.broadcast_to(jnp.sqrt(jnp.sum(square,keepdims=True)),norm_ref.shape)
    @pl.when(me<count)
    def _(): others(everyone,me,lambda to: down(to).wait_send())
    def end_block(at):
        block(at).wait_send()
        landed(came_ref,recv_sem,at)
    others(parts,here,end_block)
    own.wait()

def share(sent,square,vectors,cores):
    parts,rows,width=sent.shape
    count=vectors.shape[0]+1
    everyone=parts*cores
    rows_in=jnp.concatenate([vectors,jnp.zeros_like(vectors[:1]).at[0,0].set(square)]).reshape(count,8,-1)
    tile=rows_in.shape[1:]
    vm=pl.BlockSpec(memory_space=pltpu.VMEM)
    dma=pltpu.SemaphoreType.DMA
    came,total,norm=pl.pallas_call(partial(share_kernel,parts,cores),
        out_shape=(jax.ShapeDtypeStruct(sent.shape,sent.dtype),jax.ShapeDtypeStruct(rows_in.shape,jnp.float32),jax.ShapeDtypeStruct((8,128),jnp.float32)),
        in_specs=[vm,vm],out_specs=[vm,vm,vm],
        scratch_shapes=[pltpu.VMEM((everyone,)+tile,jnp.float32),dma,dma((parts,)),dma((parts,)),
            dma((everyone,)),dma((everyone,)),dma((everyone,)),dma((everyone,))],
        compiler_params=pltpu.CompilerParams(collective_id=0,has_side_effects=True,vmem_limit_bytes=6*1024*1024),
    )(sent,rows_in)
    return came,total.reshape(count,-1)[:-1],norm[0,0]

BS=256; STEP=10
weight_rate=0.03; weight_decay=0.01
HI=lax.Precision.HIGHEST
def hdot(a,b,dims,precision=HI):
    return lax.dot_general(a,b,(dims,((),())),precision=precision,preferred_element_type=jnp.float32)
DIM_NN=((1,),(0,)); DIM_NT=((1,),(1,)); DIM_TN=((0,),(0,))

def parts2(a):
    top=a.astype(jnp.bfloat16)
    return top,(a-top.astype(jnp.float32)).astype(jnp.bfloat16)

def dot1(a,b,dims):
    return lax.dot_general(a,b,(dims,((),())),preferred_element_type=jnp.float32)

def dot3(a,b,dims):
    a0,a1=a; b0,b1=b
    return dot1(a0,b0,dims)+(dot1(a0,b1,dims)+dot1(a1,b0,dims))

def soap_kernel(clip_ref,g_ref,first,second,master,left,right,ql_ref,qr_ref,
                first_o,second_o,master_o,copy_o,left_o,right_o,al_o,ar_o,ml_o,mr_o):
    clip=clip_ref[0,0]
    g=g_ref[0]
    ql=ql_ref[0]; qr=qr_ref[0]
    scale=0.05*clip*clip
    left_new=0.95*left[0]+scale*dot1(g,g,DIM_NT)
    left_o[0]=left_new
    al=hdot(left_new,ql,DIM_NN); al_o[0]=al
    ml_o[0]=hdot(al,al,DIM_TN)
    right_new=0.95*right[0]+scale*dot1(g,g,DIM_TN)
    right_o[0]=right_new
    ar=hdot(right_new,qr,DIM_NN); ar_o[0]=ar
    mr_o[0]=hdot(ar,ar,DIM_TN)
    ql2=parts2(ql); qr2=parts2(qr)
    half=dot1(ql2[0],g,DIM_TN)+dot1(ql2[1],g,DIM_TN)
    rot=clip*dot3(parts2(half),qr2,DIM_NN)
    f=0.9*first[0]+0.1*rot; first_o[0]=f
    s=0.99*second[0]+0.01*rot*rot; second_o[0]=s
    ratio=f/(1.0-0.9**STEP)/(jnp.sqrt(s/(1.0-0.99**STEP))+1e-8)
    stepped=dot3(parts2(dot3(ql2,parts2(ratio),DIM_NN)),qr2,DIM_NT)
    m=master[0]-weight_rate*(stepped+weight_decay*master[0])
    master_o[0]=m; copy_o[0]=m.astype(jnp.bfloat16)

def soap_stage(clip,g,first,second,master,left,right,ql,qr):
    n=g.shape[0]
    spec=pl.BlockSpec((1,BS,BS),lambda i:(i,0,0))
    f32=jax.ShapeDtypeStruct((n,BS,BS),jnp.float32)
    return pl.pallas_call(soap_kernel,grid=(n,),
        out_shape=(f32,f32,f32,jax.ShapeDtypeStruct((n,BS,BS),jnp.bfloat16),f32,f32,f32,f32,f32,f32),
        in_specs=[pl.BlockSpec(memory_space=pltpu.SMEM)]+[spec]*8,
        out_specs=[spec]*10,
        compiler_params=pltpu.CompilerParams(vmem_limit_bytes=48*1024*1024),
    )(clip.reshape(1,1),g,first,second,master,left,right,ql,qr)

PW=64
def chol_kernel(al_ref,ar_ref,ml_ref,mr_ref,ql_o,qr_o,work,tile):
    n=al_ref.shape[0]; pairs=n
    def load(m,_):
        work[m]=ml_ref[m]; work[n+m]=mr_ref[m]
        return 0
    lax.fori_loop(0,n,load,0)
    lane=lax.broadcasted_iota(jnp.int32,(1,2*PW),1)
    base=lane//PW*PW
    bigcol=lax.broadcasted_iota(jnp.int32,(PW,BS),1)
    bigrow=lax.broadcasted_iota(jnp.int32,(PW,BS),0)
    lower=lax.broadcasted_iota(jnp.int32,(PW,2*PW),1)%PW<=lax.broadcasted_iota(jnp.int32,(PW,2*PW),0)
    diag=lane-base==lax.broadcasted_iota(jnp.int32,(PW,2*PW),0)
    odd=lax.broadcasted_iota(jnp.int32,(PW,2*PW),0)%2==1
    beside=odd&(lane-base==lax.broadcasted_iota(jnp.int32,(PW,2*PW),0)-1)
    for p in range(BS//PW):
        lo=p*PW; at=slice(lo,lo+PW)
        for j in range(pairs):
            tile[j]=jnp.concatenate([work[2*j,at,at],work[2*j+1,at,at]],axis=1)
        for quarter in range(4):
            top=quarter*PW//4; height=PW-top
            rows=lax.broadcasted_iota(jnp.int32,(height,2*PW),0)+top
            def step(half,_):
                k=2*half
                below=rows>k+1
                here=lane-base
                clear=below&((here==k)|(here==k+1))
                at=jnp.broadcast_to(base+k,(height,2*PW))
                ts=[tile[j,top:,:] for j in range(pairs)]
                r1s=[jnp.broadcast_to(tile[j,pl.ds(k,1),:],(8,2*PW)) for j in range(pairs)]
                r2s=[jnp.broadcast_to(tile[j,pl.ds(k+1,1),:],(8,2*PW)) for j in range(pairs)]
                c1s=[jnp.take_along_axis(t,at,axis=1) for t in ts]
                c2s=[jnp.take_along_axis(t,at+1,axis=1) for t in ts]
                new=[]
                for t,c1,c2,r1,r2 in zip(ts,c1s,c2s,r1s,r2s):
                    p=jnp.take_along_axis(r1,at[:8],axis=1)
                    q=jnp.take_along_axis(r1,at[:8]+1,axis=1)
                    w=jnp.take_along_axis(r2,at[:8]+1,axis=1)
                    scale=1.0/(p*w-q*q)
                    r1=jnp.where(here==k,1.0,jnp.where(here==k+1,0.0,r1))
                    r2=jnp.where(here==k+1,1.0,jnp.where(here==k,0.0,r2))
                    u1=((w*r1-q*r2)*scale)[0:1]
                    u2=((p*r2-q*r1)*scale)[0:1]
                    new.append(jnp.where(clear,0.0,t)-jnp.where(below,c1,0.0)*u1-jnp.where(below,c2,0.0)*u2)
                for j in range(pairs): tile[j,top:,:]=new[j]
                return 0
            lax.fori_loop(top//2,(top+PW//4)//2,step,0)
        for j in range(pairs):
            t=tile[j]
            def column(mask):
                return jnp.where(lane<PW,jnp.sum(jnp.where(mask&(lane<PW),t,0.0),axis=1,keepdims=True),
                    jnp.sum(jnp.where(mask&(lane>=PW),t,0.0),axis=1,keepdims=True))
            own=column(diag)
            cross=column(beside)
            unit=jnp.where(diag,1.0,jnp.where(lower&~beside,t,0.0))
            ratio=jnp.where(odd,cross/pltpu.roll(own,1,0),0.0)
            tile[j]=(unit-ratio*pltpu.roll(unit,1,0))*lax.rsqrt(own-ratio*cross)
        inside=(bigcol>=lo)&(bigcol<lo+PW)
        eye=jnp.where(bigcol-lo==bigrow,1.0,0.0)
        def apply(j,_):
            both=tile[j]
            for s in range(2):
                m=2*j+s
                r=hdot(both[:,s*PW:(s+1)*PW],jnp.where(inside,eye,work[m,at,:]),DIM_NN)
                work[m,at,:]=r
                if p<BS//PW-1:
                    rest=jnp.where(inside[0:1],0.0,work[m,lo+PW:,:])
                    work[m,lo+PW:,:]=rest-hdot(r[:,lo+PW:],r,DIM_TN)
            return 0
        lax.fori_loop(0,pairs,apply,0,unroll=2 if pairs%2==0 else 1)
    keep=lax.broadcasted_iota(jnp.int32,(BS,BS),1)<=lax.broadcasted_iota(jnp.int32,(BS,BS),0)
    def final(m,_):
        ql_o[m]=dot3(parts2(al_ref[m]),parts2(jnp.where(keep,work[m],0.0)),DIM_NT)
        qr_o[m]=dot3(parts2(ar_ref[m]),parts2(jnp.where(keep,work[n+m],0.0)),DIM_NT)
        return 0
    lax.fori_loop(0,n,final,0)

def chol_stage(al,ar,ml,mr):
    n=al.shape[0]
    f32=jax.ShapeDtypeStruct((n,BS,BS),jnp.float32)
    vm=pl.BlockSpec(memory_space=pltpu.VMEM)
    return pl.pallas_call(chol_kernel,out_shape=(f32,f32),in_specs=[vm]*4,out_specs=[vm]*2,
        scratch_shapes=[pltpu.VMEM((2*n,BS,BS),jnp.float32),pltpu.VMEM((n,PW,2*PW),jnp.float32)],
        compiler_params=pltpu.CompilerParams(vmem_limit_bytes=32*1024*1024))(al,ar,ml,mr)

def soap(clip,g,first,second,master,left,right,ql,qr):
    f,s,m,c,l,r,al,ar,ml,mr=soap_stage(clip,g,first,second,master,left,right,ql,qr)
    lr,rr=chol_stage(al,ar,ml,mr)
    return f,s,m,c,l,r,lr,rr


LEN = 1024
shared_rate = 0.6
split_rate = 0.2
clip_limit = 1.0
SWAP = [(0, 1), (1, 0)]


def adam_step(gradient, first_state, second_state, values, step_rate):
    first_new = 0.9 * first_state + 0.1 * gradient
    second_new = 0.99 * second_state + 0.01 * gradient * gradient
    ratio = first_new / (1.0 - 0.9**STEP) / (jnp.sqrt(second_new / (1.0 - 0.99**STEP)) + 1e-08)
    return (first_new, second_new, values - step_rate * ratio)


def norm_forward(values, gain, shift):
    hat, _ = hat_of(values)
    return (hat * gain + shift).astype(jnp.bfloat16)


def dot32(a, b):
    return jnp.dot(a, b, preferred_element_type=jnp.float32)


def low(a):
    return a.astype(jnp.bfloat16)


def wide(a):
    return a.astype(jnp.float32)


def exchange(array):
    return lax.ppermute(array, "mp", SWAP)


def to_parts(array, parts):
    stacked, height, width = array.shape
    return array.reshape(stacked * height // BS, parts, BS // parts, width)


def tie(*arrays):
    return lax.optimization_barrier(arrays)


class Staged:
    def __init__(self, terms, first_bits, led=False):
        parts = 2 ** len(first_bits) if led else terms[0].shape[1]
        bits = parts.bit_length() - 1
        self.parts = parts
        self.order = list(first_bits) + [b for b in range(bits) if b not in first_bits]
        self.order = [b for b in self.order if b < bits]
        self.left = list(self.order) if led else list(range(bits - 1, -1, -1))
        self.start = 0 if led else 1
        if led:
            self.terms = [a.reshape((2,) * bits + (-1,) + a.shape[-2:]) for a in terms]
        else:
            self.terms = [a.reshape((a.shape[0],) + (2,) * bits + a.shape[2:]) for a in terms]
        self.got = None

    @classmethod
    def begun(cls, give, keep, first_bits, parts):
        bits = parts.bit_length() - 1
        self = cls.__new__(cls)
        self.parts = parts
        shape = (2,) * (bits - 1) + give.shape[1:]
        self.terms = [keep.reshape(shape)]
        b = first_bits[0]
        self.left = [a for a in range(bits - 1, -1, -1) if a != b]
        self.start = 0
        self.order = list(first_bits[1:]) + [a for a in range(bits) if a not in first_bits]
        self.got = lax.ppermute(give.reshape(shape), "dp", [(i, i ^ (1 << b)) for i in range(parts)])
        return self

    def send(self):
        if not self.order:
            return
        b = self.order.pop(0)
        axis = self.start + self.left.index(b)
        self.left.remove(b)
        mine = (lax.axis_index("dp") >> b) & 1
        give = [lax.dynamic_index_in_dim(a, 1 - mine, axis, keepdims=False) for a in self.terms]
        give = give[0] if len(give) == 1 else low(sum(wide(a) for a in give))
        self.got = lax.ppermute(give, "dp", [(i, i ^ (1 << b)) for i in range(self.parts)])
        self.terms = [lax.dynamic_index_in_dim(a, mine, axis, keepdims=False) for a in self.terms]

    def take(self):
        if self.got is not None:
            self.terms.append(self.got)
            self.terms = [low(sum(wide(a) for a in self.terms))]
            self.got = None

    def finish(self):
        self.take()
        while self.order:
            self.send()
            self.take()
        return self.terms[0]


def checkpoint(anchor, *sums):
    waiting = [s for s in sums if s.got is not None]
    anchor, *got = tie(anchor, *[s.got for s in waiting])
    for s, g in zip(waiting, got):
        s.got = g
        s.take()
        s.send()
    return anchor


def all_sum(array, parts):
    array = array + lax.ppermute(array, "mp", SWAP)
    for b in range(parts.bit_length() - 1):
        array = array + lax.ppermute(array, "dp", [(i, i ^ (1 << b)) for i in range(parts)])
    return array


def slot_order(block_slot):
    numbers = jnp.arange(block_slot.shape[0], dtype=jnp.int32)
    return jnp.sum(jnp.where(block_slot[None, :] == numbers[:, None], numbers[None, :], 0), axis=1)


def on_device(
    parts,
    mp_size,
    tokens,
    memory,
    cotangent,
    bucket,
    target_lengths,
    memory_lengths,
    block_slot,
    col_weights,
    row_weights,
    shared_vectors,
    split_vectors,
    shared_first,
    shared_second,
    split_first,
    split_second,
    slot_first,
    slot_second,
    slot_master,
    slot_left,
    slot_right,
    left_basis,
    right_basis,
):
    core = lax.axis_index("mp")
    aligned = BS // parts == PART
    half = col_weights.shape[2]
    shared = shared_vectors
    own_bucket = lax.dynamic_index_in_dim(bucket, core, 0, keepdims=False)
    own_target = lax.dynamic_index_in_dim(target_lengths, core, 0, keepdims=False)
    own_memory = lax.dynamic_index_in_dim(memory_lengths, core, 0, keepdims=False)
    rows = tokens.shape[0]
    self_at = self_plan(own_bucket, rows)
    cross_at = cross_plan(own_bucket, own_memory, rows, memory.shape[0])
    places = jnp.arange(rows, dtype=jnp.int32)
    size = rows // jnp.left_shift(jnp.int32(1), own_bucket)
    segment = places // size
    live = jnp.any(
        (segment[:, None] == jnp.arange(4, dtype=jnp.int32)[None, :])
        & ((places - segment * size)[:, None] < own_target[None, :]),
        axis=1,
    )
    cols = (col_weights, exchange(col_weights))
    rws = (row_weights, exchange(row_weights))
    splits = (split_vectors, exchange(split_vectors))
    both = (0, 1)

    tokens_wide = wide(tokens)
    normed1 = norm_forward(tokens_wide, shared[0], shared[1])
    query, key, value, mem_key, mem_value, self_out, self_log = ([], [], [], [], [], [], [])
    for h in both:
        query.append(low(dot32(normed1, cols[h][0]) + splits[h][0]))
        key.append(low(dot32(normed1, cols[h][1])))
        value.append(low(dot32(normed1, cols[h][2]) + splits[h][1]))
        mem_key.append(low(dot32(memory, cols[h][4])))
        mem_value.append(low(dot32(memory, cols[h][5]) + splits[h][3]))
        out, log = attention(query[h], key[h], value[h], self_at, True)
        self_out.append(out)
        self_log.append(log)
    resid1, normed2 = join_forward(tokens, self_out, rws, 0, shared[6], shared[2], shared[3])
    cross_query, cross_out, cross_log = ([], [], [])
    for h in both:
        cross_query.append(low(dot32(normed2, cols[h][3]) + splits[h][2]))
        out, log = attention(cross_query[h], mem_key[h], mem_value[h], cross_at, False)
        cross_out.append(out)
        cross_log.append(log)
    resid2, normed3 = join_forward(resid1, cross_out, rws, 1, shared[7], shared[4], shared[5])
    grad_out = jnp.where(live[:, None], cotangent, jnp.zeros_like(cotangent))
    down_peer, back_peer, up_grad, down_grad, up_bias_peer = feed_forward(normed3, grad_out, cols[1], rws[1], splits[1], aligned)
    up_peer = exchange(up_grad)
    down_grad_peer = exchange(down_grad)
    down_own, back_own, up_grad, down_grad, up_bias_own = feed_forward(normed3, grad_out, cols[0], rws[0], splits[0], aligned)
    output = low(resid2 + (down_own + down_peer) + shared[8])
    up_bias = [up_bias_own[:, 0], up_bias_peer[:, 0]]
    back_own, up_peer, down_grad_peer = tie(back_own, up_peer, down_grad_peer)
    if aligned:
        down_sum = Staged([down_grad, down_grad_peer], DOWN_BITS, led=True)
        up_sum = Staged([up_grad, up_peer], UP_BITS, led=True)
    else:
        down_sum = Staged([to_parts(down_grad, parts), to_parts(down_grad_peer, parts)], (1, 2, 0))
        up_sum = Staged([to_parts(up_grad, parts), to_parts(up_peer, parts)], (0, 1))
    down_sum.send()
    up_sum.send()
    grad_resid2, grad2, sums3 = join_back(
        None, None, 0, (back_own, back_peer), (resid2, grad_out, shared[4]), low_too=True
    )

    def outer(x, g):
        return low(jnp.einsum("td,te->de", x, g, preferred_element_type=jnp.float32))

    row1_peer = exchange(outer(cross_out[1], grad2))
    row1_own = outer(cross_out[0], grad2)

    def cross_back(h, grad):
        return attention_back(
            cross_query[h], mem_key[h], mem_value[h], grad, cross_out[h], cross_log[h], cross_at, False
        )

    grad_cq, grad_mk, grad_mv = ([None, None], [None, None], [None, None])
    grad = [low(jnp.einsum("td,fd->tf", grad2, rws[h][1], preferred_element_type=jnp.float32)) for h in both]
    grad_cq[1], grad_mk[1], grad_mv[1] = cross_back(1, grad[1])
    cross_peer = exchange(outer_plain((normed2, memory), (0, 1, 1), (grad_cq[1], grad_mk[1], grad_mv[1])))
    grad[0], cross_peer = tie(checkpoint(grad[0], down_sum, up_sum), cross_peer)
    grad_cq[0], grad_mk[0], grad_mv[0] = cross_back(0, grad[0])
    (grad_cq[0], grad_mk[0], grad_mv[0]), row1_peer = tie(
        checkpoint((grad_cq[0], grad_mk[0], grad_mv[0]), down_sum, up_sum), row1_peer
    )
    if aligned:
        ((give, keep),) = outer_split(
            (normed2, memory), (0, 1, 1), (grad_cq[0], grad_mk[0], grad_mv[0]), cross_peer, ((0, 4, 0),), lax.axis_index("dp")
        )
        cross_sum = Staged.begun(give, keep, (0, 1), parts)
    else:
        cross_own = jnp.stack([outer(normed2, grad_cq[0]), outer(memory, grad_mk[0]), outer(memory, grad_mv[0])])
        cross_sum = Staged([to_parts(cross_own, parts), to_parts(cross_peer, parts)], (0, 1))
        cross_sum.send()
    grad_resid1, grad1, sums2 = join_back(
        [[grad_cq[0]], [grad_cq[1]]], cols, 3, (), (resid1, grad_resid2, shared[2]), low_too=True
    )
    grad1 = checkpoint(grad1, down_sum, up_sum)
    row0_peer = exchange(outer(self_out[1], grad1))
    row0_own = outer(self_out[0], grad1)

    def self_back(h, grad):
        return attention_back(query[h], key[h], value[h], grad, self_out[h], self_log[h], self_at, True)

    grad_q, grad_k, grad_v = ([None, None], [None, None], [None, None])
    grad = [low(jnp.einsum("td,fd->tf", grad1, rws[h][0], preferred_element_type=jnp.float32)) for h in both]
    grad[1], row0_peer = tie(grad[1], row0_peer)
    row_sum = Staged(
        [
            to_parts(jnp.stack([row0_own, row1_own]), parts),
            to_parts(jnp.stack([row0_peer, row1_peer]), parts),
        ],
        (1, 0),
    )
    row_sum.send()
    grad_q[1], grad_k[1], grad_v[1] = self_back(1, grad[1])
    self_peer = exchange(outer_plain((normed1,), (0, 0, 0), (grad_q[1], grad_k[1], grad_v[1])))
    grad[0], self_peer = tie(checkpoint(grad[0], down_sum, up_sum, cross_sum, row_sum), self_peer)
    grad_q[0], grad_k[0], grad_v[0] = self_back(0, grad[0])
    grad_q[0], grad_k[0], grad_v[0] = checkpoint((grad_q[0], grad_k[0], grad_v[0]), cross_sum, row_sum)
    if aligned:
        (a, b) = outer_split(
            (normed1,), (0, 0, 0), (grad_q[0], grad_k[0], grad_v[0]), self_peer, ((0, 2, 0), (2, 4, 1)), lax.axis_index("dp")
        )
        (grad_q[0], grad_k[0], grad_v[0]), *a = tie((grad_q[0], grad_k[0], grad_v[0]), *a)
        self_a = Staged.begun(*a, (0, 1), parts)
        self_b = Staged.begun(*b, (1, 0), parts)
    else:
        self_own = jnp.stack([outer(normed1, grad_q[0]), outer(normed1, grad_k[0]), outer(normed1, grad_v[0])])
        self_terms = [to_parts(self_own, parts), to_parts(self_peer, parts)]
        self_terms = [a.reshape((3, 2, -1) + a.shape[1:]).swapaxes(0, 1) for a in self_terms]
        self_terms = [a.reshape((2, -1) + a.shape[3:]) for a in self_terms]
        self_a = Staged([a[0] for a in self_terms], (0, 1))
        self_b = Staged([a[1] for a in self_terms], (1, 0))
        self_a.send()
        self_b.send()
    input_grad, sums1 = join_back(
        [[grad_q[h], grad_k[h], grad_v[h]] for h in both], cols, 0, (), (tokens, grad_resid1, shared[0])
    )
    input_grad, sums1, grad_mk[0] = checkpoint(
        (input_grad, sums1, grad_mk[0]), cross_sum, row_sum, self_a, self_b
    )
    (memory_grad,) = join_back([[grad_mk[h], grad_mv[h]] for h in both], cols, 2)
    memory_grad, sums1 = checkpoint((memory_grad, sums1), cross_sum, row_sum, self_a, self_b)
    self_piece = jnp.stack([a.finish().reshape((3, -1) + (BS // parts, half)) for a in (self_a, self_b)], axis=1)
    self_piece = self_piece.reshape((-1, BS // parts, half))
    cross_piece = cross_sum.finish()
    up_piece = up_sum.finish()
    down_piece = down_sum.finish()
    row_piece = row_sum.finish()

    def column_sum(a):
        return jnp.sum(wide(a), axis=0)

    shared_grad = jnp.concatenate(
        [
            sums1[0:2],
            sums2[0:2],
            sums3[0:2],
            sums2[2:3],
            sums3[2:3],
            column_sum(grad_out)[None],
        ]
    )
    split_grad = [
        jnp.concatenate(
            [
                jnp.stack([column_sum(grad_q[h]), column_sum(grad_v[h]), column_sum(grad_cq[h]), column_sum(grad_mv[h])]),
                up_bias[h],
            ]
        )
        for h in both
    ]
    first = jnp.where(core == 0, split_grad[0], split_grad[1])
    second = jnp.where(core == 0, split_grad[1], split_grad[0])
    vectors = jnp.concatenate([shared_grad, jnp.concatenate([first, second], axis=1)], axis=0)
    def blocks(piece):
        m, rows_in, width = piece.shape
        return (
            piece.reshape(m, rows_in, width // BS, BS).transpose(0, 2, 1, 3).reshape(-1, rows_in, BS)
        )

    pieces = jnp.concatenate(
        [
            blocks(self_piece),
            blocks(cross_piece),
            blocks(up_piece),
            blocks(row_piece),
            blocks(down_piece),
        ],
        axis=0,
    )
    square = jnp.sum(wide(pieces) * wide(pieces))
    owned = slot_first.shape[0]
    part_rows = BS // parts
    sent = jnp.take(pieces, slot_order(block_slot), axis=0)
    if part_rows % 16 == 0 and vectors.shape[0] < parts * mp_size:
        came, vectors, grad_norm = share(sent.reshape(parts, owned * part_rows, BS), square, vectors, mp_size)
    else:
        came = lax.all_to_all(sent.reshape(parts, owned, part_rows, BS), "dp", 0, 0, tiled=True)
        vectors = all_sum(vectors, parts)
        grad_norm = jnp.sqrt(all_sum(square.reshape(1, 1), parts)[0, 0] + jnp.sum(vectors * vectors))
    shared_sum = vectors[:9]
    split_sum = vectors[9:]
    mine = came.reshape(parts, owned, part_rows, BS).transpose(1, 0, 2, 3).reshape(owned, BS, BS)
    clip = clip_limit / jnp.maximum(grad_norm, clip_limit)

    def flat(a):
        return a.reshape(owned, BS, BS)

    updated = soap(
        clip,
        mine,
        flat(slot_first),
        flat(slot_second),
        flat(slot_master),
        flat(slot_left),
        flat(slot_right),
        flat(left_basis),
        flat(right_basis),
    )
    first_moment, second_moment, master_weight, master_copy, left_stat, right_stat, left_rotation, right_rotation = (
        a.reshape(slot_first.shape) for a in updated
    )
    shared_mean, shared_square, shared_values = adam_step(
        shared_sum * clip, shared_first, shared_second, shared_vectors, shared_rate
    )
    split_own = lax.dynamic_slice_in_dim(split_sum, core * half, half, axis=1)
    split_mean, split_square, split_values = adam_step(
        split_own * clip, split_first, split_second, split_vectors, split_rate
    )
    return (
        output,
        input_grad,
        memory_grad,
        first_moment,
        second_moment,
        master_weight,
        master_copy,
        left_stat,
        right_stat,
        left_rotation,
        right_rotation,
        shared_mean,
        shared_square,
        shared_values,
        split_mean,
        split_square,
        split_values,
        grad_norm,
    )


def solution(mesh):
    rows = P(("dp", "mp"), None)
    slots = P("dp", "mp", None, None)
    split = P(None, "mp")
    placed = (
        (rows, rows, rows, P("dp"), P("dp", None), P("dp", None), P())
        + (P(None, None, "mp"), P(None, "mp", None), P(), split, P(), P(), split, split)
        + (slots,) * 7
    )
    return jax.shard_map(
        partial(on_device, mesh.shape["dp"], mesh.shape["mp"]),
        mesh=mesh,
        in_specs=placed,
        out_specs=(rows,) * 3 + (slots,) * 8 + (P(),) * 3 + (split,) * 3 + (P(),),
        check_vma=False,
    )
```

```python
from functools import partial

import jax
import jax.numpy as jnp
from jax import lax
from jax.experimental import pallas as pl
from jax.experimental.pallas import tpu as pltpu
from jax.sharding import PartitionSpec as P

HEAD_DIM=64; TQ=256
SCALE=HEAD_DIM**-0.5
EXPC=SCALE*1.4426950408889634
NEG=-1e30
NT=(((1,),(1,)),((),()))
NN=(((1,),(0,)),((),()))

def rows_of(i,n=1):
    if isinstance(i,int): return slice(i*TQ,(i+n)*TQ)
    return pl.ds(pl.multiple_of(i*TQ,TQ),n*TQ)

def head_cols(h):
    return slice(h*HEAD_DIM,(h+1)*HEAD_DIM)

def lanes_of(pair):
    return pl.ds(pl.multiple_of(pair*128,128),128)

def allowed(causal,limit,j):
    r=lax.broadcasted_iota(jnp.int32,(TQ,TQ),0)
    if causal: return r<=lax.broadcasted_iota(jnp.int32,(TQ,TQ),1)
    return r<limit-j*TQ

def each_case(causal,plan,tiles,pairs,emit):
    def over(n,body):
        def step(i,_):
            body(i)
            return 0
        lax.fori_loop(0,n,step,0)
    for b in range(3):
        count=1<<b; size=tiles>>b
        if b==0 and not causal:
            for n in (size,size//2):
                fits=plan[1]>TQ*size//2 if n==size else plan[1]<=TQ*size//2
                @pl.when((plan[0]==b)&fits)
                def _(n=n):
                    over(pairs,lambda pair: emit(pair,[(0,size,n,plan[1],n-size//2)]))
        else:
            @pl.when(plan[0]==b)
            def _(count=count,size=size):
                if count==1: over(pairs,lambda pair: emit(pair,[(0,size,size,None,size-1)]))
                else: over(pairs,lambda pair: over(count,lambda s: emit(pair,[(s*size,size,size,None if causal else plan[1+s],0)])))

def tile_items(causal,segments):
    out=[]
    for t0,qn,kn,limit,masked in segments:
        for i in range(qn):
            n=i+1 if causal else kn
            out.append((t0+i,t0,n,limit,n-1 if causal else masked))
    return out

def fwd_kernel(causal, tiles, plan, q_ref, k_ref, v_ref, o_ref, l_ref, vt_ref):
    pairs=q_ref.shape[1]//128
    def turn(pair,_):
        vt_ref[pair]=v_ref[:,lanes_of(pair)].astype(jnp.float32).T.astype(jnp.bfloat16)
        return 0
    lax.fori_loop(0,pairs,turn,0)
    def emit(pair,segments):
        lanes=lanes_of(pair)
        items=[(t,h) for t in tile_items(causal,segments) for h in range(2)]
        def scores(item):
            (i,k0,n,limit,masked),h=item
            q=q_ref[rows_of(i),lanes][:,head_cols(h)]
            parts=[]
            for j in range(n):
                s=lax.dot_general(k_ref[rows_of(k0+j),lanes][:,head_cols(h)],q,NT,preferred_element_type=jnp.float32)
                if j>=masked:
                    s=jnp.where(allowed(causal,limit,j),s,NEG)
                parts.append(s)
            return parts
        ahead=scores(items[0])
        held=None
        for c,((i,k0,n,limit,masked),h) in enumerate(items):
            parts=ahead
            if c+1<len(items): ahead=scores(items[c+1])
            top=parts[0].max(axis=0,keepdims=True)
            for s in parts[1:]: top=jnp.maximum(top,s.max(axis=0,keepdims=True))
            total=None; acc=None
            for j,s in enumerate(parts):
                p=jnp.exp2((s-top)*EXPC)
                t=p.sum(axis=0,keepdims=True)
                total=t if total is None else total+t
                a=lax.dot_general(vt_ref[pair,head_cols(h),rows_of(k0+j)],p.astype(jnp.bfloat16),NN,preferred_element_type=jnp.float32)
                acc=a if acc is None else acc+a
            acc=acc*(1.0/total)
            l_ref[pair,h:h+1,rows_of(i)]=top+jnp.log2(total)*(1.0/EXPC)
            if h==0: held=acc
            else: o_ref[rows_of(i),lanes]=jnp.concatenate([held,acc],axis=0).T.astype(o_ref.dtype)
    each_case(causal,plan,tiles,pairs,emit)

VM=pl.BlockSpec(memory_space=pltpu.VMEM)
SM=pl.BlockSpec(memory_space=pltpu.SMEM)

def attention(q,k,v,plan,causal):
    T,W=q.shape; M=k.shape[0]; pairs=W//128; tiles=T//TQ
    return pl.pallas_call(
        partial(fwd_kernel,causal,tiles),
        out_shape=(jax.ShapeDtypeStruct((T,W),jnp.bfloat16),jax.ShapeDtypeStruct((pairs,2,T),jnp.float32)),
        in_specs=[SM,VM,VM,VM],out_specs=[VM,VM],
        scratch_shapes=[pltpu.VMEM((pairs,128,M),jnp.bfloat16)],
        compiler_params=pltpu.CompilerParams(vmem_limit_bytes=8*1024*1024),
        cost_estimate=pl.CostEstimate(flops=4*T*M*W//2,bytes_accessed=8*T*W,transcendentals=T*M*W//128),
    )(plan,q,k,v)

def bwd_kernel(causal, tiles, plan, q_ref, k_ref, v_ref, g_ref, o_ref, l_ref, dq_ref, dk_ref, dv_ref, kt_ref, p_ref, s_ref, d_ref):
    pairs=q_ref.shape[1]//128
    ones=jnp.ones((8,HEAD_DIM),jnp.bfloat16)
    def turn(pair,_):
        lanes=lanes_of(pair)
        kt_ref[pair]=k_ref[:,lanes].astype(jnp.float32).T.astype(jnp.bfloat16)
        prod=g_ref[:,lanes].astype(jnp.float32)*o_ref[:,lanes].astype(jnp.float32)
        top=prod.astype(jnp.bfloat16)
        rest=(prod-top.astype(jnp.float32)).astype(jnp.bfloat16)
        for h in range(2):
            d_ref[pair,h]=(lax.dot_general(ones,top[:,head_cols(h)],NT,preferred_element_type=jnp.float32)
                +lax.dot_general(ones,rest[:,head_cols(h)],NT,preferred_element_type=jnp.float32))
        return 0
    lax.fori_loop(0,pairs,turn,0)
    def emit(pair,segments):
        lanes=lanes_of(pair)
        items=[(i,k0,j,n,limit,masked,h) for i,k0,n,limit,masked in tile_items(causal,segments) for j in range(n) for h in range(2)]
        def products(item):
            i,k0,j,n,limit,masked,h=item
            return (lax.dot_general(k_ref[rows_of(k0+j),lanes][:,head_cols(h)],q_ref[rows_of(i),lanes][:,head_cols(h)],NT,preferred_element_type=jnp.float32),
                    lax.dot_general(v_ref[rows_of(k0+j),lanes][:,head_cols(h)],g_ref[rows_of(i),lanes][:,head_cols(h)],NT,preferred_element_type=jnp.float32))
        ahead=products(items[0])
        acc=[None,None]
        for c,(i,k0,j,n,limit,masked,h) in enumerate(items):
            s,dp=ahead
            if c+1<len(items): ahead=products(items[c+1])
            p=jnp.exp2((s-l_ref[pair,h:h+1,rows_of(i)])*EXPC)
            if j>=masked: p=jnp.where(allowed(causal,limit,j),p,0.0)
            p_ref[h,rows_of(k0+j),rows_of(i)]=p.astype(jnp.bfloat16)
            ds=(p*(dp-d_ref[pair,h,0:1,rows_of(i)])).astype(jnp.bfloat16)
            s_ref[h,rows_of(k0+j),rows_of(i)]=ds
            a=lax.dot_general(kt_ref[pair,head_cols(h),rows_of(k0+j)],ds,NN,preferred_element_type=jnp.float32)
            acc[h]=a if j==0 else acc[h]+a
            if j==n-1 and h==1:
                dq_ref[rows_of(i),lanes]=(jnp.concatenate(acc,axis=0)*SCALE).T.astype(dq_ref.dtype)
        for t0,qn,kn,limit,masked in segments:
            for j in range(qn):
                if j>=kn:
                    dk_ref[rows_of(t0+j),lanes]=jnp.zeros((TQ,128),dk_ref.dtype)
                    dv_ref[rows_of(t0+j),lanes]=jnp.zeros((TQ,128),dv_ref.dtype)
                    continue
                cols=rows_of(t0+j,qn-j) if causal else rows_of(t0,qn)
                both=[]
                for h in range(2):
                    both.append((lax.dot_general(p_ref[h,rows_of(t0+j),cols],g_ref[cols,lanes][:,head_cols(h)],NN,preferred_element_type=jnp.float32),
                                 lax.dot_general(s_ref[h,rows_of(t0+j),cols],q_ref[cols,lanes][:,head_cols(h)],NN,preferred_element_type=jnp.float32)))
                dv_ref[rows_of(t0+j),lanes]=jnp.concatenate([a for a,b in both],axis=1).astype(dv_ref.dtype)
                dk_ref[rows_of(t0+j),lanes]=(jnp.concatenate([b for a,b in both],axis=1)*SCALE).astype(dk_ref.dtype)
    each_case(causal,plan,tiles,pairs,emit)

def attention_back(q,k,v,g,out,logs,plan,causal):
    T,W=q.shape; M=k.shape[0]; pairs=W//128; tiles=T//TQ
    narrow=jax.ShapeDtypeStruct((T,W),jnp.bfloat16)
    return pl.pallas_call(
        partial(bwd_kernel,causal,tiles),
        out_shape=(narrow,jax.ShapeDtypeStruct((M,W),jnp.bfloat16),jax.ShapeDtypeStruct((M,W),jnp.bfloat16)),
        in_specs=[SM]+[VM]*6,out_specs=[VM]*3,
        scratch_shapes=[pltpu.VMEM((pairs,128,M),jnp.bfloat16),pltpu.VMEM((2,M,T),jnp.bfloat16),pltpu.VMEM((2,M,T),jnp.bfloat16),pltpu.VMEM((pairs,2,8,T),jnp.float32)],
        compiler_params=pltpu.CompilerParams(vmem_limit_bytes=14*1024*1024),
        cost_estimate=pl.CostEstimate(flops=10*T*M*W//2,bytes_accessed=14*T*W,transcendentals=T*M*W//128),
    )(plan,q,k,v,g,out,logs)

def self_plan(bucket,T):
    return bucket.reshape(1)

def cross_plan(bucket,lengths,T,M):
    return jnp.concatenate([bucket.reshape(1),lengths])

CHUNK=256
JOIN=pltpu.CompilerParams(vmem_limit_bytes=20*1024*1024)

def hat_of(values):
    centered=values-jnp.mean(values,axis=-1,keepdims=True)
    inverse=lax.rsqrt(jnp.mean(centered*centered,axis=-1,keepdims=True)+1e-05)
    return centered*inverse,inverse

def join_kernel(v_ref,a_ref,b_ref,wa_ref,wb_ref,r_ref,sum_ref,norm_ref):
    product=(lax.dot_general(a_ref[...],wa_ref[0],NN,preferred_element_type=jnp.float32)
        +lax.dot_general(b_ref[...],wb_ref[0],NN,preferred_element_type=jnp.float32))
    values=v_ref[...].astype(jnp.float32)+product+r_ref[0:1,:]
    sum_ref[...]=values
    hat,_=hat_of(values)
    norm_ref[...]=(hat*r_ref[1:2,:]+r_ref[2:3,:]).astype(norm_ref.dtype)

def join_forward(values,halves,rows,index,shift,gain,bias):
    T,D=values.shape; H=halves[0].shape[1]
    part=pl.BlockSpec((CHUNK,D),lambda i:(i,0)); narrow=pl.BlockSpec((CHUNK,H),lambda i:(i,0))
    weight=pl.BlockSpec((1,H,D),lambda i:(index,0,0))
    return pl.pallas_call(join_kernel,grid=(T//CHUNK,),
        out_shape=(jax.ShapeDtypeStruct((T,D),jnp.float32),jax.ShapeDtypeStruct((T,D),jnp.bfloat16)),
        in_specs=[part,narrow,narrow,weight,weight,pl.BlockSpec((3,D),lambda i:(0,0))],out_specs=[part,part],
        compiler_params=JOIN,cost_estimate=pl.CostEstimate(flops=4*T*D*H,bytes_accessed=10*T*D+4*T*H+4*H*D,transcendentals=T),
    )(values,*halves,*rows,jnp.stack([shift,gain,bias]))

def back_kernel(terms,extras,norm,low_too,*refs):
    refs=list(refs)
    take=lambda n: [refs.pop(0) for _ in range(n)]
    gs=take(2*terms); ws=take(2 if terms else 0); ex=take(extras)
    acc=None
    for h in range(2 if terms else 0):
        for s in range(terms):
            a=lax.dot_general(gs[h*terms+s][...],ws[h][s],NT,preferred_element_type=jnp.float32)
            acc=a if acc is None else acc+a
    for e in ex:
        acc=e[...] if acc is None else acc+e[...]
    if not norm:
        refs.pop(0)[...]=acc
        return
    v_ref,g_ref,gain_ref=take(3)
    hat,inverse=hat_of(v_ref[...].astype(jnp.float32))
    inner=acc*gain_ref[...]
    back=inverse*(inner-jnp.mean(inner,axis=-1,keepdims=True)-hat*jnp.mean(inner*hat,axis=-1,keepdims=True))
    new=g_ref[...].astype(jnp.float32)+back
    refs.pop(0)[...]=new
    if low_too: refs.pop(0)[...]=new.astype(jnp.bfloat16)
    sums=refs.pop(0)
    @pl.when(pl.program_id(0)==0)
    def _(): sums[...]=jnp.zeros_like(sums)
    sums[0:1,:]+=jnp.sum(acc*hat,axis=0,keepdims=True)
    sums[1:2,:]+=jnp.sum(acc,axis=0,keepdims=True)
    sums[2:3,:]+=jnp.sum(new,axis=0,keepdims=True)

def join_back(gs,cols,index,extras=(),norm=None,low_too=False):
    terms=len(gs[0]) if gs else 0
    T,D=extras[0].shape if extras else (gs[0][0].shape[0],cols[0].shape[1])
    part=pl.BlockSpec((CHUNK,D),lambda i:(i,0))
    args=[]; specs=[]
    if terms:
        H=gs[0][0].shape[1]
        for h in range(2):
            for g in gs[h]: args.append(g); specs.append(pl.BlockSpec((CHUNK,H),lambda i:(i,0)))
        for w in cols: args.append(w); specs.append(pl.BlockSpec((terms,D,H),lambda i:(index,0,0),pipeline_mode=pl.Buffered(1)))
    for e in extras: args.append(e); specs.append(part)
    full=jax.ShapeDtypeStruct((T,D),jnp.float32)
    outs=[full]; out_specs=[part]
    if norm:
        values,grad,gain=norm
        args+=[values,grad,gain[None]]; specs+=[part,part,pl.BlockSpec((1,D),lambda i:(0,0))]
        if low_too: outs.append(jax.ShapeDtypeStruct((T,D),jnp.bfloat16)); out_specs.append(part)
        outs.append(jax.ShapeDtypeStruct((8,D),jnp.float32)); out_specs.append(pl.BlockSpec((8,D),lambda i:(0,0)))
    return pl.pallas_call(partial(back_kernel,terms,len(extras),norm is not None,low_too),grid=(T//CHUNK,),
        out_shape=tuple(outs),in_specs=specs,out_specs=tuple(out_specs),compiler_params=JOIN,
        cost_estimate=pl.CostEstimate(flops=4*terms*T*D*512+T*D*20,bytes_accessed=20*T*D+4*terms*D*512,transcendentals=T),
    )(*args)

PART=16
def outer_kernel(pick,cuts,dp_ref,*refs):
    refs=list(refs); n=len(pick)
    xs=[refs.pop(0) for _ in range(max(pick)+1)]
    gs=[refs.pop(0) for _ in range(n)]
    recv=refs.pop(0)
    outs=[(refs.pop(0),refs.pop(0)) for _ in cuts]
    held=refs.pop(0)
    parts=BS//PART
    for s in range(n):
        held[s]=(lax.dot_general(xs[pick[s]][...],gs[s][...],(((0,),(0,)),((),())),preferred_element_type=jnp.float32)
            +recv[s].astype(jnp.float32)).astype(held.dtype)
    for (give,keep),(first,last,bit) in zip(outs,cuts):
        mine=(dp_ref[0]>>bit)&1
        for s in range(n):
            for i in range(first,last):
                m=s*(last-first)+i-first
                for kk in range(parts//2):
                    low=(kk>>bit<<(bit+1))|(kk&((1<<bit)-1))
                    at=i*BS+low*PART
                    other=pl.ds(pl.multiple_of(at+(1-mine)*(PART<<bit),PART),PART)
                    own=pl.ds(pl.multiple_of(at+mine*(PART<<bit),PART),PART)
                    give[kk,m]=held[s,other,:]
                    keep[kk,m]=held[s,own,:]

def outer_split(xs,pick,gs,recv,cuts,index):
    n=len(gs); D=xs[0].shape[1]; H=gs[0].shape[1]; parts=BS//PART
    vm=pl.BlockSpec(memory_space=pltpu.VMEM)
    shapes=[]
    for first,last,bit in cuts:
        shapes+=[jax.ShapeDtypeStruct((parts//2,n*(last-first),PART,H),jnp.bfloat16)]*2
    out=pl.pallas_call(partial(outer_kernel,pick,cuts),out_shape=tuple(shapes),
        in_specs=[pl.BlockSpec(memory_space=pltpu.SMEM)]+[vm]*(len(xs)+n+1),out_specs=tuple([vm]*len(shapes)),
        scratch_shapes=[pltpu.VMEM((n,D,H),jnp.bfloat16)],
        compiler_params=pltpu.CompilerParams(vmem_limit_bytes=12*1024*1024),
        cost_estimate=pl.CostEstimate(flops=2*n*xs[0].shape[0]*D*H,bytes_accessed=8*n*D*H,transcendentals=0),
    )(index.reshape(1).astype(jnp.int32),*xs,*gs,recv)
    return [(out[2*i],out[2*i+1]) for i in range(len(cuts))]

def plain_kernel(pick,*refs):
    xs,gs,out=refs[:max(pick)+1],refs[max(pick)+1:-1],refs[-1]
    for s,x in enumerate(pick):
        out[s]=lax.dot_general(xs[x][...],gs[s][...],(((0,),(0,)),((),())),preferred_element_type=jnp.float32).astype(out.dtype)

def outer_plain(xs,pick,gs):
    n=len(gs); D=xs[0].shape[1]; H=gs[0].shape[1]
    vm=pl.BlockSpec(memory_space=pltpu.VMEM)
    return pl.pallas_call(partial(plain_kernel,pick),out_shape=jax.ShapeDtypeStruct((n,D,H),jnp.bfloat16),
        in_specs=[vm]*(len(xs)+n),out_specs=vm,compiler_params=pltpu.CompilerParams(vmem_limit_bytes=12*1024*1024),
        cost_estimate=pl.CostEstimate(flops=2*n*xs[0].shape[0]*D*H,bytes_accessed=8*n*D*H,transcendentals=0),
    )(*xs,*gs)

COLS=(((0,),(0,)),((),()))
def prod(a,b,dims):
    return lax.dot_general(a,b,dims,preferred_element_type=jnp.float32)

def gelu_parts(v):
    t=1.0/(1.0+(0.3275911*0.7071067811865476)*jnp.abs(v))
    e=jnp.exp2(v*v*(-0.5*1.4426950408889634))
    poly=t*(0.5*0.254829592+t*(0.5*-0.284496736+t*(0.5*1.421413741+t*(0.5*-1.453152027+t*(0.5*1.061405429)))))
    tail=poly*e
    phi=jnp.where(v>=0.0,1.0-tail,tail)
    return v*phi,phi+v*e*0.3989422804014327

UP_BITS=(0,1,2,3)
DOWN_BITS=(1,2,0,3)
def spread(ref,value,order):
    if len(ref.shape)==3:
        ref[0]=value
        return
    for i in range(value.shape[0]//BS):
        for p in range(BS//PART):
            at=i*BS+p*PART
            ref[tuple((p>>b)&1 for b in order)+(0,i)]=value[at:at+PART,:]

def feed_kernel(x_ref,g_ref,up_ref,dn_ref,b_ref,down_ref,back_ref,gu_ref,gd_ref,gb_ref,hid_ref,pre_ref):
    rows=x_ref.shape[0]; step=512
    first=pl.program_id(0)==0
    @pl.when(first)
    def _():
        down_ref[...]=jnp.zeros_like(down_ref)
        back_ref[...]=jnp.zeros_like(back_ref)
    up=up_ref[0]; dn=dn_ref[0]; bias=b_ref[0]
    def ahead(r):
        at=slice(r*step,(r+1)*step)
        return prod(x_ref[at,:],up,NN),prod(g_ref[at,:],dn,NT)
    count=rows//step
    nxt=ahead(0)
    total=None
    for r in range(count):
        at=slice(r*step,(r+1)*step)
        pre,gh=nxt
        if r+1<count: nxt=ahead(r+1)
        hidden,slope=gelu_parts(pre+bias)
        hidden=hidden.astype(jnp.bfloat16)
        hid_ref[at,:]=hidden
        gp=(gh.astype(jnp.bfloat16).astype(jnp.float32)*slope).astype(jnp.bfloat16)
        pre_ref[at,:]=gp
        s=jnp.sum(gp.astype(jnp.float32),axis=0,keepdims=True)
        total=s if total is None else total+s
        down_ref[at,:]+=prod(hidden,dn,NN)
        back_ref[at,:]+=prod(gp,up,NT)
    gb_ref[0]=total
    spread(gu_ref,prod(x_ref[...],pre_ref[...],COLS).astype(gu_ref.dtype),UP_BITS)
    spread(gd_ref,prod(hid_ref[...],g_ref[...],COLS).astype(gd_ref.dtype),DOWN_BITS)

def feed_forward(x,g,col,row,bias,aligned):
    T,D=x.shape; H=col.shape[2]
    f32=jnp.float32; bf=jnp.bfloat16
    once=pl.BlockSpec((T,D),lambda s:(0,0),pipeline_mode=pl.Buffered(1))
    whole=pl.BlockSpec((T,D),lambda s:(0,0))
    def grad(height,width):
        if not aligned: return jax.ShapeDtypeStruct((4,height,width),bf),pl.BlockSpec((1,height,width),lambda s:(s,0,0))
        shape=(2,2,2,2,4,height//BS,PART,width)
        return jax.ShapeDtypeStruct(shape,bf),pl.BlockSpec(shape[:4]+(1,)+shape[5:],lambda s:(0,0,0,0,s,0,0,0))
    (gu,gu_spec),(gd,gd_spec)=grad(D,H),grad(H,D)
    return pl.pallas_call(feed_kernel,grid=(4,),
        out_shape=(jax.ShapeDtypeStruct((T,D),f32),jax.ShapeDtypeStruct((T,D),f32),gu,
                   gd,jax.ShapeDtypeStruct((4,1,H),f32)),
        in_specs=[once,once,pl.BlockSpec((1,D,H),lambda s:(s+6,0,0)),pl.BlockSpec((1,H,D),lambda s:(s+2,0,0)),pl.BlockSpec((1,1,H),lambda s:(s,0,0))],
        out_specs=[whole,whole,gu_spec,gd_spec,pl.BlockSpec((1,1,H),lambda s:(s,0,0))],
        scratch_shapes=[pltpu.VMEM((T,H),bf),pltpu.VMEM((T,H),bf)],
        compiler_params=pltpu.CompilerParams(vmem_limit_bytes=50*1024*1024),
        cost_estimate=pl.CostEstimate(flops=6*2*4*T*D*H,bytes_accessed=4*T*D+8*T*D+16*D*H*2,transcendentals=8*T*H),
    )(x,g,col,row,bias[4:8,None,:])

MESH=pl.DeviceIdType.MESH

def share_kernel(parts, cores, sent_ref, rows_ref, came_ref, total_ref, norm_ref, arrived, own_sem, send_sem, recv_sem, up_send, up_recv, down_send, down_recv):
    here=lax.axis_index("dp"); core=lax.axis_index("mp")
    me=here*cores+core
    everyone=parts*cores
    count=rows_ref.shape[0]
    barrier=pltpu.get_barrier_semaphore()
    def place(at):
        return (at//cores,at%cores)
    def others(n,mine,body):
        for at in range(n):
            @pl.when(mine!=at)
            def _(at=at): body(at)
    others(everyone,me,lambda at: pl.semaphore_signal(barrier,inc=1,device_id=place(at),device_id_type=MESH))
    own=pltpu.make_async_copy(sent_ref.at[here],came_ref.at[here],own_sem)
    own.start()
    pl.semaphore_wait(barrier,everyone-1)
    def up(to):
        return pltpu.make_async_remote_copy(src_ref=rows_ref.at[to],dst_ref=arrived.at[me],send_sem=up_send.at[to],recv_sem=up_recv.at[me],
            device_id=place(to),device_id_type=MESH)
    def down(to):
        return pltpu.make_async_remote_copy(src_ref=total_ref.at[me],dst_ref=total_ref.at[me],send_sem=down_send.at[to],recv_sem=down_recv.at[me],
            device_id=place(to),device_id_type=MESH)
    def block(to):
        return pltpu.make_async_remote_copy(src_ref=sent_ref.at[to],dst_ref=came_ref.at[here],send_sem=send_sem.at[to],recv_sem=recv_sem.at[here],
            device_id=(to,core),device_id_type=MESH)
    def landed(ref,sem,at):
        pltpu.make_async_copy(ref.at[at],ref.at[at],sem.at[at]).wait()
    others(count,me,lambda to: up(to).start())
    others(parts,here,lambda to: block(to).start())
    @pl.when(me<count)
    def _():
        arrived[me]=rows_ref[me]
        others(everyone,me,lambda at: landed(arrived,up_recv,at))
        total_ref[me]=jnp.sum(arrived[...],axis=0)
        others(everyone,me,lambda to: down(to).start())
    others(count,me,lambda to: up(to).wait_send())
    others(count,me,lambda at: landed(total_ref,down_recv,at))
    vectors=total_ref[0:count-1]
    square=jnp.sum(vectors*vectors,axis=0)+total_ref[count-1]
    norm_ref[...]=jnp.broadcast_to(jnp.sqrt(jnp.sum(square,keepdims=True)),norm_ref.shape)
    @pl.when(me<count)
    def _(): others(everyone,me,lambda to: down(to).wait_send())
    def end_block(at):
        block(at).wait_send()
        landed(came_ref,recv_sem,at)
    others(parts,here,end_block)
    own.wait()

def share(sent,square,vectors,cores):
    parts,rows,width=sent.shape
    count=vectors.shape[0]+1
    everyone=parts*cores
    rows_in=jnp.concatenate([vectors,jnp.zeros_like(vectors[:1]).at[0,0].set(square)]).reshape(count,8,-1)
    tile=rows_in.shape[1:]
    vm=pl.BlockSpec(memory_space=pltpu.VMEM)
    dma=pltpu.SemaphoreType.DMA
    came,total,norm=pl.pallas_call(partial(share_kernel,parts,cores),
        out_shape=(jax.ShapeDtypeStruct(sent.shape,sent.dtype),jax.ShapeDtypeStruct(rows_in.shape,jnp.float32),jax.ShapeDtypeStruct((8,128),jnp.float32)),
        in_specs=[vm,vm],out_specs=[vm,vm,vm],
        scratch_shapes=[pltpu.VMEM((everyone,)+tile,jnp.float32),dma,dma((parts,)),dma((parts,)),
            dma((everyone,)),dma((everyone,)),dma((everyone,)),dma((everyone,))],
        compiler_params=pltpu.CompilerParams(collective_id=0,has_side_effects=True,vmem_limit_bytes=6*1024*1024),
    )(sent,rows_in)
    return came,total.reshape(count,-1)[:-1],norm[0,0]

BS=256; STEP=10
weight_rate=0.03; weight_decay=0.01
HI=lax.Precision.HIGHEST
def hdot(a,b,dims,precision=HI):
    return lax.dot_general(a,b,(dims,((),())),precision=precision,preferred_element_type=jnp.float32)
DIM_NN=((1,),(0,)); DIM_NT=((1,),(1,)); DIM_TN=((0,),(0,))

def parts2(a):
    top=a.astype(jnp.bfloat16)
    return top,(a-top.astype(jnp.float32)).astype(jnp.bfloat16)

def dot1(a,b,dims):
    return lax.dot_general(a,b,(dims,((),())),preferred_element_type=jnp.float32)

def dot3(a,b,dims):
    a0,a1=a; b0,b1=b
    return dot1(a0,b0,dims)+(dot1(a0,b1,dims)+dot1(a1,b0,dims))

def soap_kernel(clip_ref,g_ref,first,second,master,left,right,ql_ref,qr_ref,
                first_o,second_o,master_o,copy_o,left_o,right_o,al_o,ar_o,ml_o,mr_o):
    clip=clip_ref[0,0]
    g=g_ref[0]
    ql=ql_ref[0]; qr=qr_ref[0]
    scale=0.05*clip*clip
    left_new=0.95*left[0]+scale*dot1(g,g,DIM_NT)
    left_o[0]=left_new
    al=hdot(left_new,ql,DIM_NN); al_o[0]=al
    ml_o[0]=hdot(al,al,DIM_TN)
    right_new=0.95*right[0]+scale*dot1(g,g,DIM_TN)
    right_o[0]=right_new
    ar=hdot(right_new,qr,DIM_NN); ar_o[0]=ar
    mr_o[0]=hdot(ar,ar,DIM_TN)
    ql2=parts2(ql); qr2=parts2(qr)
    half=dot1(ql2[0],g,DIM_TN)+dot1(ql2[1],g,DIM_TN)
    rot=clip*dot3(parts2(half),qr2,DIM_NN)
    f=0.9*first[0]+0.1*rot; first_o[0]=f
    s=0.99*second[0]+0.01*rot*rot; second_o[0]=s
    ratio=f/(1.0-0.9**STEP)/(jnp.sqrt(s/(1.0-0.99**STEP))+1e-8)
    stepped=dot3(parts2(dot3(ql2,parts2(ratio),DIM_NN)),qr2,DIM_NT)
    m=master[0]-weight_rate*(stepped+weight_decay*master[0])
    master_o[0]=m; copy_o[0]=m.astype(jnp.bfloat16)

def soap_stage(clip,g,first,second,master,left,right,ql,qr):
    n=g.shape[0]
    spec=pl.BlockSpec((1,BS,BS),lambda i:(i,0,0))
    f32=jax.ShapeDtypeStruct((n,BS,BS),jnp.float32)
    return pl.pallas_call(soap_kernel,grid=(n,),
        out_shape=(f32,f32,f32,jax.ShapeDtypeStruct((n,BS,BS),jnp.bfloat16),f32,f32,f32,f32,f32,f32),
        in_specs=[pl.BlockSpec(memory_space=pltpu.SMEM)]+[spec]*8,
        out_specs=[spec]*10,
        compiler_params=pltpu.CompilerParams(vmem_limit_bytes=48*1024*1024),
    )(clip.reshape(1,1),g,first,second,master,left,right,ql,qr)

PW=64
def chol_kernel(al_ref,ar_ref,ml_ref,mr_ref,ql_o,qr_o,work,tile):
    n=al_ref.shape[0]; pairs=n
    def load(m,_):
        work[m]=ml_ref[m]; work[n+m]=mr_ref[m]
        return 0
    lax.fori_loop(0,n,load,0)
    lane=lax.broadcasted_iota(jnp.int32,(1,2*PW),1)
    base=lane//PW*PW
    bigcol=lax.broadcasted_iota(jnp.int32,(PW,BS),1)
    bigrow=lax.broadcasted_iota(jnp.int32,(PW,BS),0)
    lower=lax.broadcasted_iota(jnp.int32,(PW,2*PW),1)%PW<=lax.broadcasted_iota(jnp.int32,(PW,2*PW),0)
    diag=lane-base==lax.broadcasted_iota(jnp.int32,(PW,2*PW),0)
    odd=lax.broadcasted_iota(jnp.int32,(PW,2*PW),0)%2==1
    beside=odd&(lane-base==lax.broadcasted_iota(jnp.int32,(PW,2*PW),0)-1)
    for p in range(BS//PW):
        lo=p*PW; at=slice(lo,lo+PW)
        for j in range(pairs):
            tile[j]=jnp.concatenate([work[2*j,at,at],work[2*j+1,at,at]],axis=1)
        for quarter in range(4):
            top=quarter*PW//4; height=PW-top
            rows=lax.broadcasted_iota(jnp.int32,(height,2*PW),0)+top
            def step(half,_):
                k=2*half
                below=rows>k+1
                here=lane-base
                clear=below&((here==k)|(here==k+1))
                at=jnp.broadcast_to(base+k,(height,2*PW))
                ts=[tile[j,top:,:] for j in range(pairs)]
                r1s=[jnp.broadcast_to(tile[j,pl.ds(k,1),:],(8,2*PW)) for j in range(pairs)]
                r2s=[jnp.broadcast_to(tile[j,pl.ds(k+1,1),:],(8,2*PW)) for j in range(pairs)]
                c1s=[jnp.take_along_axis(t,at,axis=1) for t in ts]
                c2s=[jnp.take_along_axis(t,at+1,axis=1) for t in ts]
                new=[]
                for t,c1,c2,r1,r2 in zip(ts,c1s,c2s,r1s,r2s):
                    p=jnp.take_along_axis(r1,at[:8],axis=1)
                    q=jnp.take_along_axis(r1,at[:8]+1,axis=1)
                    w=jnp.take_along_axis(r2,at[:8]+1,axis=1)
                    scale=1.0/(p*w-q*q)
                    r1=jnp.where(here==k,1.0,jnp.where(here==k+1,0.0,r1))
                    r2=jnp.where(here==k+1,1.0,jnp.where(here==k,0.0,r2))
                    u1=((w*r1-q*r2)*scale)[0:1]
                    u2=((p*r2-q*r1)*scale)[0:1]
                    new.append(jnp.where(clear,0.0,t)-jnp.where(below,c1,0.0)*u1-jnp.where(below,c2,0.0)*u2)
                for j in range(pairs): tile[j,top:,:]=new[j]
                return 0
            lax.fori_loop(top//2,(top+PW//4)//2,step,0)
        for j in range(pairs):
            t=tile[j]
            def column(mask):
                return jnp.where(lane<PW,jnp.sum(jnp.where(mask&(lane<PW),t,0.0),axis=1,keepdims=True),
                    jnp.sum(jnp.where(mask&(lane>=PW),t,0.0),axis=1,keepdims=True))
            own=column(diag)
            cross=column(beside)
            unit=jnp.where(diag,1.0,jnp.where(lower&~beside,t,0.0))
            ratio=jnp.where(odd,cross/pltpu.roll(own,1,0),0.0)
            tile[j]=(unit-ratio*pltpu.roll(unit,1,0))*lax.rsqrt(own-ratio*cross)
        inside=(bigcol>=lo)&(bigcol<lo+PW)
        eye=jnp.where(bigcol-lo==bigrow,1.0,0.0)
        def apply(j,_):
            both=tile[j]
            for s in range(2):
                m=2*j+s
                r=hdot(both[:,s*PW:(s+1)*PW],jnp.where(inside,eye,work[m,at,:]),DIM_NN)
                work[m,at,:]=r
                if p<BS//PW-1:
                    rest=jnp.where(inside[0:1],0.0,work[m,lo+PW:,:])
                    work[m,lo+PW:,:]=rest-hdot(r[:,lo+PW:],r,DIM_TN)
            return 0
        lax.fori_loop(0,pairs,apply,0,unroll=2 if pairs%2==0 else 1)
    keep=lax.broadcasted_iota(jnp.int32,(BS,BS),1)<=lax.broadcasted_iota(jnp.int32,(BS,BS),0)
    def final(m,_):
        ql_o[m]=dot3(parts2(al_ref[m]),parts2(jnp.where(keep,work[m],0.0)),DIM_NT)
        qr_o[m]=dot3(parts2(ar_ref[m]),parts2(jnp.where(keep,work[n+m],0.0)),DIM_NT)
        return 0
    lax.fori_loop(0,n,final,0)

def chol_stage(al,ar,ml,mr):
    n=al.shape[0]
    f32=jax.ShapeDtypeStruct((n,BS,BS),jnp.float32)
    vm=pl.BlockSpec(memory_space=pltpu.VMEM)
    return pl.pallas_call(chol_kernel,out_shape=(f32,f32),in_specs=[vm]*4,out_specs=[vm]*2,
        scratch_shapes=[pltpu.VMEM((2*n,BS,BS),jnp.float32),pltpu.VMEM((n,PW,2*PW),jnp.float32)],
        compiler_params=pltpu.CompilerParams(vmem_limit_bytes=32*1024*1024))(al,ar,ml,mr)

def soap(clip,g,first,second,master,left,right,ql,qr):
    f,s,m,c,l,r,al,ar,ml,mr=soap_stage(clip,g,first,second,master,left,right,ql,qr)
    lr,rr=chol_stage(al,ar,ml,mr)
    return f,s,m,c,l,r,lr,rr


LEN = 1024
shared_rate = 0.6
split_rate = 0.2
clip_limit = 1.0
SWAP = [(0, 1), (1, 0)]


def adam_step(gradient, first_state, second_state, values, step_rate):
    first_new = 0.9 * first_state + 0.1 * gradient
    second_new = 0.99 * second_state + 0.01 * gradient * gradient
    ratio = first_new / (1.0 - 0.9**STEP) / (jnp.sqrt(second_new / (1.0 - 0.99**STEP)) + 1e-08)
    return (first_new, second_new, values - step_rate * ratio)


def norm_forward(values, gain, shift):
    hat, _ = hat_of(values)
    return (hat * gain + shift).astype(jnp.bfloat16)


def dot32(a, b):
    return jnp.dot(a, b, preferred_element_type=jnp.float32)


def low(a):
    return a.astype(jnp.bfloat16)


def wide(a):
    return a.astype(jnp.float32)


def exchange(array):
    return lax.ppermute(array, "mp", SWAP)


def to_parts(array, parts):
    stacked, height, width = array.shape
    return array.reshape(stacked * height // BS, parts, BS // parts, width)


def tie(*arrays):
    return lax.optimization_barrier(arrays)


class Staged:
    def __init__(self, terms, first_bits, led=False):
        parts = 2 ** len(first_bits) if led else terms[0].shape[1]
        bits = parts.bit_length() - 1
        self.parts = parts
        self.order = list(first_bits) + [b for b in range(bits) if b not in first_bits]
        self.order = [b for b in self.order if b < bits]
        self.left = list(self.order) if led else list(range(bits - 1, -1, -1))
        self.start = 0 if led else 1
        if led:
            self.terms = [a.reshape((2,) * bits + (-1,) + a.shape[-2:]) for a in terms]
        else:
            self.terms = [a.reshape((a.shape[0],) + (2,) * bits + a.shape[2:]) for a in terms]
        self.got = None

    @classmethod
    def begun(cls, give, keep, first_bits, parts):
        bits = parts.bit_length() - 1
        self = cls.__new__(cls)
        self.parts = parts
        shape = (2,) * (bits - 1) + give.shape[1:]
        self.terms = [keep.reshape(shape)]
        b = first_bits[0]
        self.left = [a for a in range(bits - 1, -1, -1) if a != b]
        self.start = 0
        self.order = list(first_bits[1:]) + [a for a in range(bits) if a not in first_bits]
        self.got = lax.ppermute(give.reshape(shape), "dp", [(i, i ^ (1 << b)) for i in range(parts)])
        return self

    def send(self):
        if not self.order:
            return
        b = self.order.pop(0)
        axis = self.start + self.left.index(b)
        self.left.remove(b)
        mine = (lax.axis_index("dp") >> b) & 1
        give = [lax.dynamic_index_in_dim(a, 1 - mine, axis, keepdims=False) for a in self.terms]
        give = give[0] if len(give) == 1 else low(sum(wide(a) for a in give))
        self.got = lax.ppermute(give, "dp", [(i, i ^ (1 << b)) for i in range(self.parts)])
        self.terms = [lax.dynamic_index_in_dim(a, mine, axis, keepdims=False) for a in self.terms]

    def take(self):
        if self.got is not None:
            self.terms.append(self.got)
            self.terms = [low(sum(wide(a) for a in self.terms))]
            self.got = None

    def finish(self):
        self.take()
        while self.order:
            self.send()
            self.take()
        return self.terms[0]


def checkpoint(anchor, *sums):
    waiting = [s for s in sums if s.got is not None]
    anchor, *got = tie(anchor, *[s.got for s in waiting])
    for s, g in zip(waiting, got):
        s.got = g
        s.take()
        s.send()
    return anchor


def all_sum(array, parts):
    array = array + lax.ppermute(array, "mp", SWAP)
    for b in range(parts.bit_length() - 1):
        array = array + lax.ppermute(array, "dp", [(i, i ^ (1 << b)) for i in range(parts)])
    return array


def slot_order(block_slot):
    numbers = jnp.arange(block_slot.shape[0], dtype=jnp.int32)
    return jnp.sum(jnp.where(block_slot[None, :] == numbers[:, None], numbers[None, :], 0), axis=1)


def on_device(
    parts,
    mp_size,
    tokens,
    memory,
    cotangent,
    bucket,
    target_lengths,
    memory_lengths,
    block_slot,
    col_weights,
    row_weights,
    shared_vectors,
    split_vectors,
    shared_first,
    shared_second,
    split_first,
    split_second,
    slot_first,
    slot_second,
    slot_master,
    slot_left,
    slot_right,
    left_basis,
    right_basis,
):
    core = lax.axis_index("mp")
    aligned = BS // parts == PART
    half = col_weights.shape[2]
    shared = shared_vectors
    own_bucket = lax.dynamic_index_in_dim(bucket, core, 0, keepdims=False)
    own_target = lax.dynamic_index_in_dim(target_lengths, core, 0, keepdims=False)
    own_memory = lax.dynamic_index_in_dim(memory_lengths, core, 0, keepdims=False)
    rows = tokens.shape[0]
    self_at = self_plan(own_bucket, rows)
    cross_at = cross_plan(own_bucket, own_memory, rows, memory.shape[0])
    places = jnp.arange(rows, dtype=jnp.int32)
    size = rows // jnp.left_shift(jnp.int32(1), own_bucket)
    segment = places // size
    live = jnp.any(
        (segment[:, None] == jnp.arange(4, dtype=jnp.int32)[None, :])
        & ((places - segment * size)[:, None] < own_target[None, :]),
        axis=1,
    )
    cols = (col_weights, exchange(col_weights))
    rws = (row_weights, exchange(row_weights))
    splits = (split_vectors, exchange(split_vectors))
    both = (0, 1)

    tokens_wide = wide(tokens)
    normed1 = norm_forward(tokens_wide, shared[0], shared[1])
    query, key, value, mem_key, mem_value, self_out, self_log = ([], [], [], [], [], [], [])
    for h in both:
        query.append(low(dot32(normed1, cols[h][0]) + splits[h][0]))
        key.append(low(dot32(normed1, cols[h][1])))
        value.append(low(dot32(normed1, cols[h][2]) + splits[h][1]))
        mem_key.append(low(dot32(memory, cols[h][4])))
        mem_value.append(low(dot32(memory, cols[h][5]) + splits[h][3]))
        out, log = attention(query[h], key[h], value[h], self_at, True)
        self_out.append(out)
        self_log.append(log)
    resid1, normed2 = join_forward(tokens, self_out, rws, 0, shared[6], shared[2], shared[3])
    cross_query, cross_out, cross_log = ([], [], [])
    for h in both:
        cross_query.append(low(dot32(normed2, cols[h][3]) + splits[h][2]))
        out, log = attention(cross_query[h], mem_key[h], mem_value[h], cross_at, False)
        cross_out.append(out)
        cross_log.append(log)
    resid2, normed3 = join_forward(resid1, cross_out, rws, 1, shared[7], shared[4], shared[5])
    grad_out = jnp.where(live[:, None], cotangent, jnp.zeros_like(cotangent))
    down_peer, back_peer, up_grad, down_grad, up_bias_peer = feed_forward(normed3, grad_out, cols[1], rws[1], splits[1], aligned)
    up_peer = exchange(up_grad)
    down_grad_peer = exchange(down_grad)
    down_own, back_own, up_grad, down_grad, up_bias_own = feed_forward(normed3, grad_out, cols[0], rws[0], splits[0], aligned)
    up_bias = [up_bias_own[:, 0], up_bias_peer[:, 0]]
    back_own, up_peer, down_grad_peer = tie(back_own, up_peer, down_grad_peer)
    if aligned:
        down_sum = Staged([down_grad, down_grad_peer], DOWN_BITS, led=True)
        up_sum = Staged([up_grad, up_peer], UP_BITS, led=True)
    else:
        down_sum = Staged([to_parts(down_grad, parts), to_parts(down_grad_peer, parts)], (1, 2, 0))
        up_sum = Staged([to_parts(up_grad, parts), to_parts(up_peer, parts)], (0, 1))
    down_sum.send()
    up_sum.send()
    grad_resid2, grad2, sums3 = join_back(
        None, None, 0, (back_own, back_peer), (resid2, grad_out, shared[4]), low_too=True
    )

    def outer(x, g):
        return low(jnp.einsum("td,te->de", x, g, preferred_element_type=jnp.float32))

    row1_peer = exchange(outer(cross_out[1], grad2))
    row1_own = outer(cross_out[0], grad2)

    def cross_back(h, grad):
        return attention_back(
            cross_query[h], mem_key[h], mem_value[h], grad, cross_out[h], cross_log[h], cross_at, False
        )

    grad_cq, grad_mk, grad_mv = ([None, None], [None, None], [None, None])
    grad = [low(jnp.einsum("td,fd->tf", grad2, rws[h][1], preferred_element_type=jnp.float32)) for h in both]
    grad_cq[1], grad_mk[1], grad_mv[1] = cross_back(1, grad[1])
    cross_peer = exchange(outer_plain((normed2, memory), (0, 1, 1), (grad_cq[1], grad_mk[1], grad_mv[1])))
    grad[0], cross_peer = tie(checkpoint(grad[0], down_sum, up_sum), cross_peer)
    grad_cq[0], grad_mk[0], grad_mv[0] = cross_back(0, grad[0])
    (grad_cq[0], grad_mk[0], grad_mv[0]), row1_peer = tie(
        checkpoint((grad_cq[0], grad_mk[0], grad_mv[0]), down_sum, up_sum), row1_peer
    )
    if aligned:
        ((give, keep),) = outer_split(
            (normed2, memory), (0, 1, 1), (grad_cq[0], grad_mk[0], grad_mv[0]), cross_peer, ((0, 4, 0),), lax.axis_index("dp")
        )
        cross_sum = Staged.begun(give, keep, (0, 1), parts)
    else:
        cross_own = jnp.stack([outer(normed2, grad_cq[0]), outer(memory, grad_mk[0]), outer(memory, grad_mv[0])])
        cross_sum = Staged([to_parts(cross_own, parts), to_parts(cross_peer, parts)], (0, 1))
        cross_sum.send()
    grad_resid1, grad1, sums2 = join_back(
        [[grad_cq[0]], [grad_cq[1]]], cols, 3, (), (resid1, grad_resid2, shared[2]), low_too=True
    )
    grad1 = checkpoint(grad1, down_sum, up_sum)
    row0_peer = exchange(outer(self_out[1], grad1))
    row0_own = outer(self_out[0], grad1)

    def self_back(h, grad):
        return attention_back(query[h], key[h], value[h], grad, self_out[h], self_log[h], self_at, True)

    grad_q, grad_k, grad_v = ([None, None], [None, None], [None, None])
    grad = [low(jnp.einsum("td,fd->tf", grad1, rws[h][0], preferred_element_type=jnp.float32)) for h in both]
    grad[1], row0_peer = tie(grad[1], row0_peer)
    row_sum = Staged(
        [
            to_parts(jnp.stack([row0_own, row1_own]), parts),
            to_parts(jnp.stack([row0_peer, row1_peer]), parts),
        ],
        (1, 0),
    )
    row_sum.send()
    grad_q[1], grad_k[1], grad_v[1] = self_back(1, grad[1])
    self_peer = exchange(outer_plain((normed1,), (0, 0, 0), (grad_q[1], grad_k[1], grad_v[1])))
    grad[0], self_peer = tie(checkpoint(grad[0], down_sum, up_sum, cross_sum, row_sum), self_peer)
    grad_q[0], grad_k[0], grad_v[0] = self_back(0, grad[0])
    grad_q[0], grad_k[0], grad_v[0] = checkpoint((grad_q[0], grad_k[0], grad_v[0]), cross_sum, row_sum)
    if aligned:
        (a, b) = outer_split(
            (normed1,), (0, 0, 0), (grad_q[0], grad_k[0], grad_v[0]), self_peer, ((0, 2, 0), (2, 4, 1)), lax.axis_index("dp")
        )
        (grad_q[0], grad_k[0], grad_v[0]), *a = tie((grad_q[0], grad_k[0], grad_v[0]), *a)
        self_a = Staged.begun(*a, (0, 1), parts)
        self_b = Staged.begun(*b, (1, 0), parts)
    else:
        self_own = jnp.stack([outer(normed1, grad_q[0]), outer(normed1, grad_k[0]), outer(normed1, grad_v[0])])
        self_terms = [to_parts(self_own, parts), to_parts(self_peer, parts)]
        self_terms = [a.reshape((3, 2, -1) + a.shape[1:]).swapaxes(0, 1) for a in self_terms]
        self_terms = [a.reshape((2, -1) + a.shape[3:]) for a in self_terms]
        self_a = Staged([a[0] for a in self_terms], (0, 1))
        self_b = Staged([a[1] for a in self_terms], (1, 0))
        self_a.send()
        self_b.send()
    input_grad, sums1 = join_back(
        [[grad_q[h], grad_k[h], grad_v[h]] for h in both], cols, 0, (), (tokens, grad_resid1, shared[0])
    )
    input_grad, sums1, grad_mk[0] = checkpoint(
        (input_grad, sums1, grad_mk[0]), cross_sum, row_sum, self_a, self_b
    )
    (memory_grad,) = join_back([[grad_mk[h], grad_mv[h]] for h in both], cols, 2)
    memory_grad, sums1, down_own = checkpoint((memory_grad, sums1, down_own), cross_sum, row_sum, self_a, self_b)
    output = low(resid2 + (down_own + down_peer) + shared[8])
    self_piece = jnp.stack([a.finish().reshape((3, -1) + (BS // parts, half)) for a in (self_a, self_b)], axis=1)
    self_piece = self_piece.reshape((-1, BS // parts, half))
    cross_piece = cross_sum.finish()
    up_piece = up_sum.finish()
    down_piece = down_sum.finish()
    row_piece = row_sum.finish()

    def column_sum(a):
        return jnp.sum(wide(a), axis=0)

    shared_grad = jnp.concatenate(
        [
            sums1[0:2],
            sums2[0:2],
            sums3[0:2],
            sums2[2:3],
            sums3[2:3],
            column_sum(grad_out)[None],
        ]
    )
    split_grad = [
        jnp.concatenate(
            [
                jnp.stack([column_sum(grad_q[h]), column_sum(grad_v[h]), column_sum(grad_cq[h]), column_sum(grad_mv[h])]),
                up_bias[h],
            ]
        )
        for h in both
    ]
    first = jnp.where(core == 0, split_grad[0], split_grad[1])
    second = jnp.where(core == 0, split_grad[1], split_grad[0])
    vectors = jnp.concatenate([shared_grad, jnp.concatenate([first, second], axis=1)], axis=0)
    def blocks(piece):
        m, rows_in, width = piece.shape
        return (
            piece.reshape(m, rows_in, width // BS, BS).transpose(0, 2, 1, 3).reshape(-1, rows_in, BS)
        )

    pieces = jnp.concatenate(
        [
            blocks(self_piece),
            blocks(cross_piece),
            blocks(up_piece),
            blocks(row_piece),
            blocks(down_piece),
        ],
        axis=0,
    )
    square = jnp.sum(wide(pieces) * wide(pieces))
    owned = slot_first.shape[0]
    part_rows = BS // parts
    sent = jnp.take(pieces, slot_order(block_slot), axis=0)
    if part_rows % 16 == 0 and vectors.shape[0] < parts * mp_size:
        came, vectors, grad_norm = share(sent.reshape(parts, owned * part_rows, BS), square, vectors, mp_size)
    else:
        came = lax.all_to_all(sent.reshape(parts, owned, part_rows, BS), "dp", 0, 0, tiled=True)
        vectors = all_sum(vectors, parts)
        grad_norm = jnp.sqrt(all_sum(square.reshape(1, 1), parts)[0, 0] + jnp.sum(vectors * vectors))
    shared_sum = vectors[:9]
    split_sum = vectors[9:]
    mine = came.reshape(parts, owned, part_rows, BS).transpose(1, 0, 2, 3).reshape(owned, BS, BS)
    clip = clip_limit / jnp.maximum(grad_norm, clip_limit)

    def flat(a):
        return a.reshape(owned, BS, BS)

    updated = soap(
        clip,
        mine,
        flat(slot_first),
        flat(slot_second),
        flat(slot_master),
        flat(slot_left),
        flat(slot_right),
        flat(left_basis),
        flat(right_basis),
    )
    first_moment, second_moment, master_weight, master_copy, left_stat, right_stat, left_rotation, right_rotation = (
        a.reshape(slot_first.shape) for a in updated
    )
    shared_mean, shared_square, shared_values = adam_step(
        shared_sum * clip, shared_first, shared_second, shared_vectors, shared_rate
    )
    split_own = lax.dynamic_slice_in_dim(split_sum, core * half, half, axis=1)
    split_mean, split_square, split_values = adam_step(
        split_own * clip, split_first, split_second, split_vectors, split_rate
    )
    return (
        output,
        input_grad,
        memory_grad,
        first_moment,
        second_moment,
        master_weight,
        master_copy,
        left_stat,
        right_stat,
        left_rotation,
        right_rotation,
        shared_mean,
        shared_square,
        shared_values,
        split_mean,
        split_square,
        split_values,
        grad_norm,
    )


def solution(mesh):
    rows = P(("dp", "mp"), None)
    slots = P("dp", "mp", None, None)
    split = P(None, "mp")
    placed = (
        (rows, rows, rows, P("dp"), P("dp", None), P("dp", None), P())
        + (P(None, None, "mp"), P(None, "mp", None), P(), split, P(), P(), split, split)
        + (slots,) * 7
    )
    return jax.shard_map(
        partial(on_device, mesh.shape["dp"], mesh.shape["mp"]),
        mesh=mesh,
        in_specs=placed,
        out_specs=(rows,) * 3 + (slots,) * 8 + (P(),) * 3 + (split,) * 3 + (P(),),
        check_vma=False,
    )
```
